256 devices in a mesh: lat: 4 (over x_hi, core), lon: 64 (over x_lo, z, y).
Axes of the slice: x: 4 (x_hi: 2, x_lo: 2; x = x_hi * 2 + x_lo), y: 4, z: 8, core: 2. Of those that a mesh axis runs over, the one named last changes fastest.
Arguments:
- inputs: bfloat16 [32, 2048, 1024], P(None, 'lon', 'lat'), may hold values from -6 to 6
- kernel_one: bfloat16 [3, 3, 32, 32], replicated, may hold values from -0.375 to 0.375
- kernel_two: bfloat16 [3, 3, 32, 32], replicated, may hold values from -0.375 to 0.375
- cotangent: bfloat16 [32, 2048, 1024], P(None, 'lon', 'lat'), may hold values from -6 to 6
Outputs:
- input_grad: bfloat16 [32, 2048, 1024], P(None, 'lon', 'lat')
- kernel_one_grad: float32 [3, 3, 32, 32], replicated
- kernel_two_grad: float32 [3, 3, 32, 32], replicated
The draws below stay inside these ranges and needn't reach their ends.
All inputs are finite; a program needn't handle non-finite values.
Results may differ from the reference program's by a relative error of at most 0.0032.
Values may be sent and summed in bfloat16 or wider, within the bound.
No kernel may reach another device: no remote copies, remote signals or barrier semaphores. Data moves between devices by JAX's collectives and lax.ppermute only.
A program may use at most 128 MiB of HBM per device.

```python
import math
import jax
import jax.numpy as jnp
from jax import lax

CH = 32
LON_DEV = 32
NLON = 2048
NLAT = 1024


def levels(rng, extent, cuts, least, high):
    def one(dim, shards_of):
        draws = jax.random.uniform(jax.random.fold_in(jax.random.fold_in(rng, 6), dim), (shards_of,), jnp.float32, least / len(cuts), high / len(cuts))
        return jnp.repeat(jnp.exp(draws), extent[dim] // shards_of).reshape((-1,) + (1,) * (len(extent) - dim - 1))

    level = one(*cuts[0])
    for cut in cuts[1:]:
        level = level * one(*cut)
    return level


def scatter_about(key, extent, scale, most, cuts=(), kind=jnp.bfloat16):
    entries = scale * jax.random.normal(key, extent, jnp.float32)
    if cuts:
        entries = entries * levels(key, extent, cuts, -0.22, 0.18)
    return jnp.clip(entries, -most, most).astype(kind)


def setup_inputs(seed: int = 0) -> dict:
    splits = jax.random.split(jax.random.key(seed), 5)
    return {
        "inputs": scatter_about(splits[0], (CH, NLON, NLAT), 1.0, 6.0, ((1, 64), (2, 4))),
        "kernel_one": scatter_about(splits[1], (3, 3, CH, CH), (9 * CH) ** -0.5, 0.375),
        "kernel_two": scatter_about(splits[2], (3, 3, CH, CH), (9 * CH) ** -0.5, 0.375),
        "cotangent": scatter_about(splits[3], (CH, NLON, NLAT), 1.0, 6.0, ((1, 64), (2, 4))),
    }


def convolve(source, kernel):
    lon_cells = source.shape[1] - 2
    lat_cells = source.shape[2] - 2
    values = source.astype(jnp.float32)
    summed = jnp.zeros((kernel.shape[2], lon_cells, lat_cells), jnp.float32)
    for tap_row in range(3):
        for tap_col in range(3):
            summed = summed + jnp.einsum('oc,cij->oij', kernel[tap_row, tap_col].astype(jnp.float32), values[:, tap_row:tap_row + lon_cells, tap_col:tap_col + lat_cells])
    return summed

def kernel_terms(upstream, source):
    lon_cells = upstream.shape[1]
    lat_cells = upstream.shape[2]
    upper = upstream.astype(jnp.float32)
    values = source.astype(jnp.float32)
    rows_list = []
    for tap_row in range(3):
        row_taps = []
        for tap_col in range(3):
            row_taps.append(jnp.einsum('oij,cij->oc', upper, values[:, tap_row:tap_row + lon_cells, tap_col:tap_col + lat_cells]))
        rows_list.append(jnp.stack(row_taps))
    return jnp.stack(rows_list)

def flipped(kernel):
    return jnp.transpose(jnp.flip(kernel, (0, 1)), (0, 1, 3, 2))

def silu_slope(pre_act):
    sigmoid_value = jax.nn.sigmoid(pre_act)
    return sigmoid_value * (1.0 + pre_act * (1.0 - sigmoid_value))

def reference(inputs, kernel_one, kernel_two, cotangent):
    block_width = LON_DEV
    block_count = NLON // block_width
    grad_scale = 1.0 / math.sqrt(NLAT * NLON)

    def widen(source):
        wrapped = jnp.concatenate([source[:, -2:], source, source[:, :2]], 1)
        return jnp.pad(wrapped, ((0, 0), (0, 0), (2, 2)))
    padded_in = widen(inputs)
    padded_cot = widen(cotangent)
    lat_pos = jnp.arange(NLAT + 2, dtype=jnp.int32) - 1
    inside = ((lat_pos >= 0) & (lat_pos < NLAT)).astype(jnp.float32)
    back_one = flipped(kernel_one)
    back_two = flipped(kernel_two)

    def block_step(totals, block_index):
        offset = (block_index * block_width).astype(jnp.int32)
        in_block = lax.dynamic_slice_in_dim(padded_in, offset, block_width + 4, 1)
        cot_block = lax.dynamic_slice_in_dim(padded_cot, offset, block_width + 4, 1)
        pre_act = convolve(in_block, kernel_one)
        activation = (jax.nn.silu(pre_act) * inside).astype(jnp.bfloat16)
        back_grad = convolve(cot_block, back_two)
        pre_grad = (back_grad * silu_slope(pre_act) * inside).astype(jnp.bfloat16)
        own_cot = cot_block[:, 2:-2, 2:-2]
        result = (own_cot.astype(jnp.float32) + convolve(pre_grad, back_one)).astype(jnp.bfloat16)
        grad_one = totals[0] + kernel_terms(pre_grad[:, 1:-1, 1:-1], in_block[:, 1:-1, 1:-1])
        grad_two = totals[1] + kernel_terms(own_cot, activation)
        return ((grad_one, grad_two), result)
    empty_sums = jnp.zeros((3, 3, CH, CH), jnp.float32)
    totals, pieces = lax.scan(block_step, (empty_sums, empty_sums), jnp.arange(block_count, dtype=jnp.int32))
    input_grad = jnp.moveaxis(pieces, 0, 1).reshape(CH, NLON, NLAT)
    return (input_grad, totals[0] * grad_scale, totals[1] * grad_scale)
```

```python
import math

import jax
import jax.numpy as jnp
from jax import lax
from jax.sharding import PartitionSpec as P


def with_halo(block, sides, width, periodic):
    for axis, dim in sides:
        count = lax.axis_size(axis)
        forward = [(i, i + 1) for i in range(count - 1)]
        if periodic:
            forward.append((count - 1, 0))
        backward = [(target, source) for source, target in forward]
        low = lax.ppermute(
            lax.slice_in_dim(block, block.shape[dim] - width, None, axis=dim), axis, forward
        )
        high = lax.ppermute(lax.slice_in_dim(block, 0, width, axis=dim), axis, backward)
        block = jnp.concatenate([low, block, high], axis=dim)
    return block


def convolve(source, kernel):
    summed = lax.conv_general_dilated(
        source[None],
        kernel,
        (1, 1),
        "VALID",
        dimension_numbers=("NCHW", "HWOI", "NCHW"),
        preferred_element_type=jnp.float32,
    )
    return summed[0]


def kernel_terms(upstream, source):
    lhs_batch = source[:, None]
    rhs_taps = upstream[:, None]
    summed = lax.conv_general_dilated(
        lhs_batch,
        rhs_taps,
        (1, 1),
        "VALID",
        dimension_numbers=("NCHW", "OIHW", "NCHW"),
        preferred_element_type=jnp.float32,
    )
    return jnp.transpose(summed, (2, 3, 1, 0))


def flipped(kernel):
    return jnp.transpose(jnp.flip(kernel, (0, 1)), (0, 1, 3, 2))


def silu_slope(pre_act):
    sigmoid_value = jax.nn.sigmoid(pre_act)
    return sigmoid_value * (1.0 + pre_act * (1.0 - sigmoid_value))


def pairs(counts, partner):
    lat_count, lon_count = counts
    listed = []
    for lat in range(lat_count):
        for lon in range(lon_count):
            to_lat, to_lon = partner(lat, lon)
            listed.append((lat * lon_count + lon, to_lat * lon_count + to_lon))
    return listed


def x_partner(mask):
    def partner(lat, lon):
        place = ((lat >> 1) * 2 + (lon >> 5)) ^ mask
        return (place >> 1) * 2 + (lat & 1), (place & 1) * 32 + (lon & 31)

    return partner


def y_partner(mask):
    return lambda lat, lon: (lat, lon ^ mask)


def z_partner(mask):
    def partner(lat, lon):
        place = (lon >> 2) & 7
        if mask == 3:
            place = (place + (1 if place % 2 else -1)) % 8
        else:
            place ^= mask
        return lat, (lon & 35) | (place << 2)

    return partner


def exchange(value, partner):
    counts = (lax.axis_size("lat"), lax.axis_size("lon"))
    return lax.ppermute(value, ("lat", "lon"), pairs(counts, partner))


def sum_of_four(value, partner):
    near, far, wrap = [exchange(value, partner(mask)) for mask in (1, 2, 3)]
    return (value + near) + (far + wrap)


def sum_everywhere(halves):
    core = lax.axis_index("lat") % 2
    other_core = lambda lat, lon: (lat ^ 1, lon)
    mine = lax.dynamic_index_in_dim(halves, core, 0, False)
    theirs = lax.dynamic_index_in_dim(halves, 1 - core, 0, False)
    total = mine + exchange(theirs, other_core)
    total = sum_of_four(total, x_partner)
    total = sum_of_four(total, y_partner)
    total = total + exchange(total, z_partner(4))
    total = sum_of_four(total, z_partner)
    other = exchange(total, other_core)
    first = jnp.where(core == 0, total, other)
    second = jnp.where(core == 0, other, total)
    return jnp.stack([first, second])


def on_device(inputs, kernel_one, kernel_two, cotangent):
    channels = inputs.shape[0]
    lon_cells = inputs.shape[1]
    lat_cells = inputs.shape[2]
    grad_scale = 1.0 / math.sqrt(
        lon_cells * lat_cells * lax.axis_size("lat") * lax.axis_size("lon")
    )
    stacked = jnp.concatenate([inputs, cotangent], 0)
    back_one = flipped(kernel_one)
    back_two = flipped(kernel_two)
    lon_wide = with_halo(stacked, (("lon", 1),), 1, True)
    extended = with_halo(lon_wide, (("lat", 2),), 1, False)
    in_cycle = extended[:channels]
    cot_cycle = extended[channels:]
    pre_act = convolve(in_cycle, kernel_one)
    activation = jax.nn.silu(pre_act).astype(jnp.bfloat16)
    act_lon = with_halo(activation, (("lon", 1),), 1, True)
    act_cycle = with_halo(act_lon, (("lat", 2),), 1, False)
    back_grad = convolve(cot_cycle, back_two)
    pre_local = (back_grad * silu_slope(pre_act)).astype(jnp.bfloat16)
    grad_lon = with_halo(pre_local, (("lon", 1),), 1, True)
    grad_cycle = with_halo(grad_lon, (("lat", 2),), 1, False)
    grad_two = kernel_terms(cotangent, act_cycle) * grad_scale
    input_grad = (cotangent.astype(jnp.float32) + convolve(grad_cycle, back_one)).astype(
        jnp.bfloat16
    )
    grad_one = kernel_terms(pre_local, in_cycle) * grad_scale
    halves = jnp.stack([grad_one.reshape(-1, 128), grad_two.reshape(-1, 128)])
    summed = sum_everywhere(halves)
    return (
        input_grad,
        summed[0].reshape(grad_one.shape),
        summed[1].reshape(grad_two.shape),
    )


def solution(mesh):
    placed = (P(None, "lon", "lat"), P(), P(), P(None, "lon", "lat"))
    return jax.shard_map(
        on_device,
        mesh=mesh,
        in_specs=placed,
        out_specs=(P(None, "lon", "lat"), P(), P()),
        check_vma=False,
    )
```

```python
import functools
import math

import jax
import jax.numpy as jnp
import numpy as np
from jax import lax
from jax.experimental import pallas as pl
from jax.experimental.pallas import tpu as pltpu
from jax.sharding import PartitionSpec as P

BF = jnp.bfloat16
F32 = jnp.float32
GROUP = 6
WINDOW = GROUP + 2
HALF = 16
PARAMS = pltpu.CompilerParams(vmem_limit_bytes=40 * 2**20)


def dot(left, right):
    return lax.dot_general(left, right, (((1,), (0,)), ((), ())), preferred_element_type=F32)


def dot_lanes(left, right):
    return lax.dot_general(left, right, (((1,), (1,)), ((), ())), preferred_element_type=F32)


def dot_rows(left, right):
    return lax.dot_general(left, right, (((0,), (0,)), ((), ())), preferred_element_type=F32)


def iota(shape, dim):
    return lax.broadcasted_iota(jnp.int32, shape, dim)


def call(kernel, outs, scratch, flops, *operands):
    bytes_moved = sum(o.size * o.dtype.itemsize for o in (*operands, *outs))
    return pl.pallas_call(
        kernel,
        out_shape=outs,
        in_specs=[pl.BlockSpec(memory_space=pltpu.VMEM)] * len(operands),
        out_specs=[pl.BlockSpec(memory_space=pltpu.VMEM)] * len(outs),
        scratch_shapes=scratch,
        compiler_params=PARAMS,
        cost_estimate=pl.CostEstimate(flops=flops, bytes_accessed=bytes_moved, transcendentals=0),
    )(*operands)


def shape(*dims, dtype=BF):
    return jax.ShapeDtypeStruct(dims, dtype)


def is_odd():
    return lax.axis_index("lat") % 2


def pack_kernel(x_ref, cot_ref, perm_ref, xl_ref, cl_ref, core_ref, mid_ref):
    lat_cells = x_ref.shape[2]
    odd = is_odd()
    row = iota((2 * HALF, lat_cells), 0)
    lane = iota((2 * HALF, lat_cells), 1)
    high = jnp.where(row < HALF, 1 - odd, odd)
    cell = jnp.where(high == 1, lat_cells - 2, 0) + row % 2
    edges = jnp.zeros((2 * HALF, xl_ref.shape[0]), F32)
    for place, (source, target) in enumerate(((x_ref, xl_ref), (cot_ref, cl_ref))):
        for part in range(source.shape[1] // HALF):
            block = source[:, part * HALF : (part + 1) * HALF, :].reshape(-1, lat_cells)
            rows = block.shape[0]
            target[part * rows : (part + 1) * rows, :] = dot(perm_ref[...], block).astype(BF)
        chosen = ((row % HALF) // 2 == place) & (lane == cell)
        edges = edges + dot_lanes(chosen.astype(F32).astype(BF), target[...])
    core_ref[...] = edges[:HALF].astype(BF)
    mid_ref[...] = edges[HALF:].astype(BF)


def weight_kernel(one_ref, two_ref, first_ref, back_ref):
    channels = one_ref.shape[2]
    lanes = WINDOW * channels
    tiled = (iota((channels, lanes), 1) % channels == iota((channels, lanes), 0)).astype(F32).astype(BF)
    block = iota((channels, lanes), 1) // channels
    for q in range(3):
        firsts = [dot(one_ref[p, q], tiled) for p in range(3)]
        backs = [dot_rows(two_ref[2 - p, 2 - q], tiled) for p in range(3)]
        for bases, target in ((firsts, first_ref), (backs, back_ref)):
            for a in range(GROUP):
                band = jnp.zeros((channels, lanes), F32)
                for p in range(3):
                    band = jnp.where(block == a + p, bases[p], band)
                target[q, a * channels : (a + 1) * channels, :] = band.astype(BF)


def last_weight_kernel(one_ref, last_ref):
    channels = one_ref.shape[2]
    rows, lanes = last_ref.shape[1:]
    tiled = (iota((channels, lanes), 1) % channels == iota((channels, lanes), 0)).astype(F32).astype(BF)
    spread = (iota((rows, channels), 0) // HALF == iota((rows, channels), 1)).astype(F32).astype(BF)
    step = iota((rows, lanes), 1) // channels - iota((rows, lanes), 0) % HALF
    for q in range(3):
        total = jnp.zeros((rows, lanes), F32)
        for p in range(3):
            base = dot_rows(one_ref[2 - p, 2 - q], tiled).astype(BF)
            total = jnp.where(step == p, dot(spread, base), total)
        last_ref[q] = total.astype(BF)


def halo_place(odd, place, lat_cells):
    row = iota((2 * HALF, lat_cells), 0)
    lane = iota((2 * HALF, lat_cells), 1)
    from_low = jnp.where(row < HALF, odd, 1 - odd) == 1
    wanted_row = 2 * place + jnp.where(from_low, 1, 0)
    wanted_lane = jnp.where(from_low, 0, lat_cells - 1)
    return ((row % HALF == wanted_row) & (lane == wanted_lane)).astype(F32).astype(BF)


def write_shifted(values, edge_columns, target, rows):
    lat_cells = values.shape[1]
    lane = iota(values.shape, 1)
    wide = values.astype(F32)
    below = jnp.where(lane == 0, edge_columns, pltpu.roll(wide, 1, 1))
    above = jnp.where(lane == lat_cells - 1, edge_columns, pltpu.roll(wide, lat_cells - 1, 1))
    target[0, rows, :] = below.astype(BF)
    target[1, rows, :] = values
    target[2, rows, :] = above.astype(BF)


def activate(pre_act, back_grad):
    sigmoid_value = 0.5 * jnp.tanh(0.5 * pre_act) + 0.5
    activation = pre_act * sigmoid_value
    slope = sigmoid_value + activation * (1.0 - sigmoid_value)
    return activation, back_grad * slope


def conv_rows(weight_ref, shifted, rows, out_rows):
    count = rows.stop - rows.start
    return sum(dot(weight_ref[q, :out_rows, :count], shifted[q, rows, :]) for q in range(3))


def inner_kernel(x_ref, cot_ref, core_ref, mid_ref, first_ref, back_ref, pre_ref, grads_ref, xs, cs, total):
    lat_cells = x_ref.shape[1]
    channels = grads_ref.shape[2]
    odd = is_odd()
    halos = jnp.concatenate([core_ref[...], mid_ref[...]], 0)
    everything = slice(0, x_ref.shape[0])
    for place, (source, target) in enumerate(((x_ref, xs), (cot_ref, cs))):
        columns = dot_rows(halos, halo_place(odd, place, lat_cells))
        write_shifted(source[...], columns, target, everything)
    group_rows = GROUP * channels
    for k in range(pre_ref.shape[0] // group_rows):
        rows = slice(k * group_rows, k * group_rows + WINDOW * channels)
        pre_act = conv_rows(first_ref, xs, rows, group_rows)
        back_grad = conv_rows(back_ref, cs, rows, group_rows)
        activation, pre_grad = activate(pre_act, back_grad)
        activation = activation.astype(BF)
        pre_grad = pre_grad.astype(BF)
        pre_ref[k * group_rows : (k + 1) * group_rows, :] = pre_grad
        for q in range(3):
            for place, (own, raw) in enumerate(((pre_grad, xs), (activation, cs))):
                term = dot_lanes(own, raw[q, rows, :])
                if k == 0:
                    total[place, q] = term
                else:
                    total[place, q] += term
    for place in range(2):
        for q in range(3):
            summed = jnp.zeros((channels, WINDOW * channels), F32)
            for a in range(GROUP):
                band = total[place, q, a * channels : (a + 1) * channels, :]
                if a:
                    band = pltpu.roll(band, WINDOW * channels - a * channels, 1)
                summed = summed + band
            grads_ref[place, q] = summed[:, :128]


def edge_kernel(x_ref, cot_ref, core_ref, mid_ref, left_ref, right_ref, first_ref, back_ref, grads_ref,
                low_ref, high_ref, out_ref, xs, cs):
    lat_cells = x_ref.shape[1]
    channels = grads_ref.shape[2]
    odd = is_odd()
    two = 2 * channels
    own_rows = x_ref.shape[0]
    sums = [[grads_ref[place, q][:, : 3 * channels] for q in range(3)] for place in range(2)]
    for side, (message, target) in enumerate(((left_ref, low_ref), (right_ref, high_ref))):
        own = slice(0, two) if side == 0 else slice(own_rows - two, own_rows)
        sent = message[2 * two : 2 * two + HALF, :]
        sent_halos = jnp.concatenate([sent[:, :two], sent[:, two : 2 * two]], 0).astype(F32)
        own_halos = jnp.concatenate([core_ref[:, own], mid_ref[:, own]], 0).astype(F32)
        order = (sent_halos, own_halos) if side == 0 else (own_halos, sent_halos)
        halos = jnp.concatenate(order, 1).astype(BF)
        for place, (source, shifted) in enumerate(((x_ref, xs), (cot_ref, cs))):
            sent_rows = message[place * two : (place + 1) * two, :]
            order = (sent_rows, source[own, :]) if side == 0 else (source[own, :], sent_rows)
            columns = dot_rows(halos, halo_place(odd, place, lat_cells))
            write_shifted(jnp.concatenate(order, 0), columns, shifted, slice(0, 2 * two))
        rows = slice(0, 2 * two)
        pre_act = conv_rows(first_ref, xs, rows, two)
        back_grad = conv_rows(back_ref, cs, rows, two)
        activation, pre_grad = activate(pre_act, back_grad)
        pre_grad = pre_grad.astype(BF)
        target[...] = pre_grad
        mine = slice(channels, two) if side == 0 else slice(0, channels)
        near = slice(channels, 2 * two) if side == 0 else slice(0, 3 * channels)
        activation = activation[mine].astype(BF)
        pre_grad = pre_grad[mine]
        for q in range(3):
            sums[0][q] = sums[0][q] + dot_lanes(pre_grad, xs[q, near, :])
            sums[1][q] = sums[1][q] + dot_lanes(activation, cs[q, near, :])
    for place in range(2):
        for q in range(3):
            out_ref[place, q, :, : 3 * channels] = sums[place][q]
            out_ref[place, q, :, 3 * channels :] = jnp.zeros((channels, 128 - 3 * channels), F32)


def last_kernel(x_ref, cot_ref, core_ref, mid_ref, left_ref, right_ref, first_ref, back_ref, low_ref, pre_ref,
                high_ref, last_ref, raw_ref, out_ref, rows_buffer, strips, ps):
    lat_cells = x_ref.shape[1]
    channels = out_ref.shape[0]
    two = 2 * channels
    own_rows = x_ref.shape[0]
    wide_rows = own_rows + 2 * two
    odd = is_odd()
    core, mid = core_ref[...].astype(F32), mid_ref[...].astype(F32)
    lat = lax.axis_index("lat")
    lat_count = lax.axis_size("lat")

    def halo_lanes(value, first):
        parts = [left_ref[2 * two : 2 * two + HALF, first : first + two].astype(F32), value,
                 right_ref[2 * two : 2 * two + HALF, first : first + two].astype(F32)]
        return parts

    def put(target, parts):
        target[:, 0:two] = parts[0]
        target[:, two : two + own_rows] = parts[1]
        target[:, two + own_rows : wide_rows] = parts[2]

    put(strips.at[0], halo_lanes(core, 0))
    put(strips.at[1], halo_lanes(mid, two))
    core_wide, mid_wide = strips[0], strips[1]
    low = jnp.where(odd == 1, core_wide, mid_wide)
    high = jnp.where(odd == 1, mid_wide, core_wide)
    row = iota((HALF, lat_cells), 0)
    lane = iota((HALF, lat_cells), 1)
    ends = ((row < 2) & (lane == row * (lat_cells - 1))).astype(F32).astype(BF)
    values = []
    span = 4 * channels
    window = 6 * channels
    for place, (source, weight_ref) in enumerate(((x_ref, first_ref), (cot_ref, back_ref))):
        rows_buffer[0:two, :] = left_ref[place * two : (place + 1) * two, :]
        rows_buffer[two : two + own_rows, :] = source[...]
        rows_buffer[two + own_rows : wide_rows, :] = right_ref[place * two : (place + 1) * two, :]
        own = dot_lanes(ends, rows_buffer[...])
        low_rows = [low[2 * place : 2 * place + 1], low[2 * place + 1 : 2 * place + 2], own[0:1]]
        high_rows = [own[1:2], high[2 * place : 2 * place + 1], high[2 * place + 1 : 2 * place + 2]]
        total = None
        for q in range(3):
            which = iota((HALF, wide_rows), 0)
            strip = jnp.where(which == 0, low_rows[q], jnp.where(which == 1, high_rows[q], 0.0))
            strip = jnp.concatenate([strip, jnp.zeros((HALF, 128), F32)], 1)
            stacked = jnp.concatenate(
                [strip[:, k : k + window] for k in range(0, wide_rows, span)], 0
            ).astype(BF)
            term = dot_lanes(stacked, weight_ref[q, :span, :window])
            total = term if total is None else total + term
        values.append(total)
    _, pre_grad = activate(*values)
    beyond = jnp.where(iota(pre_grad.shape, 0) % HALF == 0, lat, lat_count - 1 - lat)
    pre_grad = jnp.where(beyond > 0, pre_grad, 0.0)
    pre_strip = jnp.concatenate(
        [pre_grad[k : k + HALF] for k in range(0, pre_grad.shape[0], HALF)], 1
    ).astype(BF)
    wide = pre_ref.shape[0] + 2 * two
    columns = dot_rows(pre_strip, ends)[:wide]
    rows_buffer[0:two, :] = low_ref[...]
    rows_buffer[two : wide - two, :] = pre_ref[...]
    rows_buffer[wide - two : wide, :] = high_ref[...]
    write_shifted(rows_buffer[0:wide, :], columns, ps, slice(0, wide))
    count = last_ref.shape[2]
    for part in range(out_ref.shape[1] // HALF):
        start = part * HALF * channels
        total = sum(dot(last_ref[q], ps[q, start : start + count, :]) for q in range(3))
        lons = slice(part * HALF, (part + 1) * HALF)
        total = total.reshape(channels, HALF, lat_cells) + raw_ref[:, lons, :].astype(F32)
        out_ref[:, lons, :] = total.astype(BF)


def result_kernel(scale, mine_ref, other_ref, one_ref, two_ref):
    channels = one_ref.shape[2]
    odd = is_odd()
    first = jnp.where(odd == 0, mine_ref[...], other_ref[...]) * scale
    second = jnp.where(odd == 0, other_ref[...], mine_ref[...]) * scale
    for q in range(3):
        for p in range(3):
            lanes = slice(p * channels, (p + 1) * channels)
            one_ref[p, q] = first[q][:, lanes]
            two_ref[2 - p, 2 - q] = second[q][:, lanes].T


def pairs(counts, partner):
    lat_count, lon_count = counts
    listed = []
    for lat in range(lat_count):
        for lon in range(lon_count):
            to_lat, to_lon = partner(lat, lon)
            listed.append((lat * lon_count + lon, to_lat * lon_count + to_lon))
    return listed


def x_partner(mask):
    def partner(lat, lon):
        place = ((lat >> 1) * 2 + (lon >> 5)) ^ mask
        return (place >> 1) * 2 + (lat & 1), (place & 1) * 32 + (lon & 31)

    return partner


def y_partner(mask):
    return lambda lat, lon: (lat, lon ^ mask)


def z_partner(mask):
    def partner(lat, lon):
        place = (lon >> 2) & 7
        if mask == 3:
            place = (place + (1 if place % 2 else -1)) % 8
        else:
            place ^= mask
        return lat, (lon & 35) | (place << 2)

    return partner


def exchange(value, partner):
    counts = (lax.axis_size("lat"), lax.axis_size("lon"))
    return lax.ppermute(value, ("lat", "lon"), pairs(counts, partner))


def sum_of_four(value, partner):
    near, far, wrap = [exchange(value, partner(mask)) for mask in (1, 2, 3)]
    return (value + near) + (far + wrap)


def sum_everywhere(halves):
    core = lax.axis_index("lat") % 2
    other_core = lambda lat, lon: (lat ^ 1, lon)
    mine = lax.dynamic_index_in_dim(halves, core, 0, False)
    theirs = lax.dynamic_index_in_dim(halves, 1 - core, 0, False)
    total = mine + exchange(theirs, other_core)
    total = sum_of_four(total, x_partner)
    total = sum_of_four(total, y_partner)
    total = total + exchange(total, z_partner(4))
    total = sum_of_four(total, z_partner)
    other = exchange(total, other_core)
    return total, other


def lat_exchange(core, mid):
    count = lax.axis_size("lat")
    inner = [pair for low in range(1, count - 1, 2) for pair in ((low, low + 1), (low + 1, low))]
    return lax.ppermute(core, "lat", [(i, i ^ 1) for i in range(count)]), lax.ppermute(mid, "lat", inner)


def on_device(inputs, kernel_one, kernel_two, cotangent):
    channels, lon_cells, lat_cells = inputs.shape
    cells = lon_cells * lat_cells * lax.axis_size("lat") * lax.axis_size("lon")
    rows = channels * lon_cells
    two = 2 * channels
    place = np.arange(HALF * channels)
    perm = np.zeros((HALF * channels, HALF * channels), np.float32)
    perm[place, (place % channels) * HALF + place // channels] = 1.0
    perm = jnp.asarray(perm, BF)

    x_rows, cot_rows, core_out, mid_out = call(
        pack_kernel,
        [shape(rows, lat_cells), shape(rows, lat_cells), shape(HALF, rows), shape(HALF, rows)],
        [],
        10**9,
        inputs,
        cotangent,
        perm,
    )
    core_in, mid_in = lat_exchange(core_out, mid_out)

    def message(part):
        pieces = jnp.concatenate([core_in[:, part], mid_in[:, part]], 1)
        pieces = jnp.pad(pieces, ((0, 0), (0, lat_cells - 2 * two)))
        return jnp.concatenate([x_rows[part], cot_rows[part], pieces], 0)

    count = lax.axis_size("lon")
    to_left = message(slice(0, two))
    to_right = message(slice(rows - two, rows))
    from_left = lax.ppermute(to_right, "lon", [(i, (i + 1) % count) for i in range(count)])
    from_right = lax.ppermute(to_left, "lon", [((i + 1) % count, i) for i in range(count)])

    first, back = call(
        weight_kernel,
        [shape(3, GROUP * channels, WINDOW * channels)] * 2,
        [],
        10**8,
        kernel_one,
        kernel_two,
    )
    inner_rows = rows - two
    shifted = pltpu.VMEM((3, rows, lat_cells), BF)
    pre_inner, inner_grads = call(
        inner_kernel,
        [shape(inner_rows, lat_cells), shape(2, 3, channels, 128, dtype=F32)],
        [shifted, shifted, pltpu.VMEM((2, 3, GROUP * channels, WINDOW * channels), F32)],
        4 * 10**9,
        x_rows, cot_rows, core_in, mid_in, first, back,
    )
    edge_shifted = pltpu.VMEM((3, 2 * two, lat_cells), BF)
    pre_low, pre_high, grads = call(
        edge_kernel,
        [shape(two, lat_cells), shape(two, lat_cells), shape(2, 3, channels, 128, dtype=F32)],
        [edge_shifted, edge_shifted],
        10**9,
        x_rows, cot_rows, core_in, mid_in, from_left, from_right, first, back, inner_grads,
    )
    (last_weights,) = call(
        last_weight_kernel,
        [shape(3, HALF * channels, (HALF + 2) * channels)],
        [],
        10**9,
        kernel_one,
    )
    (input_grad,) = call(
        last_kernel,
        [shape(channels, lon_cells, lat_cells)],
        [
            pltpu.VMEM((rows + 2 * two, lat_cells), BF),
            pltpu.VMEM((2, HALF, rows + 2 * two), F32),
            pltpu.VMEM((3, rows + two, lat_cells), BF),
        ],
        2 * 10**9,
        x_rows, cot_rows, core_in, mid_in, from_left, from_right, first, back,
        pre_low, pre_inner, pre_high, last_weights, cotangent,
    )
    mine, other = sum_everywhere(grads.reshape(2, 3 * channels, 128))
    grad_one, grad_two = call(
        functools.partial(result_kernel, 1.0 / math.sqrt(cells)),
        [shape(3, 3, channels, channels, dtype=F32)] * 2,
        [],
        10**6,
        mine.reshape(3, channels, 128),
        other.reshape(3, channels, 128),
    )
    return (input_grad, grad_one, grad_two)


def solution(mesh):
    placed = (P(None, "lon", "lat"), P(), P(), P(None, "lon", "lat"))
    return jax.shard_map(
        on_device,
        mesh=mesh,
        in_specs=placed,
        out_specs=(P(None, "lon", "lat"), P(), P()),
        check_vma=False,
    )
```

```python
import functools
import math

import jax
import jax.numpy as jnp
from jax import lax
from jax.experimental import pallas as pl
from jax.experimental.pallas import tpu as pltpu
from jax.sharding import PartitionSpec as P

BF = jnp.bfloat16
F32 = jnp.float32
GROUP = 6
WINDOW = GROUP + 2
HALF = 16
PARAMS = pltpu.CompilerParams(vmem_limit_bytes=40 * 2**20)


def dot(left, right):
    return lax.dot_general(left, right, (((1,), (0,)), ((), ())), preferred_element_type=F32)


def dot_lanes(left, right):
    return lax.dot_general(left, right, (((1,), (1,)), ((), ())), preferred_element_type=F32)


def dot_rows(left, right):
    return lax.dot_general(left, right, (((0,), (0,)), ((), ())), preferred_element_type=F32)


def iota(shape, dim):
    return lax.broadcasted_iota(jnp.int32, shape, dim)


def call(kernel, outs, scratch, flops, *operands, hbm_in=(), hbm_out=()):
    spaces = [pltpu.HBM if i in hbm_in else pltpu.VMEM for i in range(len(operands))]
    out_spaces = [pltpu.HBM if i in hbm_out else pltpu.VMEM for i in range(len(outs))]
    bytes_moved = sum(o.size * o.dtype.itemsize for o in (*operands, *outs))
    operands = [pltpu.with_memory_space_constraint(o, pltpu.HBM) if i in hbm_in else o for i, o in enumerate(operands)]
    return pl.pallas_call(
        kernel,
        out_shape=outs,
        in_specs=[pl.BlockSpec(memory_space=space) for space in spaces],
        out_specs=[pl.BlockSpec(memory_space=space) for space in out_spaces],
        scratch_shapes=scratch,
        compiler_params=PARAMS,
        cost_estimate=pl.CostEstimate(flops=flops, bytes_accessed=bytes_moved, transcendentals=0),
    )(*operands)


def shape(*dims, dtype=BF):
    return jax.ShapeDtypeStruct(dims, dtype)


def is_odd():
    return lax.axis_index("lat") % 2


def pack_kernel(x_ref, cot_ref, one_hbm, two_hbm, xl_ref, cl_ref, core_ref, mid_ref, first_ref, back_ref, last_ref,
                raw, one_ref, two_ref, perm, sems):
    channels, lon_cells, lat_cells = x_ref.shape
    parts = lon_cells // HALF
    pieces = 2
    span = channels // pieces
    kernels = [
        pltpu.make_async_copy(source, target, sems.at[place])
        for place, (source, target) in enumerate(((one_hbm, one_ref), (two_hbm, two_ref)))
    ]
    copies = []
    for place, source in enumerate((x_ref, cot_ref)):
        for part in range(parts):
            for piece in range(pieces):
                number = (place * parts + part) * pieces + piece
                some = pl.ds(piece * span, span)
                copies.append(
                    pltpu.make_async_copy(
                        source.at[some, pl.ds(part * HALF, HALF), :],
                        raw.at[place * parts + part, some],
                        sems.at[2 + number],
                    )
                )
    for copy in (*kernels, *copies):
        copy.start()
    to_row = iota(perm.shape, 0)
    from_row = iota(perm.shape, 1)
    moved = (to_row % channels) * HALF + to_row // channels
    perm[...] = jnp.where(from_row == moved, 1.0, 0.0).astype(BF)
    for copy in kernels:
        copy.wait()
    write_weights(one_ref, two_ref, first_ref, back_ref, last_ref)
    odd = is_odd()
    row = iota((2 * HALF, lat_cells), 0)
    lane = iota((2 * HALF, lat_cells), 1)
    high = jnp.where(row < HALF, 1 - odd, odd)
    cell = jnp.where(high == 1, lat_cells - 2, 0) + row % 2
    edges = jnp.zeros((2 * HALF, xl_ref.shape[0]), F32)
    rows = HALF * channels
    for place, target in enumerate((xl_ref, cl_ref)):
        for part in range(parts):
            number = place * parts + part
            for copy in copies[number * pieces : (number + 1) * pieces]:
                copy.wait()
            block = raw[number].reshape(rows, lat_cells)
            target[part * rows : (part + 1) * rows, :] = dot(perm[...], block).astype(BF)
        chosen = ((row % HALF) // 2 == place) & (lane == cell)
        edges = edges + dot_lanes(chosen.astype(F32).astype(BF), target[...])
    core_ref[...] = edges[:HALF].astype(BF)
    mid_ref[...] = edges[HALF:].astype(BF)


def write_weights(one_ref, two_ref, first_ref, back_ref, last_ref):
    channels = one_ref.shape[2]
    lanes = WINDOW * channels
    tiled = (iota((channels, lanes), 1) % channels == iota((channels, lanes), 0)).astype(F32).astype(BF)
    block = iota((channels, lanes), 1) // channels
    for q in range(3):
        firsts = [dot(one_ref[p, q], tiled) for p in range(3)]
        backs = [dot_rows(two_ref[2 - p, 2 - q], tiled) for p in range(3)]
        lasts = [dot_rows(one_ref[2 - p, 2 - q], tiled) for p in range(3)]
        for bases, target in ((firsts, first_ref), (backs, back_ref), (lasts, last_ref)):
            for a in range(GROUP):
                band = jnp.zeros((channels, lanes), F32)
                for p in range(3):
                    band = jnp.where(block == a + p, bases[p], band)
                target[q, a * channels : (a + 1) * channels, :] = band.astype(BF)


def halo_place(odd, place, lat_cells):
    row = iota((2 * HALF, lat_cells), 0)
    lane = iota((2 * HALF, lat_cells), 1)
    from_low = jnp.where(row < HALF, odd, 1 - odd) == 1
    wanted_row = 2 * place + jnp.where(from_low, 1, 0)
    wanted_lane = jnp.where(from_low, 0, lat_cells - 1)
    return ((row % HALF == wanted_row) & (lane == wanted_lane)).astype(F32).astype(BF)


def write_shifted(values, edge_columns, target, rows):
    lat_cells = values.shape[1]
    lane = iota(values.shape, 1)
    wide = values.astype(F32)
    below = jnp.where(lane == 0, edge_columns, pltpu.roll(wide, 1, 1))
    above = jnp.where(lane == lat_cells - 1, edge_columns, pltpu.roll(wide, lat_cells - 1, 1))
    target[0, rows, :] = below.astype(BF)
    target[1, rows, :] = values
    target[2, rows, :] = above.astype(BF)


def activate(pre_act, back_grad):
    sigmoid_value = 0.5 * jnp.tanh(0.5 * pre_act) + 0.5
    activation = pre_act * sigmoid_value
    slope = sigmoid_value + activation * (1.0 - sigmoid_value)
    return activation, back_grad * slope


def conv_rows(weight_ref, shifted, rows, out_rows):
    count = rows.stop - rows.start
    return sum(dot(weight_ref[q, :out_rows, :count], shifted[q, rows, :]) for q in range(3))


def inner_kernel(x_ref, cot_ref, core_ref, mid_ref, first_ref, back_ref, pre_ref, grads_ref, xs, cs, total):
    lat_cells = x_ref.shape[1]
    channels = grads_ref.shape[2]
    odd = is_odd()
    halos = jnp.concatenate([core_ref[...], mid_ref[...]], 0)
    everything = slice(0, x_ref.shape[0])
    for place, (source, target) in enumerate(((x_ref, xs), (cot_ref, cs))):
        columns = dot_rows(halos, halo_place(odd, place, lat_cells))
        write_shifted(source[...], columns, target, everything)
    group_rows = GROUP * channels
    for k in range(pre_ref.shape[0] // group_rows):
        rows = slice(k * group_rows, k * group_rows + WINDOW * channels)
        pre_act = conv_rows(first_ref, xs, rows, group_rows)
        back_grad = conv_rows(back_ref, cs, rows, group_rows)
        activation, pre_grad = activate(pre_act, back_grad)
        activation = activation.astype(BF)
        pre_grad = pre_grad.astype(BF)
        pre_ref[k * group_rows : (k + 1) * group_rows, :] = pre_grad
        for q in range(3):
            for place, (own, raw) in enumerate(((pre_grad, xs), (activation, cs))):
                term = dot_lanes(own, raw[q, rows, :])
                if k == 0:
                    total[place, q] = term
                else:
                    total[place, q] += term
    for place in range(2):
        for q in range(3):
            summed = jnp.zeros((channels, WINDOW * channels), F32)
            for a in range(GROUP):
                band = total[place, q, a * channels : (a + 1) * channels, :]
                if a:
                    band = pltpu.roll(band, WINDOW * channels - a * channels, 1)
                summed = summed + band
            grads_ref[place, q] = summed[:, :128]


def edge_kernel(x_ref, cot_ref, core_ref, mid_ref, left_ref, right_ref, first_ref, back_ref, grads_ref,
                low_ref, high_ref, out_ref, xs, cs):
    lat_cells = x_ref.shape[1]
    channels = grads_ref.shape[2]
    odd = is_odd()
    two = 2 * channels
    own_rows = x_ref.shape[0]
    sums = [[grads_ref[place, q][:, : 3 * channels] for q in range(3)] for place in range(2)]
    for side, (message, target) in enumerate(((left_ref, low_ref), (right_ref, high_ref))):
        own = slice(0, two) if side == 0 else slice(own_rows - two, own_rows)
        sent = message[2 * two : 2 * two + HALF, :]
        sent_halos = jnp.concatenate([sent[:, :two], sent[:, two : 2 * two]], 0).astype(F32)
        own_halos = jnp.concatenate([core_ref[:, own], mid_ref[:, own]], 0).astype(F32)
        order = (sent_halos, own_halos) if side == 0 else (own_halos, sent_halos)
        halos = jnp.concatenate(order, 1).astype(BF)
        for place, (source, shifted) in enumerate(((x_ref, xs), (cot_ref, cs))):
            sent_rows = message[place * two : (place + 1) * two, :]
            order = (sent_rows, source[own, :]) if side == 0 else (source[own, :], sent_rows)
            columns = dot_rows(halos, halo_place(odd, place, lat_cells))
            write_shifted(jnp.concatenate(order, 0), columns, shifted, slice(0, 2 * two))
        rows = slice(0, 2 * two)
        pre_act = conv_rows(first_ref, xs, rows, two)
        back_grad = conv_rows(back_ref, cs, rows, two)
        activation, pre_grad = activate(pre_act, back_grad)
        pre_grad = pre_grad.astype(BF)
        target[...] = pre_grad
        mine = slice(channels, two) if side == 0 else slice(0, channels)
        near = slice(channels, 2 * two) if side == 0 else slice(0, 3 * channels)
        activation = activation[mine].astype(BF)
        pre_grad = pre_grad[mine]
        for q in range(3):
            sums[0][q] = sums[0][q] + dot_lanes(pre_grad, xs[q, near, :])
            sums[1][q] = sums[1][q] + dot_lanes(activation, cs[q, near, :])
    for place in range(2):
        pack_taps(sums[place], out_ref.at[place])


def pack_taps(taps, out_ref):
    channels = taps[0].shape[0]
    used = 3 * channels
    for q in range(2):
        out_ref[q * channels : (q + 1) * channels, :] = jnp.concatenate(
            [taps[q], taps[2][:, q * channels : (q + 1) * channels]], 1
        )
    rest = taps[2][:, 2 * channels : used]
    count = 128 // channels
    rows = channels // count
    out_ref[2 * channels :, :] = jnp.concatenate(
        [rest[i * rows : (i + 1) * rows] for i in range(count)], 1
    )


def unpack_taps(packed, channels):
    used = 3 * channels
    count = 128 // channels
    main = [packed[q * channels : (q + 1) * channels] for q in range(2)]
    rest = packed[2 * channels :]
    last = jnp.concatenate([rest[:, i * channels : (i + 1) * channels] for i in range(count)], 0)
    third = jnp.concatenate([main[0][:, used:], main[1][:, used:], last], 1)
    return [main[0], main[1], third]


def last_kernel(x_ref, cot_ref, core_ref, mid_ref, left_ref, right_ref, first_ref, back_ref, low_ref, pre_ref,
                high_ref, last_ref, raw_ref, partial_ref, out_ref, passed_ref, rows_buffer, strips, ps, placed, result, sems):
    passed_ref[...] = partial_ref[...]
    lat_cells = x_ref.shape[1]
    channels = out_ref.shape[0]
    two = 2 * channels
    own_rows = x_ref.shape[0]
    wide_rows = own_rows + 2 * two
    odd = is_odd()
    core, mid = core_ref[...].astype(F32), mid_ref[...].astype(F32)
    lat = lax.axis_index("lat")
    lat_count = lax.axis_size("lat")

    def halo_lanes(value, first):
        parts = [left_ref[2 * two : 2 * two + HALF, first : first + two].astype(F32), value,
                 right_ref[2 * two : 2 * two + HALF, first : first + two].astype(F32)]
        return parts

    def put(target, parts):
        target[:, 0:two] = parts[0]
        target[:, two : two + own_rows] = parts[1]
        target[:, two + own_rows : wide_rows] = parts[2]

    put(strips.at[0], halo_lanes(core, 0))
    put(strips.at[1], halo_lanes(mid, two))
    core_wide, mid_wide = strips[0], strips[1]
    low = jnp.where(odd == 1, core_wide, mid_wide)
    high = jnp.where(odd == 1, mid_wide, core_wide)
    row = iota((HALF, lat_cells), 0)
    lane = iota((HALF, lat_cells), 1)
    ends = ((row < 2) & (lane == row * (lat_cells - 1))).astype(F32).astype(BF)
    values = []
    span = 4 * channels
    window = 6 * channels
    for place, (source, weight_ref) in enumerate(((x_ref, first_ref), (cot_ref, back_ref))):
        rows_buffer[0:two, :] = left_ref[place * two : (place + 1) * two, :]
        rows_buffer[two : two + own_rows, :] = source[...]
        rows_buffer[two + own_rows : wide_rows, :] = right_ref[place * two : (place + 1) * two, :]
        own = dot_lanes(ends, rows_buffer[...])
        low_rows = [low[2 * place : 2 * place + 1], low[2 * place + 1 : 2 * place + 2], own[0:1]]
        high_rows = [own[1:2], high[2 * place : 2 * place + 1], high[2 * place + 1 : 2 * place + 2]]
        total = None
        for q in range(3):
            which = iota((HALF, wide_rows), 0)
            strip = jnp.where(which == 0, low_rows[q], jnp.where(which == 1, high_rows[q], 0.0))
            strip = jnp.concatenate([strip, jnp.zeros((HALF, 128), F32)], 1)
            stacked = jnp.concatenate(
                [strip[:, k : k + window] for k in range(0, wide_rows, span)], 0
            ).astype(BF)
            term = dot_lanes(stacked, weight_ref[q, :span, :window])
            total = term if total is None else total + term
        values.append(total)
    _, pre_grad = activate(*values)
    beyond = jnp.where(iota(pre_grad.shape, 0) % HALF == 0, lat, lat_count - 1 - lat)
    pre_grad = jnp.where(beyond > 0, pre_grad, 0.0)
    pre_strip = jnp.concatenate(
        [pre_grad[k : k + HALF] for k in range(0, pre_grad.shape[0], HALF)], 1
    ).astype(BF)
    wide = pre_ref.shape[0] + 2 * two
    columns = dot_rows(pre_strip, ends)[:wide]
    rows_buffer[0:two, :] = low_ref[...]
    rows_buffer[two : wide - two, :] = pre_ref[...]
    rows_buffer[wide - two : wide, :] = high_ref[...]
    write_shifted(rows_buffer[0:wide, :], columns, ps, slice(0, wide))
    lon_cells = out_ref.shape[1]
    copies = []
    done = 0
    for first in range(0, lon_cells, GROUP):
        lons = min(GROUP, lon_cells - first)
        rows = slice(first * channels, (first + lons + 2) * channels)
        total = conv_rows(last_ref, ps, rows, lons * channels)
        for a in range(lons):
            lon_rows = total[a * channels : (a + 1) * channels]
            for tile in range(lat_cells // 128):
                lanes = slice(tile * 128, (tile + 1) * 128)
                placed[tile, pl.ds(first + a, channels, stride=lon_cells), :] = lon_rows[:, lanes]
        if first + lons >= done + HALF:
            part = slice(done, done + HALF)
            for tile in range(lat_cells // 128):
                lanes = slice(tile * 128, (tile + 1) * 128)
                block = placed[tile].reshape(channels, lon_cells, 128)[:, part, :]
                block = block + raw_ref[:, part, lanes].astype(F32)
                result[:, part, lanes] = block.astype(BF)
            copy = pltpu.make_async_copy(
                result.at[:, pl.ds(done, HALF), :], out_ref.at[:, pl.ds(done, HALF), :], sems.at[done // HALF]
            )
            copy.start()
            copies.append(copy)
            done += HALF
    for copy in copies:
        copy.wait()


def result_kernel(scale, mine_ref, other_ref, one_ref, two_ref):
    channels = one_ref.shape[2]
    odd = is_odd()
    first = jnp.where(odd == 0, mine_ref[...], other_ref[...]) * scale
    second = jnp.where(odd == 0, other_ref[...], mine_ref[...]) * scale
    first = unpack_taps(first, channels)
    second = unpack_taps(second, channels)
    for q in range(3):
        for p in range(3):
            lanes = slice(p * channels, (p + 1) * channels)
            one_ref[p, q] = first[q][:, lanes]
            two_ref[2 - p, 2 - q] = second[q][:, lanes].T


def pairs(counts, partner):
    lat_count, lon_count = counts
    listed = []
    for lat in range(lat_count):
        for lon in range(lon_count):
            to_lat, to_lon = partner(lat, lon)
            listed.append((lat * lon_count + lon, to_lat * lon_count + to_lon))
    return listed


def x_partner(mask):
    def partner(lat, lon):
        place = ((lat >> 1) * 2 + (lon >> 5)) ^ mask
        return (place >> 1) * 2 + (lat & 1), (place & 1) * 32 + (lon & 31)

    return partner


def y_partner(mask):
    return lambda lat, lon: (lat, lon ^ mask)


def z_partner(mask):
    return lambda lat, lon: (lat, lon ^ (mask << 2))


def exchange(value, partner):
    counts = (lax.axis_size("lat"), lax.axis_size("lon"))
    return lax.ppermute(value, ("lat", "lon"), pairs(counts, partner))


def sum_of_four(value, partner):
    near, far, wrap = [exchange(value, partner(mask)) for mask in (1, 2, 3)]
    return (value + near) + (far + wrap)


def sum_everywhere(halves, between):
    core = lax.axis_index("lat") % 2
    other_core = lambda lat, lon: (lat ^ 1, lon)
    mine = lax.dynamic_index_in_dim(halves, core, 0, False)
    theirs = lax.dynamic_index_in_dim(halves, 1 - core, 0, False)
    total = mine + exchange(theirs, other_core)
    total = sum_of_four(total, x_partner)
    total = sum_of_four(total, y_partner)
    total = sum_of_four(total, z_partner)
    far = exchange(total, z_partner(7))
    input_grad, total = between(total)
    total = total + far
    other = exchange(total, other_core)
    return total, other, input_grad


def lat_exchange(core, mid):
    count = lax.axis_size("lat")
    inner = [pair for low in range(1, count - 1, 2) for pair in ((low, low + 1), (low + 1, low))]
    return lax.ppermute(core, "lat", [(i, i ^ 1) for i in range(count)]), lax.ppermute(mid, "lat", inner)


def on_device(inputs, kernel_one, kernel_two, cotangent):
    channels, lon_cells, lat_cells = inputs.shape
    cells = lon_cells * lat_cells * lax.axis_size("lat") * lax.axis_size("lon")
    rows = channels * lon_cells
    two = 2 * channels
    weights = [shape(3, GROUP * channels, WINDOW * channels)] * 3
    x_rows, cot_rows, core_out, mid_out, first, back, last = call(
        pack_kernel,
        [shape(rows, lat_cells), shape(rows, lat_cells), shape(HALF, rows), shape(HALF, rows), *weights],
        [
            pltpu.VMEM((2 * lon_cells // HALF, channels, HALF, lat_cells), BF),
            pltpu.VMEM(kernel_one.shape, BF),
            pltpu.VMEM(kernel_two.shape, BF),
            pltpu.VMEM((HALF * channels, HALF * channels), BF),
            pltpu.SemaphoreType.DMA((2 + 4 * lon_cells // HALF,)),
        ],
        10**9,
        inputs,
        cotangent,
        kernel_one,
        kernel_two,
        hbm_in=(0, 1, 2, 3),
    )
    core_in, mid_in = lat_exchange(core_out, mid_out)

    def message(part):
        pieces = jnp.concatenate([core_in[:, part], mid_in[:, part]], 1)
        pieces = jnp.pad(pieces, ((0, 0), (0, lat_cells - 2 * two)))
        return jnp.concatenate([x_rows[part], cot_rows[part], pieces], 0)

    count = lax.axis_size("lon")
    to_left = message(slice(0, two))
    to_right = message(slice(rows - two, rows))
    from_left = lax.ppermute(to_right, "lon", [(i, (i + 1) % count) for i in range(count)])
    from_right = lax.ppermute(to_left, "lon", [((i + 1) % count, i) for i in range(count)])

    inner_rows = rows - two
    shifted = pltpu.VMEM((3, rows, lat_cells), BF)
    pre_inner, inner_grads = call(
        inner_kernel,
        [shape(inner_rows, lat_cells), shape(2, 3, channels, 128, dtype=F32)],
        [shifted, shifted, pltpu.VMEM((2, 3, GROUP * channels, WINDOW * channels), F32)],
        4 * 10**9,
        x_rows, cot_rows, core_in, mid_in, first, back,
    )
    edge_shifted = pltpu.VMEM((3, 2 * two, lat_cells), BF)
    pre_low, pre_high, grads = call(
        edge_kernel,
        [shape(two, lat_cells), shape(two, lat_cells), shape(2, 9 * channels * channels // 128, 128, dtype=F32)],
        [edge_shifted, edge_shifted],
        10**9,
        x_rows, cot_rows, core_in, mid_in, from_left, from_right, first, back, inner_grads,
    )
    def finish(partial):
        return call(
            last_kernel,
            [shape(channels, lon_cells, lat_cells), shape(*partial.shape, dtype=F32)],
            [
                pltpu.VMEM((rows + 2 * two, lat_cells), BF),
                pltpu.VMEM((2, HALF, rows + 2 * two), F32),
                pltpu.VMEM((3, rows + two, lat_cells), BF),
                pltpu.VMEM((lat_cells // 128, rows, 128), F32),
                pltpu.VMEM((channels, lon_cells, lat_cells), BF),
                pltpu.SemaphoreType.DMA((lon_cells // HALF,)),
            ],
            2 * 10**9,
            x_rows, cot_rows, core_in, mid_in, from_left, from_right, first, back,
            pre_low, pre_inner, pre_high, last, cotangent, partial,
            hbm_out=(0,),
        )

    mine, other, input_grad = sum_everywhere(grads, finish)
    grad_one, grad_two = call(
        functools.partial(result_kernel, 1.0 / math.sqrt(cells)),
        [shape(3, 3, channels, channels, dtype=F32)] * 2,
        [],
        10**6,
        mine,
        other,
    )
    return (input_grad, grad_one, grad_two)


def solution(mesh):
    placed = (P(None, "lon", "lat"), P(), P(), P(None, "lon", "lat"))
    return jax.shard_map(
        on_device,
        mesh=mesh,
        in_specs=placed,
        out_specs=(P(None, "lon", "lat"), P(), P()),
        check_vma=False,
    )
```

```python
import functools
import math

import jax
import jax.numpy as jnp
from jax import lax
from jax.experimental import pallas as pl
from jax.experimental.pallas import tpu as pltpu
from jax.sharding import PartitionSpec as P

BF = jnp.bfloat16
F32 = jnp.float32
GROUP = 6
WINDOW = GROUP + 2
HALF = 16
PARAMS = pltpu.CompilerParams(vmem_limit_bytes=16 * 2**20)


def dot(left, right):
    return lax.dot_general(left, right, (((1,), (0,)), ((), ())), preferred_element_type=F32)


def dot_lanes(left, right):
    return lax.dot_general(left, right, (((1,), (1,)), ((), ())), preferred_element_type=F32)


def dot_rows(left, right):
    return lax.dot_general(left, right, (((0,), (0,)), ((), ())), preferred_element_type=F32)


def iota(shape, dim):
    return lax.broadcasted_iota(jnp.int32, shape, dim)


def call(kernel, outs, scratch, flops, *operands, hbm_in=(), hbm_out=()):
    spaces = [pltpu.HBM if i in hbm_in else pltpu.VMEM for i in range(len(operands))]
    out_spaces = [pltpu.HBM if i in hbm_out else pltpu.VMEM for i in range(len(outs))]
    bytes_moved = sum(o.size * o.dtype.itemsize for o in (*operands, *outs))
    operands = [pltpu.with_memory_space_constraint(o, pltpu.HBM) if i in hbm_in else o for i, o in enumerate(operands)]
    return pl.pallas_call(
        kernel,
        out_shape=outs,
        in_specs=[pl.BlockSpec(memory_space=space) for space in spaces],
        out_specs=[pl.BlockSpec(memory_space=space) for space in out_spaces],
        scratch_shapes=scratch,
        compiler_params=PARAMS,
        cost_estimate=pl.CostEstimate(flops=flops, bytes_accessed=bytes_moved, transcendentals=0),
    )(*operands)


def shape(*dims, dtype=BF):
    return jax.ShapeDtypeStruct(dims, dtype)


def is_odd():
    return lax.axis_index("lat") % 2


def border_kernel(x_hbm, cot_hbm, one_hbm, two_hbm, raw_ref, one_ref, two_ref, perm_ref, core_ref, mid_ref, sems):
    channels, lon_cells, lat_cells = x_hbm.shape
    parts = lon_cells // HALF
    pieces = [(one_hbm, one_ref), (two_hbm, two_ref)]
    for place, source in enumerate((x_hbm, cot_hbm)):
        for part in range(parts):
            pieces.append((source.at[:, pl.ds(part * HALF, HALF), :], raw_ref.at[place * parts + part]))
    copies = [pltpu.make_async_copy(*piece, sems.at[number]) for number, piece in enumerate(pieces)]
    for copy in copies:
        copy.start()
    to_row = iota(perm_ref.shape, 0)
    from_row = iota(perm_ref.shape, 1)
    moved = (to_row % channels) * HALF + to_row // channels
    perm_ref[...] = jnp.where(from_row == moved, 1.0, 0.0).astype(BF)
    odd = is_odd()
    row = iota((2 * HALF, lat_cells), 0)
    lane = iota((2 * HALF, lat_cells), 1)
    high = jnp.where(row < HALF, 1 - odd, odd)
    cell = jnp.where(high == 1, lat_cells - 2, 0) + row % 2
    chosen = [
        (((row % HALF) // 2 == place) & (lane == cell)).astype(F32).astype(BF) for place in range(2)
    ]
    rows = HALF * channels
    for copy in copies:
        copy.wait()
    for part in range(parts):
        edges = sum(
            dot_lanes(chosen[place], raw_ref[place * parts + part].reshape(rows, lat_cells)) for place in range(2)
        )
        edges = dot_lanes(edges.astype(BF), perm_ref[...]).astype(BF)
        core_ref[:, part * rows : (part + 1) * rows] = edges[:HALF]
        mid_ref[:, part * rows : (part + 1) * rows] = edges[HALF:]


def row_kernel(raw_ref, perm_ref, one_ref, two_ref, xl_ref, cl_ref, first_ref, back_ref, last_ref):
    rows = perm_ref.shape[0]
    parts = xl_ref.shape[0] // rows
    for place, target in enumerate((xl_ref, cl_ref)):
        for part in range(parts):
            block = raw_ref[place * parts + part].reshape(rows, target.shape[1])
            target[part * rows : (part + 1) * rows, :] = dot(perm_ref[...], block).astype(BF)
    write_weights(one_ref, two_ref, first_ref, back_ref, last_ref)


def write_weights(one_ref, two_ref, first_ref, back_ref, last_ref):
    channels = one_ref.shape[2]
    lanes = WINDOW * channels
    tiled = (iota((channels, lanes), 1) % channels == iota((channels, lanes), 0)).astype(F32).astype(BF)
    block = iota((channels, lanes), 1) // channels
    for q in range(3):
        firsts = [dot(one_ref[p, q], tiled) for p in range(3)]
        backs = [dot_rows(two_ref[2 - p, 2 - q], tiled) for p in range(3)]
        lasts = [dot_rows(one_ref[2 - p, 2 - q], tiled) for p in range(3)]
        for bases, target in ((firsts, first_ref), (backs, back_ref), (lasts, last_ref)):
            for a in range(GROUP):
                band = jnp.zeros((channels, lanes), F32)
                for p in range(3):
                    band = jnp.where(block == a + p, bases[p], band)
                target[q, a * channels : (a + 1) * channels, :] = band.astype(BF)


def halo_place(odd, place, lat_cells):
    row = iota((2 * HALF, lat_cells), 0)
    lane = iota((2 * HALF, lat_cells), 1)
    from_low = jnp.where(row < HALF, odd, 1 - odd) == 1
    wanted_row = 2 * place + jnp.where(from_low, 1, 0)
    wanted_lane = jnp.where(from_low, 0, lat_cells - 1)
    return ((row % HALF == wanted_row) & (lane == wanted_lane)).astype(F32).astype(BF)


def write_shifted(values, edge_columns, target, rows):
    lat_cells = values.shape[1]
    lane = iota(values.shape, 1)
    wide = values.astype(F32)
    below = jnp.where(lane == 0, edge_columns, pltpu.roll(wide, 1, 1))
    above = jnp.where(lane == lat_cells - 1, edge_columns, pltpu.roll(wide, lat_cells - 1, 1))
    target[0, rows, :] = below.astype(BF)
    target[1, rows, :] = values
    target[2, rows, :] = above.astype(BF)


def activate(pre_act, back_grad):
    sigmoid_value = 0.5 * jnp.tanh(0.5 * pre_act) + 0.5
    activation = pre_act * sigmoid_value
    slope = sigmoid_value + activation * (1.0 - sigmoid_value)
    return activation, back_grad * slope


def conv_rows(weight_ref, shifted, rows, out_rows):
    count = rows.stop - rows.start
    return sum(dot(weight_ref[q, :out_rows, :count], shifted[q, rows, :]) for q in range(3))


def inner_kernel(x_ref, cot_ref, core_ref, mid_ref, first_ref, back_ref, pre_ref, grads_ref, xs, cs, total):
    lat_cells = x_ref.shape[1]
    channels = grads_ref.shape[2]
    odd = is_odd()
    halos = jnp.concatenate([core_ref[...], mid_ref[...]], 0)
    everything = slice(0, x_ref.shape[0])
    for place, (source, target) in enumerate(((x_ref, xs), (cot_ref, cs))):
        columns = dot_rows(halos, halo_place(odd, place, lat_cells))
        write_shifted(source[...], columns, target, everything)
    group_rows = GROUP * channels
    for k in range(pre_ref.shape[0] // group_rows):
        rows = slice(k * group_rows, k * group_rows + WINDOW * channels)
        pre_act = conv_rows(first_ref, xs, rows, group_rows)
        back_grad = conv_rows(back_ref, cs, rows, group_rows)
        activation, pre_grad = activate(pre_act, back_grad)
        activation = activation.astype(BF)
        pre_grad = pre_grad.astype(BF)
        pre_ref[k * group_rows : (k + 1) * group_rows, :] = pre_grad
        for q in range(3):
            for place, (own, raw) in enumerate(((pre_grad, xs), (activation, cs))):
                term = dot_lanes(own, raw[q, rows, :])
                if k == 0:
                    total[place, q] = term
                else:
                    total[place, q] += term
    for place in range(2):
        for q in range(3):
            summed = jnp.zeros((channels, WINDOW * channels), F32)
            for a in range(GROUP):
                band = total[place, q, a * channels : (a + 1) * channels, :]
                if a:
                    band = pltpu.roll(band, WINDOW * channels - a * channels, 1)
                summed = summed + band
            grads_ref[place, q] = summed[:, :128]


def edge_kernel(x_ref, cot_ref, core_ref, mid_ref, left_ref, right_ref, first_ref, back_ref, grads_ref,
                low_ref, high_ref, out_ref, xs, cs):
    lat_cells = x_ref.shape[1]
    channels = grads_ref.shape[2]
    odd = is_odd()
    two = 2 * channels
    own_rows = x_ref.shape[0]
    sums = [[grads_ref[place, q][:, : 3 * channels] for q in range(3)] for place in range(2)]
    for side, (message, target) in enumerate(((left_ref, low_ref), (right_ref, high_ref))):
        own = slice(0, two) if side == 0 else slice(own_rows - two, own_rows)
        sent = message[2 * two : 2 * two + HALF, :]
        sent_halos = jnp.concatenate([sent[:, :two], sent[:, two : 2 * two]], 0).astype(F32)
        own_halos = jnp.concatenate([core_ref[:, own], mid_ref[:, own]], 0).astype(F32)
        order = (sent_halos, own_halos) if side == 0 else (own_halos, sent_halos)
        halos = jnp.concatenate(order, 1).astype(BF)
        for place, (source, shifted) in enumerate(((x_ref, xs), (cot_ref, cs))):
            sent_rows = message[place * two : (place + 1) * two, :]
            order = (sent_rows, source[own, :]) if side == 0 else (source[own, :], sent_rows)
            columns = dot_rows(halos, halo_place(odd, place, lat_cells))
            write_shifted(jnp.concatenate(order, 0), columns, shifted, slice(0, 2 * two))
        rows = slice(0, 2 * two)
        pre_act = conv_rows(first_ref, xs, rows, two)
        back_grad = conv_rows(back_ref, cs, rows, two)
        activation, pre_grad = activate(pre_act, back_grad)
        pre_grad = pre_grad.astype(BF)
        target[...] = pre_grad
        mine = slice(channels, two) if side == 0 else slice(0, channels)
        near = slice(channels, 2 * two) if side == 0 else slice(0, 3 * channels)
        activation = activation[mine].astype(BF)
        pre_grad = pre_grad[mine]
        for q in range(3):
            sums[0][q] = sums[0][q] + dot_lanes(pre_grad, xs[q, near, :])
            sums[1][q] = sums[1][q] + dot_lanes(activation, cs[q, near, :])
    for place in range(2):
        pack_taps(sums[place], out_ref.at[place])


def pack_taps(taps, out_ref):
    channels = taps[0].shape[0]
    used = 3 * channels
    for q in range(2):
        out_ref[q * channels : (q + 1) * channels, :] = jnp.concatenate(
            [taps[q], taps[2][:, q * channels : (q + 1) * channels]], 1
        )
    rest = taps[2][:, 2 * channels : used]
    count = 128 // channels
    rows = channels // count
    out_ref[2 * channels :, :] = jnp.concatenate(
        [rest[i * rows : (i + 1) * rows] for i in range(count)], 1
    )


def unpack_taps(packed, channels):
    used = 3 * channels
    count = 128 // channels
    main = [packed[q * channels : (q + 1) * channels] for q in range(2)]
    rest = packed[2 * channels :]
    last = jnp.concatenate([rest[:, i * channels : (i + 1) * channels] for i in range(count)], 0)
    third = jnp.concatenate([main[0][:, used:], main[1][:, used:], last], 1)
    return [main[0], main[1], third]


def outer_kernel(x_ref, cot_ref, core_ref, mid_ref, left_ref, right_ref, first_ref, back_ref, low_ref, pre_ref,
                 high_ref, partial_ref, ps, passed_ref, rows_buffer, strips):
    passed_ref[...] = partial_ref[...]
    lat_cells = x_ref.shape[1]
    channels = low_ref.shape[0] // 2
    two = 2 * channels
    own_rows = x_ref.shape[0]
    wide_rows = own_rows + 2 * two
    odd = is_odd()
    core, mid = core_ref[...].astype(F32), mid_ref[...].astype(F32)
    lat = lax.axis_index("lat")
    lat_count = lax.axis_size("lat")

    def halo_lanes(value, first):
        parts = [left_ref[2 * two : 2 * two + HALF, first : first + two].astype(F32), value,
                 right_ref[2 * two : 2 * two + HALF, first : first + two].astype(F32)]
        return parts

    def put(target, parts):
        target[:, 0:two] = parts[0]
        target[:, two : two + own_rows] = parts[1]
        target[:, two + own_rows : wide_rows] = parts[2]

    put(strips.at[0], halo_lanes(core, 0))
    put(strips.at[1], halo_lanes(mid, two))
    core_wide, mid_wide = strips[0], strips[1]
    low = jnp.where(odd == 1, core_wide, mid_wide)
    high = jnp.where(odd == 1, mid_wide, core_wide)
    row = iota((HALF, lat_cells), 0)
    lane = iota((HALF, lat_cells), 1)
    ends = ((row < 2) & (lane == row * (lat_cells - 1))).astype(F32).astype(BF)
    values = []
    span = 4 * channels
    window = 6 * channels
    for place, (source, weight_ref) in enumerate(((x_ref, first_ref), (cot_ref, back_ref))):
        rows_buffer[0:two, :] = left_ref[place * two : (place + 1) * two, :]
        rows_buffer[two : two + own_rows, :] = source[...]
        rows_buffer[two + own_rows : wide_rows, :] = right_ref[place * two : (place + 1) * two, :]
        own = dot_lanes(ends, rows_buffer[...])
        low_rows = [low[2 * place : 2 * place + 1], low[2 * place + 1 : 2 * place + 2], own[0:1]]
        high_rows = [own[1:2], high[2 * place : 2 * place + 1], high[2 * place + 1 : 2 * place + 2]]
        total = None
        for q in range(3):
            which = iota((HALF, wide_rows), 0)
            strip = jnp.where(which == 0, low_rows[q], jnp.where(which == 1, high_rows[q], 0.0))
            strip = jnp.concatenate([strip, jnp.zeros((HALF, 128), F32)], 1)
            stacked = jnp.concatenate(
                [strip[:, k : k + window] for k in range(0, wide_rows, span)], 0
            ).astype(BF)
            term = dot_lanes(stacked, weight_ref[q, :span, :window])
            total = term if total is None else total + term
        values.append(total)
    _, pre_grad = activate(*values)
    beyond = jnp.where(iota(pre_grad.shape, 0) % HALF == 0, lat, lat_count - 1 - lat)
    pre_grad = jnp.where(beyond > 0, pre_grad, 0.0)
    pre_strip = jnp.concatenate(
        [pre_grad[k : k + HALF] for k in range(0, pre_grad.shape[0], HALF)], 1
    ).astype(BF)
    wide = pre_ref.shape[0] + 2 * two
    columns = dot_rows(pre_strip, ends)[:wide]
    rows_buffer[0:two, :] = low_ref[...]
    rows_buffer[two : wide - two, :] = pre_ref[...]
    rows_buffer[wide - two : wide, :] = high_ref[...]
    write_shifted(rows_buffer[0:wide, :], columns, ps, slice(0, wide))


def last_kernel(ps, last_ref, raw_ref, partial_ref, out_ref, passed_ref, placed, result, sems):
    passed_ref[...] = partial_ref[...]
    channels, lon_cells, lat_cells = out_ref.shape
    parts = lon_cells // HALF
    copies = []
    done = 0
    for first in range(0, lon_cells, GROUP):
        lons = min(GROUP, lon_cells - first)
        rows = slice(first * channels, (first + lons + 2) * channels)
        total = conv_rows(last_ref, ps, rows, lons * channels)
        for a in range(lons):
            lon_rows = total[a * channels : (a + 1) * channels]
            for tile in range(lat_cells // 128):
                lanes = slice(tile * 128, (tile + 1) * 128)
                placed[tile, pl.ds(first + a, channels, stride=lon_cells), :] = lon_rows[:, lanes]
        if first + lons >= done + HALF:
            part = slice(done, done + HALF)
            for tile in range(lat_cells // 128):
                lanes = slice(tile * 128, (tile + 1) * 128)
                block = placed[tile].reshape(channels, lon_cells, 128)[:, part, :]
                block = block + raw_ref[parts + done // HALF, :, :, lanes].astype(F32)
                result[:, part, lanes] = block.astype(BF)
            copy = pltpu.make_async_copy(
                result.at[:, pl.ds(done, HALF), :], out_ref.at[:, pl.ds(done, HALF), :], sems.at[done // HALF]
            )
            copy.start()
            copies.append(copy)
            done += HALF
    for copy in copies:
        copy.wait()


def result_kernel(scale, mine_ref, other_ref, one_ref, two_ref):
    channels = one_ref.shape[2]
    odd = is_odd()
    first = jnp.where(odd == 0, mine_ref[...], other_ref[...]) * scale
    second = jnp.where(odd == 0, other_ref[...], mine_ref[...]) * scale
    first = unpack_taps(first, channels)
    second = unpack_taps(second, channels)
    for q in range(3):
        for p in range(3):
            lanes = slice(p * channels, (p + 1) * channels)
            one_ref[p, q] = first[q][:, lanes]
            two_ref[2 - p, 2 - q] = second[q][:, lanes].T


def pairs(counts, partner):
    lat_count, lon_count = counts
    listed = []
    for lat in range(lat_count):
        for lon in range(lon_count):
            to_lat, to_lon = partner(lat, lon)
            listed.append((lat * lon_count + lon, to_lat * lon_count + to_lon))
    return listed


def x_partner(mask):
    def partner(lat, lon):
        place = ((lat >> 1) * 2 + (lon >> 5)) ^ mask
        return (place >> 1) * 2 + (lat & 1), (place & 1) * 32 + (lon & 31)

    return partner


def y_partner(mask):
    return lambda lat, lon: (lat, lon ^ mask)


def z_partner(mask):
    return lambda lat, lon: (lat, lon ^ (mask << 2))


def exchange(value, partner):
    counts = (lax.axis_size("lat"), lax.axis_size("lon"))
    return lax.ppermute(value, ("lat", "lon"), pairs(counts, partner))


def sum_of_four(value, partner, masks, beside=None):
    first, second, third = [exchange(value, partner(mask)) for mask in masks]
    result = None
    if beside is not None:
        result, value = beside(value)
    return (value + first) + (second + third), result


def sum_everywhere(halves, widen, finish):
    core = lax.axis_index("lat") % 2
    other_core = lambda lat, lon: (lat ^ 1, lon)
    mine = lax.dynamic_index_in_dim(halves, core, 0, False)
    theirs = lax.dynamic_index_in_dim(halves, 1 - core, 0, False)
    total = mine + exchange(theirs, other_core)
    total, _ = sum_of_four(total, x_partner, (1, 3, 2))
    total, shifted = sum_of_four(total, y_partner, (1, 3, 2), widen)
    total, _ = sum_of_four(total, z_partner, (1, 2, 3))
    far = exchange(total, z_partner(7))
    input_grad, total = finish(shifted, total)
    total = total + far
    other = exchange(total, other_core)
    return total, other, input_grad


def lat_exchange(core, mid):
    count = lax.axis_size("lat")
    inner = [pair for low in range(1, count - 1, 2) for pair in ((low, low + 1), (low + 1, low))]
    mid = lax.ppermute(mid, "lat", inner)
    return lax.ppermute(core, "lat", [(i, i ^ 1) for i in range(count)]), mid


def on_device(inputs, kernel_one, kernel_two, cotangent):
    channels, lon_cells, lat_cells = inputs.shape
    cells = lon_cells * lat_cells * lax.axis_size("lat") * lax.axis_size("lon")
    rows = channels * lon_cells
    two = 2 * channels
    parts = lon_cells // HALF
    weights = [shape(3, GROUP * channels, WINDOW * channels)] * 3
    raw, one, two_kernel, perm, core_out, mid_out = call(
        border_kernel,
        [
            shape(2 * parts, channels, HALF, lat_cells),
            shape(*kernel_one.shape),
            shape(*kernel_two.shape),
            shape(HALF * channels, HALF * channels),
            shape(HALF, rows),
            shape(HALF, rows),
        ],
        [pltpu.SemaphoreType.DMA((2 + 2 * parts,))],
        10**8,
        inputs,
        cotangent,
        kernel_one,
        kernel_two,
        hbm_in=(0, 1, 2, 3),
    )
    core_in, mid_in = lat_exchange(core_out, mid_out)
    x_rows, cot_rows, first, back, last = call(
        row_kernel,
        [shape(rows, lat_cells), shape(rows, lat_cells), *weights],
        [],
        10**9,
        raw,
        perm,
        one,
        two_kernel,
    )

    def message(part):
        pieces = jnp.concatenate([core_in[:, part], mid_in[:, part]], 1)
        pieces = jnp.pad(pieces, ((0, 0), (0, lat_cells - 2 * two)))
        return jnp.concatenate([x_rows[part], cot_rows[part], pieces], 0)

    count = lax.axis_size("lon")
    to_left = message(slice(0, two))
    to_right = message(slice(rows - two, rows))
    from_left = lax.ppermute(to_right, "lon", [(i, (i + 1) % count) for i in range(count)])
    from_right = lax.ppermute(to_left, "lon", [((i + 1) % count, i) for i in range(count)])

    inner_rows = rows - two
    shifted = pltpu.VMEM((3, rows, lat_cells), BF)
    pre_inner, inner_grads = call(
        inner_kernel,
        [shape(inner_rows, lat_cells), shape(2, 3, channels, 128, dtype=F32)],
        [shifted, shifted, pltpu.VMEM((2, 3, GROUP * channels, WINDOW * channels), F32)],
        4 * 10**9,
        x_rows, cot_rows, core_in, mid_in, first, back,
    )
    edge_shifted = pltpu.VMEM((3, 2 * two, lat_cells), BF)
    pre_low, pre_high, grads = call(
        edge_kernel,
        [shape(two, lat_cells), shape(two, lat_cells), shape(2, 9 * channels * channels // 128, 128, dtype=F32)],
        [edge_shifted, edge_shifted],
        10**9,
        x_rows, cot_rows, core_in, mid_in, from_left, from_right, first, back, inner_grads,
    )
    def widen(partial):
        return call(
            outer_kernel,
            [shape(3, rows + two, lat_cells), shape(*partial.shape, dtype=F32)],
            [
                pltpu.VMEM((rows + 2 * two, lat_cells), BF),
                pltpu.VMEM((2, HALF, rows + 2 * two), F32),
            ],
            10**9,
            x_rows, cot_rows, core_in, mid_in, from_left, from_right, first, back,
            pre_low, pre_inner, pre_high, partial,
        )

    def finish(shifted, partial):
        return call(
            last_kernel,
            [shape(channels, lon_cells, lat_cells), shape(*partial.shape, dtype=F32)],
            [
                pltpu.VMEM((lat_cells // 128, rows, 128), F32),
                pltpu.VMEM((channels, lon_cells, lat_cells), BF),
                pltpu.SemaphoreType.DMA((lon_cells // HALF,)),
            ],
            2 * 10**9,
            shifted, last, raw, partial,
            hbm_out=(0,),
        )

    mine, other, input_grad = sum_everywhere(grads, widen, finish)
    grad_one, grad_two = call(
        functools.partial(result_kernel, 1.0 / math.sqrt(cells)),
        [shape(3, 3, channels, channels, dtype=F32)] * 2,
        [],
        10**6,
        mine,
        other,
    )
    return (input_grad, grad_one, grad_two)


def solution(mesh):
    placed = (P(None, "lon", "lat"), P(), P(), P(None, "lon", "lat"))
    return jax.shard_map(
        on_device,
        mesh=mesh,
        in_specs=placed,
        out_specs=(P(None, "lon", "lat"), P(), P()),
        check_vma=False,
    )
```

```python
import functools
import math

import jax
import jax.numpy as jnp
from jax import lax
from jax.experimental import pallas as pl
from jax.experimental.pallas import tpu as pltpu
from jax.sharding import PartitionSpec as P

BF = jnp.bfloat16
F32 = jnp.float32
GROUP = 6
WINDOW = GROUP + 2
HALF = 16
PARAMS = pltpu.CompilerParams(vmem_limit_bytes=16 * 2**20)


def dot(left, right):
    return lax.dot_general(left, right, (((1,), (0,)), ((), ())), preferred_element_type=F32)


def dot_lanes(left, right):
    return lax.dot_general(left, right, (((1,), (1,)), ((), ())), preferred_element_type=F32)


def dot_rows(left, right):
    return lax.dot_general(left, right, (((0,), (0,)), ((), ())), preferred_element_type=F32)


def iota(shape, dim):
    return lax.broadcasted_iota(jnp.int32, shape, dim)


def call(kernel, outs, scratch, flops, *operands, hbm_in=(), hbm_out=()):
    spaces = [pltpu.HBM if i in hbm_in else pltpu.VMEM for i in range(len(operands))]
    out_spaces = [pltpu.HBM if i in hbm_out else pltpu.VMEM for i in range(len(outs))]
    bytes_moved = sum(o.size * o.dtype.itemsize for o in (*operands, *outs))
    operands = [pltpu.with_memory_space_constraint(o, pltpu.HBM) if i in hbm_in else o for i, o in enumerate(operands)]
    return pl.pallas_call(
        kernel,
        out_shape=outs,
        in_specs=[pl.BlockSpec(memory_space=space) for space in spaces],
        out_specs=[pl.BlockSpec(memory_space=space) for space in out_spaces],
        scratch_shapes=scratch,
        compiler_params=PARAMS,
        cost_estimate=pl.CostEstimate(flops=flops, bytes_accessed=bytes_moved, transcendentals=0),
    )(*operands)


def shape(*dims, dtype=BF):
    return jax.ShapeDtypeStruct(dims, dtype)


def is_odd():
    return lax.axis_index("lat") % 2


def border_kernel(x_hbm, cot_hbm, one_hbm, two_hbm, raw_ref, one_ref, two_ref, perm_ref, core_ref, mid_ref, sems):
    channels, lon_cells, lat_cells = x_hbm.shape
    parts = lon_cells // HALF
    pieces = [(one_hbm, one_ref), (two_hbm, two_ref)]
    for place, source in enumerate((x_hbm, cot_hbm)):
        for part in range(parts):
            pieces.append((source.at[:, pl.ds(part * HALF, HALF), :], raw_ref.at[place * parts + part]))
    copies = [pltpu.make_async_copy(*piece, sems.at[number]) for number, piece in enumerate(pieces)]
    for copy in copies:
        copy.start()
    to_row = iota(perm_ref.shape, 0)
    from_row = iota(perm_ref.shape, 1)
    moved = (to_row % channels) * HALF + to_row // channels
    perm_ref[...] = jnp.where(from_row == moved, 1.0, 0.0).astype(BF)
    odd = is_odd()
    row = iota((2 * HALF, lat_cells), 0)
    lane = iota((2 * HALF, lat_cells), 1)
    high = jnp.where(row < HALF, 1 - odd, odd)
    cell = jnp.where(high == 1, lat_cells - 2, 0) + row % 2
    chosen = [
        (((row % HALF) // 2 == place) & (lane == cell)).astype(F32).astype(BF) for place in range(2)
    ]
    rows = HALF * channels
    for copy in copies:
        copy.wait()
    for part in range(parts):
        edges = sum(
            dot_lanes(chosen[place], raw_ref[place * parts + part].reshape(rows, lat_cells)) for place in range(2)
        )
        edges = dot_lanes(edges.astype(BF), perm_ref[...]).astype(BF)
        core_ref[:, part * rows : (part + 1) * rows] = edges[:HALF]
        mid_ref[:, part * rows : (part + 1) * rows] = edges[HALF:]


def row_kernel(raw_ref, perm_ref, one_ref, two_ref, xl_ref, cl_ref, first_ref, back_ref):
    rows = perm_ref.shape[0]
    parts = xl_ref.shape[0] // rows
    for place, target in enumerate((xl_ref, cl_ref)):
        for part in range(parts):
            block = raw_ref[place * parts + part].reshape(rows, target.shape[1])
            target[part * rows : (part + 1) * rows, :] = dot(perm_ref[...], block).astype(BF)
    write_band(one_ref, False, first_ref)
    write_band(two_ref, True, back_ref)


def write_band(kernel, transposed, target):
    channels = kernel.shape[2]
    lanes = WINDOW * channels
    tiled = (iota((channels, lanes), 1) % channels == iota((channels, lanes), 0)).astype(F32).astype(BF)
    block = iota((channels, lanes), 1) // channels
    for q in range(3):
        if transposed:
            bases = [dot_rows(kernel[2 - p, 2 - q], tiled) for p in range(3)]
        else:
            bases = [dot(kernel[p, q], tiled) for p in range(3)]
        for a in range(GROUP):
            band = jnp.zeros((channels, lanes), F32)
            for p in range(3):
                band = jnp.where(block == a + p, bases[p], band)
            target[q, a * channels : (a + 1) * channels, :] = band.astype(BF)


def halo_place(odd, place, lat_cells):
    row = iota((2 * HALF, lat_cells), 0)
    lane = iota((2 * HALF, lat_cells), 1)
    from_low = jnp.where(row < HALF, odd, 1 - odd) == 1
    wanted_row = 2 * place + jnp.where(from_low, 1, 0)
    wanted_lane = jnp.where(from_low, 0, lat_cells - 1)
    lat = lax.axis_index("lat")
    inside = jnp.where(row < HALF, 1, lat * (lax.axis_size("lat") - 1 - lat))
    return ((row % HALF == wanted_row) & (lane == wanted_lane) & (inside > 0)).astype(F32).astype(BF)


def write_shifted(values, edge_columns, target, rows):
    lat_cells = values.shape[1]
    lane = iota(values.shape, 1)
    columns = edge_columns.astype(BF)
    target[0, rows, :] = jnp.where(lane == 0, columns, pltpu.roll(values, 1, 1))
    target[1, rows, :] = values
    target[2, rows, :] = jnp.where(lane == lat_cells - 1, columns, pltpu.roll(values, lat_cells - 1, 1))


def activate(pre_act, back_grad):
    sigmoid_value = 0.5 * jnp.tanh(0.5 * pre_act) + 0.5
    activation = pre_act * sigmoid_value
    slope = sigmoid_value + activation * (1.0 - sigmoid_value)
    return activation, back_grad * slope


def conv_rows(weight_ref, shifted, rows, out_rows):
    count = rows.stop - rows.start
    return sum(dot(weight_ref[q, :out_rows, :count], shifted[q, rows, :]) for q in range(3))


def inner_kernel(x_ref, cot_ref, core_ref, mid_ref, first_ref, back_ref, pre_ref, grads_ref, xs, cs, total):
    lat_cells = x_ref.shape[1]
    channels = grads_ref.shape[2]
    odd = is_odd()
    halos = jnp.concatenate([core_ref[...], mid_ref[...]], 0)
    everything = slice(0, x_ref.shape[0])
    for place, (source, target) in enumerate(((x_ref, xs), (cot_ref, cs))):
        columns = dot_rows(halos, halo_place(odd, place, lat_cells))
        write_shifted(source[...], columns, target, everything)
    group_rows = GROUP * channels
    for k in range(pre_ref.shape[0] // group_rows):
        rows = slice(k * group_rows, k * group_rows + WINDOW * channels)
        pre_act = conv_rows(first_ref, xs, rows, group_rows)
        back_grad = conv_rows(back_ref, cs, rows, group_rows)
        activation, pre_grad = activate(pre_act, back_grad)
        activation = activation.astype(BF)
        pre_grad = pre_grad.astype(BF)
        pre_ref[k * group_rows : (k + 1) * group_rows, :] = pre_grad
        for q in range(3):
            for place, (own, raw) in enumerate(((pre_grad, xs), (activation, cs))):
                term = dot_lanes(own, raw[q, rows, :])
                if k == 0:
                    total[place, q] = term
                else:
                    total[place, q] += term
    for place in range(2):
        for q in range(3):
            summed = jnp.zeros((channels, WINDOW * channels), F32)
            for a in range(GROUP):
                band = total[place, q, a * channels : (a + 1) * channels, :]
                if a:
                    band = pltpu.roll(band, WINDOW * channels - a * channels, 1)
                summed = summed + band
            grads_ref[place, q] = summed[:, :128]


def edge_kernel(x_ref, cot_ref, core_ref, mid_ref, left_ref, right_ref, first_ref, back_ref, grads_ref,
                low_ref, high_ref, out_ref, xs_sides, cs_sides):
    lat_cells = x_ref.shape[1]
    channels = grads_ref.shape[2]
    odd = is_odd()
    two = 2 * channels
    own_rows = x_ref.shape[0]
    sums = [[grads_ref[place, q][:, : 3 * channels] for q in range(3)] for place in range(2)]
    for side, (message, target) in enumerate(((left_ref, low_ref), (right_ref, high_ref))):
        xs, cs = xs_sides.at[side], cs_sides.at[side]
        own = slice(0, two) if side == 0 else slice(own_rows - two, own_rows)
        sent = message[2 * two : 2 * two + HALF, :]
        sent_halos = jnp.concatenate([sent[:, :two], sent[:, two : 2 * two]], 0).astype(F32)
        own_halos = jnp.concatenate([core_ref[:, own], mid_ref[:, own]], 0).astype(F32)
        order = (sent_halos, own_halos) if side == 0 else (own_halos, sent_halos)
        halos = jnp.concatenate(order, 1).astype(BF)
        for place, (source, shifted) in enumerate(((x_ref, xs), (cot_ref, cs))):
            sent_rows = message[place * two : (place + 1) * two, :]
            order = (sent_rows, source[own, :]) if side == 0 else (source[own, :], sent_rows)
            columns = dot_rows(halos, halo_place(odd, place, lat_cells))
            write_shifted(jnp.concatenate(order, 0), columns, shifted, slice(0, 2 * two))
        rows = slice(0, 2 * two)
        pre_act = conv_rows(first_ref, xs, rows, two)
        back_grad = conv_rows(back_ref, cs, rows, two)
        activation, pre_grad = activate(pre_act, back_grad)
        pre_grad = pre_grad.astype(BF)
        target[...] = pre_grad
        mine = slice(channels, two) if side == 0 else slice(0, channels)
        near = slice(channels, 2 * two) if side == 0 else slice(0, 3 * channels)
        activation = activation[mine].astype(BF)
        pre_grad = pre_grad[mine]
        for q in range(3):
            sums[0][q] = sums[0][q] + dot_lanes(pre_grad, xs[q, near, :])
            sums[1][q] = sums[1][q] + dot_lanes(activation, cs[q, near, :])
    out_ref[...] = jnp.concatenate([pack_taps(taps) for taps in sums], 0)


def pack_taps(taps):
    channels = taps[0].shape[0]
    main = [
        jnp.concatenate([taps[q], taps[2][:, q * channels : (q + 1) * channels]], 1) for q in range(2)
    ]
    rest = taps[2][:, 2 * channels :]
    count = 128 // channels
    rows = channels // count
    last = jnp.concatenate([rest[i * rows : (i + 1) * rows] for i in range(count)], 1)
    return jnp.concatenate([*main, last], 0)


def unpack_taps(packed, channels):
    used = 3 * channels
    count = 128 // channels
    main = [packed[q * channels : (q + 1) * channels] for q in range(2)]
    rest = packed[2 * channels :]
    last = jnp.concatenate([rest[:, i * channels : (i + 1) * channels] for i in range(count)], 0)
    third = jnp.concatenate([main[0][:, used:], main[1][:, used:], last], 1)
    return [main[0], main[1], third]


def outer_kernel(x_ref, cot_ref, core_ref, mid_ref, left_ref, right_ref, first_ref, back_ref, low_ref, pre_ref,
                 high_ref, one_ref, partial_ref, ps, last_ref, passed_ref, rows_buffer, strips):
    passed_ref[...] = partial_ref[...]
    write_band(one_ref, True, last_ref)
    lat_cells = x_ref.shape[1]
    channels = low_ref.shape[0] // 2
    two = 2 * channels
    own_rows = x_ref.shape[0]
    wide_rows = own_rows + 2 * two
    odd = is_odd()
    core, mid = core_ref[...].astype(F32), mid_ref[...].astype(F32)
    lat = lax.axis_index("lat")
    lat_count = lax.axis_size("lat")

    def halo_lanes(value, first):
        parts = [left_ref[2 * two : 2 * two + HALF, first : first + two].astype(F32), value,
                 right_ref[2 * two : 2 * two + HALF, first : first + two].astype(F32)]
        return parts

    def put(target, parts):
        target[:, 0:two] = parts[0]
        target[:, two : two + own_rows] = parts[1]
        target[:, two + own_rows : wide_rows] = parts[2]

    put(strips.at[0], halo_lanes(core, 0))
    put(strips.at[1], halo_lanes(mid, two))
    core_wide, mid_wide = strips[0], strips[1]
    low = jnp.where(odd == 1, core_wide, mid_wide)
    high = jnp.where(odd == 1, mid_wide, core_wide)
    row = iota((HALF, lat_cells), 0)
    lane = iota((HALF, lat_cells), 1)
    ends = ((row < 2) & (lane == row * (lat_cells - 1))).astype(F32).astype(BF)
    values = []
    span = 4 * channels
    window = 6 * channels
    for place, (source, weight_ref) in enumerate(((x_ref, first_ref), (cot_ref, back_ref))):
        rows_buffer[0:two, :] = left_ref[place * two : (place + 1) * two, :]
        rows_buffer[two : two + own_rows, :] = source[...]
        rows_buffer[two + own_rows : wide_rows, :] = right_ref[place * two : (place + 1) * two, :]
        own = dot_lanes(ends, rows_buffer[...])
        low_rows = [low[2 * place : 2 * place + 1], low[2 * place + 1 : 2 * place + 2], own[0:1]]
        high_rows = [own[1:2], high[2 * place : 2 * place + 1], high[2 * place + 1 : 2 * place + 2]]
        total = None
        for q in range(3):
            which = iota((HALF, wide_rows), 0)
            strip = jnp.where(which == 0, low_rows[q], jnp.where(which == 1, high_rows[q], 0.0))
            strip = jnp.concatenate([strip, jnp.zeros((HALF, 128), F32)], 1)
            stacked = jnp.concatenate(
                [strip[:, k : k + window] for k in range(0, wide_rows, span)], 0
            ).astype(BF)
            term = dot_lanes(stacked, weight_ref[q, :span, :window])
            total = term if total is None else total + term
        values.append(total)
    _, pre_grad = activate(*values)
    beyond = jnp.where(iota(pre_grad.shape, 0) % HALF == 0, lat, lat_count - 1 - lat)
    pre_grad = jnp.where(beyond > 0, pre_grad, 0.0)
    pre_strip = jnp.concatenate(
        [pre_grad[k : k + HALF] for k in range(0, pre_grad.shape[0], HALF)], 1
    ).astype(BF)
    wide = pre_ref.shape[0] + 2 * two
    columns = dot_rows(pre_strip, ends)[:wide]
    rows_buffer[0:two, :] = low_ref[...]
    rows_buffer[two : wide - two, :] = pre_ref[...]
    rows_buffer[wide - two : wide, :] = high_ref[...]
    write_shifted(rows_buffer[0:wide, :], columns, ps, slice(0, wide))


def last_kernel(ps, last_ref, raw_ref, partial_ref, out_ref, passed_ref, placed, result, sems):
    passed_ref[...] = partial_ref[...]
    channels, lon_cells, lat_cells = out_ref.shape
    parts = lon_cells // HALF
    copies = []
    done = 0
    for first in range(0, lon_cells, GROUP):
        lons = min(GROUP, lon_cells - first)
        rows = slice(first * channels, (first + lons + 2) * channels)
        total = conv_rows(last_ref, ps, rows, lons * channels)
        for a in range(lons):
            lon_rows = total[a * channels : (a + 1) * channels]
            for tile in range(lat_cells // 128):
                lanes = slice(tile * 128, (tile + 1) * 128)
                placed[tile, pl.ds(first + a, channels, stride=lon_cells), :] = lon_rows[:, lanes]
        if first + lons >= done + HALF:
            part = slice(done, done + HALF)
            for tile in range(lat_cells // 128):
                lanes = slice(tile * 128, (tile + 1) * 128)
                block = placed[tile].reshape(channels, lon_cells, 128)[:, part, :]
                block = block + raw_ref[parts + done // HALF, :, :, lanes].astype(F32)
                result[:, part, lanes] = block.astype(BF)
            copy = pltpu.make_async_copy(
                result.at[:, pl.ds(done, HALF), :], out_ref.at[:, pl.ds(done, HALF), :], sems.at[done // HALF]
            )
            copy.start()
            copies.append(copy)
            done += HALF
    for copy in copies:
        copy.wait()


def result_kernel(scale, total_ref, given_ref, one_ref, two_ref):
    channels = one_ref.shape[2]
    rows = total_ref.shape[0] // 2
    sums = jnp.where(is_odd() == 1, total_ref[...], given_ref[...]) * scale
    first, second = sums[:rows], sums[rows:]
    first = unpack_taps(first, channels)
    second = unpack_taps(second, channels)
    for q in range(3):
        for p in range(3):
            lanes = slice(p * channels, (p + 1) * channels)
            one_ref[p, q] = first[q][:, lanes]
            two_ref[2 - p, 2 - q] = second[q][:, lanes].T


def pairs(counts, partner):
    lat_count, lon_count = counts
    listed = []
    for lat in range(lat_count):
        for lon in range(lon_count):
            to_lat, to_lon = partner(lat, lon) if lat % 2 else (lat, lon ^ 32)
            listed.append((lat * lon_count + lon, to_lat * lon_count + to_lon))
    return listed


def x_partner(mask):
    def partner(lat, lon):
        place = ((lat >> 1) * 2 + (lon >> 5)) ^ mask
        return (place >> 1) * 2 + (lat & 1), (place & 1) * 32 + (lon & 31)

    return partner


def y_partner(mask):
    return lambda lat, lon: (lat, lon ^ mask)


def z_partner(mask):
    return lambda lat, lon: (lat, lon ^ (mask << 2))


def exchange(value, partner):
    counts = (lax.axis_size("lat"), lax.axis_size("lon"))
    return lax.ppermute(value, ("lat", "lon"), pairs(counts, partner))


def sum_of_four(value, partner, masks, beside=None):
    first, second, third = [exchange(value, partner(mask)) for mask in masks]
    result = None
    if beside is not None:
        *result, value = beside(value)
    return (value + first) + (second + third), result


def sum_everywhere(mine, widen, finish):
    swap = [(lat, lat ^ 1) for lat in range(lax.axis_size("lat"))]
    total = mine + lax.ppermute(mine, "lat", swap)
    total, _ = sum_of_four(total, x_partner, (1, 3, 2))
    total, shifted = sum_of_four(total, y_partner, (1, 3, 2), widen)
    total, _ = sum_of_four(total, z_partner, (1, 2, 3))
    far = exchange(total, z_partner(6))
    input_grad, total = finish(*shifted, total)
    total = total + far
    given = lax.ppermute(total, "lat", swap)
    return total, given, input_grad


def lat_exchange(core, mid):
    count = lax.axis_size("lat")
    mid = lax.ppermute(mid, "lat", [(i, (i - 1 if i % 2 == 0 else i + 1) % count) for i in range(count)])
    return lax.ppermute(core, "lat", [(i, i ^ 1) for i in range(count)]), mid


def on_device(inputs, kernel_one, kernel_two, cotangent):
    channels, lon_cells, lat_cells = inputs.shape
    cells = lon_cells * lat_cells * lax.axis_size("lat") * lax.axis_size("lon")
    rows = channels * lon_cells
    two = 2 * channels
    parts = lon_cells // HALF
    weights = shape(3, GROUP * channels, WINDOW * channels)
    raw, one, two_kernel, perm, core_out, mid_out = call(
        border_kernel,
        [
            shape(2 * parts, channels, HALF, lat_cells),
            shape(*kernel_one.shape),
            shape(*kernel_two.shape),
            shape(HALF * channels, HALF * channels),
            shape(HALF, rows),
            shape(HALF, rows),
        ],
        [pltpu.SemaphoreType.DMA((2 + 2 * parts,))],
        10**8,
        inputs,
        cotangent,
        kernel_one,
        kernel_two,
        hbm_in=(0, 1, 2, 3),
    )
    core_in, mid_in = lat_exchange(core_out, mid_out)
    x_rows, cot_rows, first, back = call(
        row_kernel,
        [shape(rows, lat_cells), shape(rows, lat_cells), weights, weights],
        [],
        10**9,
        raw,
        perm,
        one,
        two_kernel,
    )

    def message(part):
        pieces = jnp.concatenate([core_in[:, part], mid_in[:, part]], 1)
        pieces = jnp.pad(pieces, ((0, 0), (0, lat_cells - 2 * two)))
        return jnp.concatenate([x_rows[part], cot_rows[part], pieces], 0)

    count = lax.axis_size("lon")
    to_left = message(slice(0, two))
    to_right = message(slice(rows - two, rows))
    from_left = lax.ppermute(to_right, "lon", [(i, (i + 1) % count) for i in range(count)])
    from_right = lax.ppermute(to_left, "lon", [((i + 1) % count, i) for i in range(count)])

    inner_rows = rows - two
    shifted = pltpu.VMEM((3, rows, lat_cells), BF)
    pre_inner, inner_grads = call(
        inner_kernel,
        [shape(inner_rows, lat_cells), shape(2, 3, channels, 128, dtype=F32)],
        [shifted, shifted, pltpu.VMEM((2, 3, GROUP * channels, WINDOW * channels), F32)],
        4 * 10**9,
        x_rows, cot_rows, core_in, mid_in, first, back,
    )
    edge_shifted = pltpu.VMEM((2, 3, 2 * two, lat_cells), BF)
    partial = shape(2 * 9 * channels * channels // 128, 128, dtype=F32)
    pre_low, pre_high, grads = call(
        edge_kernel,
        [shape(two, lat_cells), shape(two, lat_cells), partial],
        [edge_shifted, edge_shifted],
        10**9,
        x_rows, cot_rows, core_in, mid_in, from_left, from_right, first, back, inner_grads,
    )
    def widen(partial):
        return call(
            outer_kernel,
            [shape(3, rows + two, lat_cells), weights, shape(*partial.shape, dtype=F32)],
            [
                pltpu.VMEM((rows + 2 * two, lat_cells), BF),
                pltpu.VMEM((2, HALF, rows + 2 * two), F32),
            ],
            10**9,
            x_rows, cot_rows, core_in, mid_in, from_left, from_right, first, back,
            pre_low, pre_inner, pre_high, one, partial,
        )

    def finish(shifted, last, partial):
        return call(
            last_kernel,
            [shape(channels, lon_cells, lat_cells), shape(*partial.shape, dtype=F32)],
            [
                pltpu.VMEM((lat_cells // 128, rows, 128), F32),
                pltpu.VMEM((channels, lon_cells, lat_cells), BF),
                pltpu.SemaphoreType.DMA((lon_cells // HALF,)),
            ],
            2 * 10**9,
            shifted, last, raw, partial,
            hbm_out=(0,),
        )

    total, given, input_grad = sum_everywhere(grads, widen, finish)
    grad_one, grad_two = call(
        functools.partial(result_kernel, 1.0 / math.sqrt(cells)),
        [shape(3, 3, channels, channels, dtype=F32)] * 2,
        [],
        10**6,
        total,
        given,
    )
    return (input_grad, grad_one, grad_two)


def solution(mesh):
    placed = (P(None, "lon", "lat"), P(), P(), P(None, "lon", "lat"))
    return jax.shard_map(
        on_device,
        mesh=mesh,
        in_specs=placed,
        out_specs=(P(None, "lon", "lat"), P(), P()),
        check_vma=False,
    )
```

```python
import functools
import math

import jax
import jax.numpy as jnp
from jax import lax
from jax.experimental import pallas as pl
from jax.experimental.pallas import tpu as pltpu
from jax.sharding import PartitionSpec as P

BF = jnp.bfloat16
F32 = jnp.float32
GROUP = 6
WINDOW = GROUP + 2
HALF = 16
PARAMS = pltpu.CompilerParams(vmem_limit_bytes=16 * 2**20)


def dot(left, right):
    return lax.dot_general(left, right, (((1,), (0,)), ((), ())), preferred_element_type=F32)


def dot_lanes(left, right):
    return lax.dot_general(left, right, (((1,), (1,)), ((), ())), preferred_element_type=F32)


def dot_rows(left, right):
    return lax.dot_general(left, right, (((0,), (0,)), ((), ())), preferred_element_type=F32)


def iota(shape, dim):
    return lax.broadcasted_iota(jnp.int32, shape, dim)


def call(kernel, outs, scratch, flops, *operands, hbm_in=(), hbm_out=()):
    spaces = [pltpu.HBM if i in hbm_in else pltpu.VMEM for i in range(len(operands))]
    out_spaces = [pltpu.HBM if i in hbm_out else pltpu.VMEM for i in range(len(outs))]
    bytes_moved = sum(o.size * o.dtype.itemsize for o in (*operands, *outs))
    operands = [pltpu.with_memory_space_constraint(o, pltpu.HBM) if i in hbm_in else o for i, o in enumerate(operands)]
    return pl.pallas_call(
        kernel,
        out_shape=outs,
        in_specs=[pl.BlockSpec(memory_space=space) for space in spaces],
        out_specs=[pl.BlockSpec(memory_space=space) for space in out_spaces],
        scratch_shapes=scratch,
        compiler_params=PARAMS,
        cost_estimate=pl.CostEstimate(flops=flops, bytes_accessed=bytes_moved, transcendentals=0),
    )(*operands)


def shape(*dims, dtype=BF):
    return jax.ShapeDtypeStruct(dims, dtype)


def is_odd():
    return lax.axis_index("lat") % 2


def border_kernel(x_hbm, cot_hbm, one_hbm, two_hbm, raw_ref, one_ref, two_ref, perm_ref, core_ref, mid_ref, sems):
    channels, lon_cells, lat_cells = x_hbm.shape
    parts = lon_cells // HALF
    pieces = [(one_hbm, one_ref), (two_hbm, two_ref)]
    for place, source in enumerate((x_hbm, cot_hbm)):
        for part in range(parts):
            pieces.append((source.at[:, pl.ds(part * HALF, HALF), :], raw_ref.at[place * parts + part]))
    copies = [pltpu.make_async_copy(*piece, sems.at[number]) for number, piece in enumerate(pieces)]
    for copy in copies:
        copy.start()
    to_row = iota(perm_ref.shape, 0)
    from_row = iota(perm_ref.shape, 1)
    moved = (to_row % channels) * HALF + to_row // channels
    perm_ref[...] = jnp.where(from_row == moved, 1.0, 0.0).astype(BF)
    odd = is_odd()
    row = iota((2 * HALF, lat_cells), 0)
    lane = iota((2 * HALF, lat_cells), 1)
    high = jnp.where(row < HALF, 1 - odd, odd)
    cell = jnp.where(high == 1, lat_cells - 2, 0) + row % 2
    chosen = [
        (((row % HALF) // 2 == place) & (lane == cell)).astype(F32).astype(BF) for place in range(2)
    ]
    rows = HALF * channels
    for copy in copies:
        copy.wait()
    folded = [[], []]
    for part in range(parts):
        edges = sum(
            dot_lanes(chosen[place], raw_ref[place * parts + part].reshape(rows, lat_cells)) for place in range(2)
        )
        edges = dot_lanes(edges.astype(BF), perm_ref[...])
        for first in range(0, rows, lat_cells):
            for half in range(2):
                folded[half].append(edges[half * HALF : half * HALF + 4, first : first + lat_cells])
    core_ref[...] = jnp.concatenate(folded[0], 0).astype(BF)
    mid_ref[...] = jnp.concatenate(folded[1], 0).astype(BF)


def unfold(edges):
    wide = edges.astype(F32)
    lanes = jnp.concatenate([wide[first : first + 4] for first in range(0, wide.shape[0], 4)], 1)
    return jnp.concatenate([lanes, jnp.zeros((HALF - 4, lanes.shape[1]), F32)], 0)


def row_kernel(raw_ref, perm_ref, one_ref, two_ref, core_ref, xl_ref, cl_ref, first_ref, back_ref, passed_ref):
    passed_ref[...] = core_ref[...]
    rows = perm_ref.shape[0]
    parts = xl_ref.shape[0] // rows
    for place, target in enumerate((xl_ref, cl_ref)):
        for part in range(parts):
            block = raw_ref[place * parts + part].reshape(rows, target.shape[1])
            target[part * rows : (part + 1) * rows, :] = dot(perm_ref[...], block).astype(BF)
    write_band(one_ref, False, first_ref)
    write_band(two_ref, True, back_ref)


def write_band(kernel, transposed, target):
    channels = kernel.shape[2]
    lanes = WINDOW * channels
    tiled = (iota((channels, lanes), 1) % channels == iota((channels, lanes), 0)).astype(F32).astype(BF)
    block = iota((channels, lanes), 1) // channels
    for q in range(3):
        if transposed:
            bases = [dot_rows(kernel[2 - p, 2 - q], tiled) for p in range(3)]
        else:
            bases = [dot(kernel[p, q], tiled) for p in range(3)]
        for a in range(GROUP):
            band = jnp.zeros((channels, lanes), F32)
            for p in range(3):
                band = jnp.where(block == a + p, bases[p], band)
            target[q, a * channels : (a + 1) * channels, :] = band.astype(BF)


def lon_is_odd():
    return lax.axis_index("lon") % 2


def message_kernel(x_ref, cot_ref, core_in, mid_in, far_ref, near_ref, core_ref, mid_ref):
    rows, lat_cells = x_ref.shape
    two = (far_ref.shape[0] - HALF) // 2
    core, mid = unfold(core_in[...]), unfold(mid_in[...])
    core_ref[...] = core.astype(BF)
    mid_ref[...] = mid.astype(BF)
    odd = lon_is_odd()
    for target, high in ((far_ref, odd), (near_ref, 1 - odd)):
        part = pl.ds(pl.multiple_of(high * (rows - two), two), two)
        target[0:two, :] = x_ref[part, :]
        target[two : 2 * two, :] = cot_ref[part, :]
        halos = [
            jnp.where(high == 1, value[:, rows - two :], value[:, :two]).astype(BF) for value in (core, mid)
        ]
        target[2 * two :, : 2 * two] = jnp.concatenate(halos, 1)
        target[2 * two :, 2 * two :] = jnp.zeros((HALF, lat_cells - 2 * two), BF)


def halo_place(odd, place, lat_cells):
    row = iota((2 * HALF, lat_cells), 0)
    lane = iota((2 * HALF, lat_cells), 1)
    from_low = jnp.where(row < HALF, odd, 1 - odd) == 1
    wanted_row = 2 * place + jnp.where(from_low, 1, 0)
    wanted_lane = jnp.where(from_low, 0, lat_cells - 1)
    lat = lax.axis_index("lat")
    inside = jnp.where(row < HALF, 1, lat * (lax.axis_size("lat") - 1 - lat))
    return ((row % HALF == wanted_row) & (lane == wanted_lane) & (inside > 0)).astype(F32).astype(BF)


def write_shifted(values, edge_columns, target, rows):
    lat_cells = values.shape[1]
    lane = iota(values.shape, 1)
    columns = edge_columns.astype(BF)
    target[0, rows, :] = jnp.where(lane == 0, columns, pltpu.roll(values, 1, 1))
    target[1, rows, :] = values
    target[2, rows, :] = jnp.where(lane == lat_cells - 1, columns, pltpu.roll(values, lat_cells - 1, 1))


def activate(pre_act, back_grad):
    sigmoid_value = 0.5 * jnp.tanh(0.5 * pre_act) + 0.5
    activation = pre_act * sigmoid_value
    slope = sigmoid_value + activation * (1.0 - sigmoid_value)
    return activation, back_grad * slope


def conv_rows(weight_ref, shifted, rows, out_rows):
    count = rows.stop - rows.start
    return sum(dot(weight_ref[q, :out_rows, :count], shifted[q, rows, :]) for q in range(3))


def inner_kernel(x_ref, cot_ref, core_ref, mid_ref, first_ref, back_ref, pre_ref, grads_ref, xs, cs, total):
    lat_cells = x_ref.shape[1]
    channels = grads_ref.shape[2]
    odd = is_odd()
    halos = jnp.concatenate([core_ref[...], mid_ref[...]], 0)
    everything = slice(0, x_ref.shape[0])
    for place, (source, target) in enumerate(((x_ref, xs), (cot_ref, cs))):
        columns = dot_rows(halos, halo_place(odd, place, lat_cells))
        write_shifted(source[...], columns, target, everything)
    group_rows = GROUP * channels
    for k in range(pre_ref.shape[0] // group_rows):
        rows = slice(k * group_rows, k * group_rows + WINDOW * channels)
        pre_act = conv_rows(first_ref, xs, rows, group_rows)
        back_grad = conv_rows(back_ref, cs, rows, group_rows)
        activation, pre_grad = activate(pre_act, back_grad)
        activation = activation.astype(BF)
        pre_grad = pre_grad.astype(BF)
        pre_ref[k * group_rows : (k + 1) * group_rows, :] = pre_grad
        for q in range(3):
            for place, (own, raw) in enumerate(((pre_grad, xs), (activation, cs))):
                term = dot_lanes(own, raw[q, rows, :])
                if k == 0:
                    total[place, q] = term
                else:
                    total[place, q] += term
    for place in range(2):
        for q in range(3):
            summed = jnp.zeros((channels, WINDOW * channels), F32)
            for a in range(GROUP):
                band = total[place, q, a * channels : (a + 1) * channels, :]
                if a:
                    band = pltpu.roll(band, WINDOW * channels - a * channels, 1)
                summed = summed + band
            grads_ref[place, q] = summed[:, :128]


def edge_kernel(x_ref, cot_ref, core_ref, mid_ref, far_ref, near_ref, first_ref, back_ref, grads_ref,
                low_ref, high_ref, out_ref, left_ref, right_ref, xs_sides, cs_sides):
    lat_cells = x_ref.shape[1]
    channels = grads_ref.shape[2]
    odd = is_odd()
    two = 2 * channels
    own_rows = x_ref.shape[0]
    sums = [[grads_ref[place, q][:, : 3 * channels] for q in range(3)] for place in range(2)]
    far, near = far_ref[...].astype(F32), near_ref[...].astype(F32)
    left_ref[...] = jnp.where(lon_is_odd() == 1, near, far).astype(BF)
    right_ref[...] = jnp.where(lon_is_odd() == 1, far, near).astype(BF)
    sides = ((left_ref, low_ref), (right_ref, high_ref))
    for side, (message, _) in enumerate(sides):
        own = slice(0, two) if side == 0 else slice(own_rows - two, own_rows)
        sent = message[2 * two : 2 * two + HALF, :]
        sent_halos = jnp.concatenate([sent[:, :two], sent[:, two : 2 * two]], 0).astype(F32)
        own_halos = jnp.concatenate([core_ref[:, own], mid_ref[:, own]], 0).astype(F32)
        order = (sent_halos, own_halos) if side == 0 else (own_halos, sent_halos)
        halos = jnp.concatenate(order, 1).astype(BF)
        for place, (source, shifted) in enumerate(((x_ref, xs_sides), (cot_ref, cs_sides))):
            sent_rows = message[place * two : (place + 1) * two, :]
            order = (sent_rows, source[own, :]) if side == 0 else (source[own, :], sent_rows)
            columns = dot_rows(halos, halo_place(odd, place, lat_cells))
            write_shifted(jnp.concatenate(order, 0), columns, shifted.at[side], slice(0, 2 * two))
    rows = slice(0, 2 * two)
    pre_acts = [conv_rows(first_ref, xs_sides.at[side], rows, two) for side in range(2)]
    back_grads = [conv_rows(back_ref, cs_sides.at[side], rows, two) for side in range(2)]
    for side, (_, target) in enumerate(sides):
        activation, pre_grad = activate(pre_acts[side], back_grads[side])
        pre_grad = pre_grad.astype(BF)
        target[...] = pre_grad
        mine = slice(channels, two) if side == 0 else slice(0, channels)
        near = slice(channels, 2 * two) if side == 0 else slice(0, 3 * channels)
        activation = activation[mine].astype(BF)
        pre_grad = pre_grad[mine]
        for q in range(3):
            sums[0][q] = sums[0][q] + dot_lanes(pre_grad, xs_sides[side, q, near, :])
            sums[1][q] = sums[1][q] + dot_lanes(activation, cs_sides[side, q, near, :])
    out_ref[...] = jnp.concatenate([pack_taps(taps) for taps in sums], 0)


def pack_taps(taps):
    channels = taps[0].shape[0]
    main = [
        jnp.concatenate([taps[q], taps[2][:, q * channels : (q + 1) * channels]], 1) for q in range(2)
    ]
    rest = taps[2][:, 2 * channels :]
    count = 128 // channels
    rows = channels // count
    last = jnp.concatenate([rest[i * rows : (i + 1) * rows] for i in range(count)], 1)
    return jnp.concatenate([*main, last], 0)


def unpack_taps(packed, channels):
    used = 3 * channels
    count = 128 // channels
    main = [packed[q * channels : (q + 1) * channels] for q in range(2)]
    rest = packed[2 * channels :]
    last = jnp.concatenate([rest[:, i * channels : (i + 1) * channels] for i in range(count)], 0)
    third = jnp.concatenate([main[0][:, used:], main[1][:, used:], last], 1)
    return [main[0], main[1], third]


def outer_kernel(x_ref, cot_ref, core_ref, mid_ref, left_ref, right_ref, first_ref, back_ref, low_ref, pre_ref,
                 high_ref, one_ref, partial_ref, ps, last_ref, passed_ref, rows_buffer, strips):
    passed_ref[...] = partial_ref[...]
    write_band(one_ref, True, last_ref)
    lat_cells = x_ref.shape[1]
    channels = low_ref.shape[0] // 2
    two = 2 * channels
    own_rows = x_ref.shape[0]
    wide_rows = own_rows + 2 * two
    odd = is_odd()
    core, mid = core_ref[...].astype(F32), mid_ref[...].astype(F32)
    lat = lax.axis_index("lat")
    lat_count = lax.axis_size("lat")

    def halo_lanes(value, first):
        parts = [left_ref[2 * two : 2 * two + HALF, first : first + two].astype(F32), value,
                 right_ref[2 * two : 2 * two + HALF, first : first + two].astype(F32)]
        return parts

    def put(target, parts):
        target[:, 0:two] = parts[0]
        target[:, two : two + own_rows] = parts[1]
        target[:, two + own_rows : wide_rows] = parts[2]

    put(strips.at[0], halo_lanes(core, 0))
    put(strips.at[1], halo_lanes(mid, two))
    core_wide, mid_wide = strips[0], strips[1]
    low = jnp.where(odd == 1, core_wide, mid_wide)
    high = jnp.where(odd == 1, mid_wide, core_wide)
    row = iota((HALF, lat_cells), 0)
    lane = iota((HALF, lat_cells), 1)
    ends = ((row < 2) & (lane == row * (lat_cells - 1))).astype(F32).astype(BF)
    values = []
    span = 4 * channels
    window = 6 * channels
    for place, (source, weight_ref) in enumerate(((x_ref, first_ref), (cot_ref, back_ref))):
        rows_buffer[0:two, :] = left_ref[place * two : (place + 1) * two, :]
        rows_buffer[two : two + own_rows, :] = source[...]
        rows_buffer[two + own_rows : wide_rows, :] = right_ref[place * two : (place + 1) * two, :]
        own = dot_lanes(ends, rows_buffer[...])
        low_rows = [low[2 * place : 2 * place + 1], low[2 * place + 1 : 2 * place + 2], own[0:1]]
        high_rows = [own[1:2], high[2 * place : 2 * place + 1], high[2 * place + 1 : 2 * place + 2]]
        total = None
        for q in range(3):
            which = iota((HALF, wide_rows), 0)
            strip = jnp.where(which == 0, low_rows[q], jnp.where(which == 1, high_rows[q], 0.0))
            strip = jnp.concatenate([strip, jnp.zeros((HALF, 128), F32)], 1)
            stacked = jnp.concatenate(
                [strip[:, k : k + window] for k in range(0, wide_rows, span)], 0
            ).astype(BF)
            term = dot_lanes(stacked, weight_ref[q, :span, :window])
            total = term if total is None else total + term
        values.append(total)
    _, pre_grad = activate(*values)
    beyond = jnp.where(iota(pre_grad.shape, 0) % HALF == 0, lat, lat_count - 1 - lat)
    pre_grad = jnp.where(beyond > 0, pre_grad, 0.0)
    pre_strip = jnp.concatenate(
        [pre_grad[k : k + HALF] for k in range(0, pre_grad.shape[0], HALF)], 1
    ).astype(BF)
    wide = pre_ref.shape[0] + 2 * two
    columns = dot_rows(pre_strip, ends)[:wide]
    rows_buffer[0:two, :] = low_ref[...]
    rows_buffer[two : wide - two, :] = pre_ref[...]
    rows_buffer[wide - two : wide, :] = high_ref[...]
    write_shifted(rows_buffer[0:wide, :], columns, ps, slice(0, wide))


def last_kernel(ps, last_ref, raw_ref, partial_ref, out_ref, passed_ref, placed, result, sems):
    passed_ref[...] = partial_ref[...]
    channels, lon_cells, lat_cells = out_ref.shape
    parts = lon_cells // HALF
    copies = []
    done = 0
    for first in range(0, lon_cells, GROUP):
        lons = min(GROUP, lon_cells - first)
        rows = slice(first * channels, (first + lons + 2) * channels)
        total = conv_rows(last_ref, ps, rows, lons * channels)
        for a in range(lons):
            lon_rows = total[a * channels : (a + 1) * channels]
            for tile in range(lat_cells // 128):
                lanes = slice(tile * 128, (tile + 1) * 128)
                placed[tile, pl.ds(first + a, channels, stride=lon_cells), :] = lon_rows[:, lanes]
        if first + lons >= done + HALF:
            part = slice(done, done + HALF)
            for tile in range(lat_cells // 128):
                lanes = slice(tile * 128, (tile + 1) * 128)
                block = placed[tile].reshape(channels, lon_cells, 128)[:, part, :]
                block = block + raw_ref[parts + done // HALF, :, :, lanes].astype(F32)
                result[:, part, lanes] = block.astype(BF)
            copy = pltpu.make_async_copy(
                result.at[:, pl.ds(done, HALF), :], out_ref.at[:, pl.ds(done, HALF), :], sems.at[done // HALF]
            )
            copy.start()
            copies.append(copy)
            done += HALF
    for copy in copies:
        copy.wait()


def result_kernel(scale, total_ref, given_ref, one_ref, two_ref):
    channels = one_ref.shape[2]
    rows = total_ref.shape[0] // 2
    sums = jnp.where(is_odd() == 1, total_ref[...], given_ref[...]) * scale
    first, second = sums[:rows], sums[rows:]
    first = unpack_taps(first, channels)
    second = unpack_taps(second, channels)
    for q in range(3):
        for p in range(3):
            lanes = slice(p * channels, (p + 1) * channels)
            one_ref[p, q] = first[q][:, lanes]
            two_ref[2 - p, 2 - q] = second[q][:, lanes].T


ALONG_X, ALONG_Y = 32, 1


def pairs(counts, partner, idle):
    lat_count, lon_count = counts
    listed = []
    for lat in range(lat_count):
        for lon in range(lon_count):
            to_lat, to_lon = partner(lat, lon) if lat % 2 else (lat, lon ^ idle)
            listed.append((lat * lon_count + lon, to_lat * lon_count + to_lon))
    return listed


def x_partner(mask):
    def partner(lat, lon):
        place = ((lat >> 1) * 2 + (lon >> 5)) ^ mask
        return (place >> 1) * 2 + (lat & 1), (place & 1) * 32 + (lon & 31)

    return partner


def y_partner(mask):
    return lambda lat, lon: (lat, lon ^ mask)


def z_partner(mask):
    return lambda lat, lon: (lat, lon ^ (mask << 2))


def exchange(value, partner, idle):
    counts = (lax.axis_size("lat"), lax.axis_size("lon"))
    return lax.ppermute(value, ("lat", "lon"), pairs(counts, partner, idle))


def sum_of_four(value, partner, masks, idle, beside=None):
    first, second, third = [exchange(value, partner(mask), idle) for mask in masks]
    result = None
    if beside is not None:
        *result, value = beside(value)
    return (value + first) + (second + third), result


def sum_everywhere(mine, widen, finish):
    total = mine + core_exchange(mine)
    total, _ = sum_of_four(total, x_partner, (1, 3, 2), ALONG_Y)
    total, shifted = sum_of_four(total, y_partner, (1, 3, 2), ALONG_X, widen)
    total, (input_grad,) = sum_of_four(
        total, z_partner, (1, 2, 3), ALONG_X, lambda value: finish(*shifted, value)
    )
    total = total + exchange(total, z_partner(6), ALONG_X)
    given = core_exchange(total)
    return total, given, input_grad


def mid_exchange(edges):
    count = lax.axis_size("lat")
    return lax.ppermute(edges, "lat", [(i, (i - 1 if i % 2 == 0 else i + 1) % count) for i in range(count)])


def core_exchange(value):
    return lax.ppermute(value, "lat", [(i, i ^ 1) for i in range(lax.axis_size("lat"))])


def on_device(inputs, kernel_one, kernel_two, cotangent):
    channels, lon_cells, lat_cells = inputs.shape
    cells = lon_cells * lat_cells * lax.axis_size("lat") * lax.axis_size("lon")
    rows = channels * lon_cells
    two = 2 * channels
    parts = lon_cells // HALF
    weights = shape(3, GROUP * channels, WINDOW * channels)
    folded = shape(4 * rows // lat_cells, lat_cells)
    raw, one, two_kernel, perm, core_out, mid_out = call(
        border_kernel,
        [
            shape(2 * parts, channels, HALF, lat_cells),
            shape(*kernel_one.shape),
            shape(*kernel_two.shape),
            shape(HALF * channels, HALF * channels),
            folded,
            folded,
        ],
        [pltpu.SemaphoreType.DMA((2 + 2 * parts,))],
        10**8,
        inputs,
        cotangent,
        kernel_one,
        kernel_two,
        hbm_in=(0, 1, 2, 3),
    )
    mid_in = mid_exchange(mid_out)
    x_rows, cot_rows, first, back, core_out = call(
        row_kernel,
        [shape(rows, lat_cells), shape(rows, lat_cells), weights, weights, folded],
        [],
        10**9,
        raw,
        perm,
        one,
        two_kernel,
        core_out,
    )
    core_in = core_exchange(core_out)

    message = shape(2 * two + HALF, lat_cells)
    edges = shape(HALF, rows)
    far_out, near_out, core_in, mid_in = call(
        message_kernel, [message, message, edges, edges], [], 10**6, x_rows, cot_rows, core_in, mid_in
    )
    count = lax.axis_size("lon")
    far_in = lax.ppermute(far_out, "lon", [(i, (i + 1 if i % 2 else i - 1) % count) for i in range(count)])
    near_in = lax.ppermute(near_out, "lon", [(i, i ^ 1) for i in range(count)])

    inner_rows = rows - two
    shifted = pltpu.VMEM((3, rows, lat_cells), BF)
    pre_inner, inner_grads = call(
        inner_kernel,
        [shape(inner_rows, lat_cells), shape(2, 3, channels, 128, dtype=F32)],
        [shifted, shifted, pltpu.VMEM((2, 3, GROUP * channels, WINDOW * channels), F32)],
        4 * 10**9,
        x_rows, cot_rows, core_in, mid_in, first, back,
    )
    edge_shifted = pltpu.VMEM((2, 3, 2 * two, lat_cells), BF)
    partial = shape(2 * 9 * channels * channels // 128, 128, dtype=F32)
    pre_low, pre_high, grads, from_left, from_right = call(
        edge_kernel,
        [shape(two, lat_cells), shape(two, lat_cells), partial, message, message],
        [edge_shifted, edge_shifted],
        10**9,
        x_rows, cot_rows, core_in, mid_in, far_in, near_in, first, back, inner_grads,
    )
    def widen(partial):
        return call(
            outer_kernel,
            [shape(3, rows + two, lat_cells), weights, shape(*partial.shape, dtype=F32)],
            [
                pltpu.VMEM((rows + 2 * two, lat_cells), BF),
                pltpu.VMEM((2, HALF, rows + 2 * two), F32),
            ],
            10**9,
            x_rows, cot_rows, core_in, mid_in, from_left, from_right, first, back,
            pre_low, pre_inner, pre_high, one, partial,
        )

    def finish(shifted, last, partial):
        return call(
            last_kernel,
            [shape(channels, lon_cells, lat_cells), shape(*partial.shape, dtype=F32)],
            [
                pltpu.VMEM((lat_cells // 128, rows, 128), F32),
                pltpu.VMEM((channels, lon_cells, lat_cells), BF),
                pltpu.SemaphoreType.DMA((lon_cells // HALF,)),
            ],
            2 * 10**9,
            shifted, last, raw, partial,
            hbm_out=(0,),
        )

    total, given, input_grad = sum_everywhere(grads, widen, finish)
    grad_one, grad_two = call(
        functools.partial(result_kernel, 1.0 / math.sqrt(cells)),
        [shape(3, 3, channels, channels, dtype=F32)] * 2,
        [],
        10**6,
        total,
        given,
    )
    return (input_grad, grad_one, grad_two)


def solution(mesh):
    placed = (P(None, "lon", "lat"), P(), P(), P(None, "lon", "lat"))
    return jax.shard_map(
        on_device,
        mesh=mesh,
        in_specs=placed,
        out_specs=(P(None, "lon", "lat"), P(), P()),
        check_vma=False,
    )
```

```python
import functools
import math

import jax
import jax.numpy as jnp
from jax import lax
from jax.experimental import pallas as pl
from jax.experimental.pallas import tpu as pltpu
from jax.sharding import PartitionSpec as P

BF = jnp.bfloat16
F32 = jnp.float32
GROUP = 6
WINDOW = GROUP + 2
HALF = 16
PARAMS = pltpu.CompilerParams(vmem_limit_bytes=16 * 2**20)


def dot(left, right):
    return lax.dot_general(left, right, (((1,), (0,)), ((), ())), preferred_element_type=F32)


def dot_lanes(left, right):
    return lax.dot_general(left, right, (((1,), (1,)), ((), ())), preferred_element_type=F32)


def dot_rows(left, right):
    return lax.dot_general(left, right, (((0,), (0,)), ((), ())), preferred_element_type=F32)


def iota(shape, dim):
    return lax.broadcasted_iota(jnp.int32, shape, dim)


def call(kernel, outs, scratch, flops, *operands, hbm_in=(), hbm_out=()):
    spaces = [pltpu.HBM if i in hbm_in else pltpu.VMEM for i in range(len(operands))]
    out_spaces = [pltpu.HBM if i in hbm_out else pltpu.VMEM for i in range(len(outs))]
    bytes_moved = sum(o.size * o.dtype.itemsize for o in (*operands, *outs))
    operands = [pltpu.with_memory_space_constraint(o, pltpu.HBM) if i in hbm_in else o for i, o in enumerate(operands)]
    return pl.pallas_call(
        kernel,
        out_shape=outs,
        in_specs=[pl.BlockSpec(memory_space=space) for space in spaces],
        out_specs=[pl.BlockSpec(memory_space=space) for space in out_spaces],
        scratch_shapes=scratch,
        compiler_params=PARAMS,
        cost_estimate=pl.CostEstimate(flops=flops, bytes_accessed=bytes_moved, transcendentals=0),
    )(*operands)


def shape(*dims, dtype=BF):
    return jax.ShapeDtypeStruct(dims, dtype)


def is_odd():
    return lax.axis_index("lat") % 2


def border_kernel(x_hbm, cot_hbm, one_hbm, two_hbm, raw_ref, one_ref, two_ref, perm_ref, core_ref, mid_ref, sems):
    channels, lon_cells, lat_cells = x_hbm.shape
    parts = lon_cells // HALF
    pieces = [(one_hbm, one_ref), (two_hbm, two_ref)]
    for place, source in enumerate((x_hbm, cot_hbm)):
        for part in range(parts):
            pieces.append((source.at[:, pl.ds(part * HALF, HALF), :], raw_ref.at[place * parts + part]))
    copies = [pltpu.make_async_copy(*piece, sems.at[number]) for number, piece in enumerate(pieces)]
    for copy in copies:
        copy.start()
    to_row = iota(perm_ref.shape, 0)
    from_row = iota(perm_ref.shape, 1)
    moved = (to_row % channels) * HALF + to_row // channels
    perm_ref[...] = jnp.where(from_row == moved, 1.0, 0.0).astype(BF)
    odd = is_odd()
    row = iota((2 * HALF, lat_cells), 0)
    lane = iota((2 * HALF, lat_cells), 1)
    high = jnp.where(row < HALF, 1 - odd, odd)
    cell = jnp.where(high == 1, lat_cells - 2, 0) + row % 2
    chosen = [
        (((row % HALF) // 2 == place) & (lane == cell)).astype(F32).astype(BF) for place in range(2)
    ]
    rows = HALF * channels
    for copy in copies:
        copy.wait()
    folded = [[], []]
    for part in range(parts):
        edges = sum(
            dot_lanes(chosen[place], raw_ref[place * parts + part].reshape(rows, lat_cells)) for place in range(2)
        )
        edges = dot_lanes(edges.astype(BF), perm_ref[...])
        for first in range(0, rows, lat_cells):
            for half in range(2):
                folded[half].append(edges[half * HALF : half * HALF + 4, first : first + lat_cells])
    core_ref[...] = jnp.concatenate(folded[0], 0).astype(BF)
    mid_ref[...] = jnp.concatenate(folded[1], 0).astype(BF)


def unfold(edges):
    wide = edges.astype(F32)
    lanes = jnp.concatenate([wide[first : first + 4] for first in range(0, wide.shape[0], 4)], 1)
    return jnp.concatenate([lanes, jnp.zeros((HALF - 4, lanes.shape[1]), F32)], 0)


def row_kernel(raw_ref, perm_ref, one_ref, two_ref, core_ref, xl_ref, cl_ref, first_ref, back_ref, passed_ref):
    passed_ref[...] = core_ref[...]
    rows = perm_ref.shape[0]
    parts = xl_ref.shape[0] // rows
    for place, target in enumerate((xl_ref, cl_ref)):
        for part in range(parts):
            block = raw_ref[place * parts + part].reshape(rows, target.shape[1])
            target[part * rows : (part + 1) * rows, :] = dot(perm_ref[...], block).astype(BF)
    write_band(one_ref, False, first_ref)
    write_band(two_ref, True, back_ref)


def write_band(kernel, transposed, target):
    channels = kernel.shape[2]
    lanes = WINDOW * channels
    tiled = (iota((channels, lanes), 1) % channels == iota((channels, lanes), 0)).astype(F32).astype(BF)
    block = iota((channels, lanes), 1) // channels
    for q in range(3):
        if transposed:
            bases = [dot_rows(kernel[2 - p, 2 - q], tiled) for p in range(3)]
        else:
            bases = [dot(kernel[p, q], tiled) for p in range(3)]
        for a in range(GROUP):
            band = jnp.zeros((channels, lanes), F32)
            for p in range(3):
                band = jnp.where(block == a + p, bases[p], band)
            target[q, a * channels : (a + 1) * channels, :] = band.astype(BF)


def lon_is_odd():
    return lax.axis_index("lon") % 2


def message_kernel(x_ref, cot_ref, core_in, mid_in, far_ref, near_ref, core_ref, mid_ref):
    rows, lat_cells = x_ref.shape
    two = (far_ref.shape[0] - HALF) // 2
    core, mid = unfold(core_in[...]), unfold(mid_in[...])
    core_ref[...] = core.astype(BF)
    mid_ref[...] = mid.astype(BF)
    odd = lon_is_odd()
    for target, high in ((far_ref, odd), (near_ref, 1 - odd)):
        part = pl.ds(pl.multiple_of(high * (rows - two), two), two)
        target[0:two, :] = x_ref[part, :]
        target[two : 2 * two, :] = cot_ref[part, :]
        halos = [
            jnp.where(high == 1, value[:, rows - two :], value[:, :two]).astype(BF) for value in (core, mid)
        ]
        target[2 * two :, : 2 * two] = jnp.concatenate(halos, 1)
        target[2 * two :, 2 * two :] = jnp.zeros((HALF, lat_cells - 2 * two), BF)


def halo_place(odd, place, lat_cells):
    row = iota((2 * HALF, lat_cells), 0)
    lane = iota((2 * HALF, lat_cells), 1)
    from_low = jnp.where(row < HALF, odd, 1 - odd) == 1
    wanted_row = 2 * place + jnp.where(from_low, 1, 0)
    wanted_lane = jnp.where(from_low, 0, lat_cells - 1)
    lat = lax.axis_index("lat")
    inside = jnp.where(row < HALF, 1, lat * (lax.axis_size("lat") - 1 - lat))
    return ((row % HALF == wanted_row) & (lane == wanted_lane) & (inside > 0)).astype(F32).astype(BF)


def write_shifted(values, edge_columns, target, rows):
    lat_cells = values.shape[1]
    lane = iota(values.shape, 1)
    columns = edge_columns.astype(BF)
    target[0, rows, :] = jnp.where(lane == 0, columns, pltpu.roll(values, 1, 1))
    target[1, rows, :] = values
    target[2, rows, :] = jnp.where(lane == lat_cells - 1, columns, pltpu.roll(values, lat_cells - 1, 1))


def activate(pre_act, back_grad):
    sigmoid_value = 1.0 / (1.0 + jnp.exp(-pre_act))
    activation = pre_act * sigmoid_value
    slope = sigmoid_value + activation * (1.0 - sigmoid_value)
    return activation, back_grad * slope


def conv_rows(weight_ref, shifted, rows, out_rows):
    count = rows.stop - rows.start
    return sum(dot(weight_ref[q, :out_rows, :count], shifted[q, rows, :]) for q in range(3))


def inner_kernel(x_ref, cot_ref, core_ref, mid_ref, first_ref, back_ref, pre_ref, grads_ref, xs, cs, total):
    lat_cells = x_ref.shape[1]
    channels = grads_ref.shape[2]
    odd = is_odd()
    halos = jnp.concatenate([core_ref[...], mid_ref[...]], 0)
    everything = slice(0, x_ref.shape[0])
    for place, (source, target) in enumerate(((x_ref, xs), (cot_ref, cs))):
        columns = dot_rows(halos, halo_place(odd, place, lat_cells))
        write_shifted(source[...], columns, target, everything)
    group_rows = GROUP * channels
    for k in range(pre_ref.shape[0] // group_rows):
        rows = slice(k * group_rows, k * group_rows + WINDOW * channels)
        pre_act = conv_rows(first_ref, xs, rows, group_rows)
        back_grad = conv_rows(back_ref, cs, rows, group_rows)
        activation, pre_grad = activate(pre_act, back_grad)
        activation = activation.astype(BF)
        pre_grad = pre_grad.astype(BF)
        pre_ref[k * group_rows : (k + 1) * group_rows, :] = pre_grad
        for q in range(3):
            for place, (own, raw) in enumerate(((pre_grad, xs), (activation, cs))):
                term = dot_lanes(own, raw[q, rows, :])
                if k == 0:
                    total[place, q] = term
                else:
                    total[place, q] += term
    for place in range(2):
        for q in range(3):
            summed = jnp.zeros((channels, WINDOW * channels), F32)
            for a in range(GROUP):
                band = total[place, q, a * channels : (a + 1) * channels, :]
                if a:
                    band = pltpu.roll(band, WINDOW * channels - a * channels, 1)
                summed = summed + band
            grads_ref[place, q] = summed[:, :128]


def edge_kernel(x_ref, cot_ref, core_ref, mid_ref, far_ref, near_ref, first_ref, back_ref, grads_ref,
                low_ref, high_ref, out_ref, left_ref, right_ref, xs_sides, cs_sides):
    lat_cells = x_ref.shape[1]
    channels = grads_ref.shape[2]
    odd = is_odd()
    two = 2 * channels
    own_rows = x_ref.shape[0]
    sums = [[grads_ref[place, q][:, : 3 * channels] for q in range(3)] for place in range(2)]
    far, near = far_ref[...].astype(F32), near_ref[...].astype(F32)
    left_ref[...] = jnp.where(lon_is_odd() == 1, near, far).astype(BF)
    right_ref[...] = jnp.where(lon_is_odd() == 1, far, near).astype(BF)
    sides = ((left_ref, low_ref), (right_ref, high_ref))
    for side, (message, _) in enumerate(sides):
        own = slice(0, two) if side == 0 else slice(own_rows - two, own_rows)
        sent = message[2 * two : 2 * two + HALF, :]
        sent_halos = jnp.concatenate([sent[:, :two], sent[:, two : 2 * two]], 0).astype(F32)
        own_halos = jnp.concatenate([core_ref[:, own], mid_ref[:, own]], 0).astype(F32)
        order = (sent_halos, own_halos) if side == 0 else (own_halos, sent_halos)
        halos = jnp.concatenate(order, 1).astype(BF)
        for place, (source, shifted) in enumerate(((x_ref, xs_sides), (cot_ref, cs_sides))):
            sent_rows = message[place * two : (place + 1) * two, :]
            order = (sent_rows, source[own, :]) if side == 0 else (source[own, :], sent_rows)
            columns = dot_rows(halos, halo_place(odd, place, lat_cells))
            write_shifted(jnp.concatenate(order, 0), columns, shifted.at[side], slice(0, 2 * two))
    rows = slice(0, 2 * two)
    pre_acts = [conv_rows(first_ref, xs_sides.at[side], rows, two) for side in range(2)]
    back_grads = [conv_rows(back_ref, cs_sides.at[side], rows, two) for side in range(2)]
    for side, (_, target) in enumerate(sides):
        activation, pre_grad = activate(pre_acts[side], back_grads[side])
        pre_grad = pre_grad.astype(BF)
        target[...] = pre_grad
        mine = slice(channels, two) if side == 0 else slice(0, channels)
        near = slice(channels, 2 * two) if side == 0 else slice(0, 3 * channels)
        activation = activation[mine].astype(BF)
        pre_grad = pre_grad[mine]
        for q in range(3):
            sums[0][q] = sums[0][q] + dot_lanes(pre_grad, xs_sides[side, q, near, :])
            sums[1][q] = sums[1][q] + dot_lanes(activation, cs_sides[side, q, near, :])
    out_ref[...] = jnp.concatenate([pack_taps(taps) for taps in sums], 0)


def pack_taps(taps):
    channels = taps[0].shape[0]
    main = [
        jnp.concatenate([taps[q], taps[2][:, q * channels : (q + 1) * channels]], 1) for q in range(2)
    ]
    rest = taps[2][:, 2 * channels :]
    count = 128 // channels
    rows = channels // count
    last = jnp.concatenate([rest[i * rows : (i + 1) * rows] for i in range(count)], 1)
    return jnp.concatenate([*main, last], 0)


def unpack_taps(packed, channels):
    used = 3 * channels
    count = 128 // channels
    main = [packed[q * channels : (q + 1) * channels] for q in range(2)]
    rest = packed[2 * channels :]
    last = jnp.concatenate([rest[:, i * channels : (i + 1) * channels] for i in range(count)], 0)
    third = jnp.concatenate([main[0][:, used:], main[1][:, used:], last], 1)
    return [main[0], main[1], third]


def outer_kernel(x_ref, cot_ref, core_ref, mid_ref, left_ref, right_ref, first_ref, back_ref, low_ref, pre_ref,
                 high_ref, one_ref, partial_ref, ps, last_ref, passed_ref, rows_buffer, strips):
    passed_ref[...] = partial_ref[...]
    write_band(one_ref, True, last_ref)
    lat_cells = x_ref.shape[1]
    channels = low_ref.shape[0] // 2
    two = 2 * channels
    own_rows = x_ref.shape[0]
    wide_rows = own_rows + 2 * two
    odd = is_odd()
    core, mid = core_ref[...].astype(F32), mid_ref[...].astype(F32)
    lat = lax.axis_index("lat")
    lat_count = lax.axis_size("lat")

    def halo_lanes(value, first):
        parts = [left_ref[2 * two : 2 * two + HALF, first : first + two].astype(F32), value,
                 right_ref[2 * two : 2 * two + HALF, first : first + two].astype(F32)]
        return parts

    def put(target, parts):
        target[:, 0:two] = parts[0]
        target[:, two : two + own_rows] = parts[1]
        target[:, two + own_rows : wide_rows] = parts[2]

    put(strips.at[0], halo_lanes(core, 0))
    put(strips.at[1], halo_lanes(mid, two))
    core_wide, mid_wide = strips[0], strips[1]
    low = jnp.where(odd == 1, core_wide, mid_wide)
    high = jnp.where(odd == 1, mid_wide, core_wide)
    row = iota((HALF, lat_cells), 0)
    lane = iota((HALF, lat_cells), 1)
    ends = ((row < 2) & (lane == row * (lat_cells - 1))).astype(F32).astype(BF)
    values = []
    span = 4 * channels
    window = 6 * channels
    for place, (source, weight_ref) in enumerate(((x_ref, first_ref), (cot_ref, back_ref))):
        rows_buffer[0:two, :] = left_ref[place * two : (place + 1) * two, :]
        rows_buffer[two : two + own_rows, :] = source[...]
        rows_buffer[two + own_rows : wide_rows, :] = right_ref[place * two : (place + 1) * two, :]
        own = dot_lanes(ends, rows_buffer[...])
        low_rows = [low[2 * place : 2 * place + 1], low[2 * place + 1 : 2 * place + 2], own[0:1]]
        high_rows = [own[1:2], high[2 * place : 2 * place + 1], high[2 * place + 1 : 2 * place + 2]]
        total = None
        for q in range(3):
            which = iota((HALF, wide_rows), 0)
            strip = jnp.where(which == 0, low_rows[q], jnp.where(which == 1, high_rows[q], 0.0))
            strip = jnp.concatenate([strip, jnp.zeros((HALF, 128), F32)], 1)
            stacked = jnp.concatenate(
                [strip[:, k : k + window] for k in range(0, wide_rows, span)], 0
            ).astype(BF)
            term = dot_lanes(stacked, weight_ref[q, :span, :window])
            total = term if total is None else total + term
        values.append(total)
    _, pre_grad = activate(*values)
    beyond = jnp.where(iota(pre_grad.shape, 0) % HALF == 0, lat, lat_count - 1 - lat)
    pre_grad = jnp.where(beyond > 0, pre_grad, 0.0)
    pre_strip = jnp.concatenate(
        [pre_grad[k : k + HALF] for k in range(0, pre_grad.shape[0], HALF)], 1
    ).astype(BF)
    wide = pre_ref.shape[0] + 2 * two
    columns = dot_rows(pre_strip, ends)[:wide]
    rows_buffer[0:two, :] = low_ref[...]
    rows_buffer[two : wide - two, :] = pre_ref[...]
    rows_buffer[wide - two : wide, :] = high_ref[...]
    write_shifted(rows_buffer[0:wide, :], columns, ps, slice(0, wide))


def last_kernel(ps, last_ref, raw_ref, partial_ref, out_ref, passed_ref, placed, result, sems):
    passed_ref[...] = partial_ref[...]
    channels, lon_cells, lat_cells = out_ref.shape
    parts = lon_cells // HALF
    copies = []
    done = 0
    for first in range(0, lon_cells, GROUP):
        lons = min(GROUP, lon_cells - first)
        rows = slice(first * channels, (first + lons + 2) * channels)
        total = conv_rows(last_ref, ps, rows, lons * channels)
        for a in range(lons):
            lon_rows = total[a * channels : (a + 1) * channels]
            for tile in range(lat_cells // 128):
                lanes = slice(tile * 128, (tile + 1) * 128)
                placed[tile, pl.ds(first + a, channels, stride=lon_cells), :] = lon_rows[:, lanes]
        if first + lons >= done + HALF:
            part = slice(done, done + HALF)
            for tile in range(lat_cells // 128):
                lanes = slice(tile * 128, (tile + 1) * 128)
                block = placed[tile].reshape(channels, lon_cells, 128)[:, part, :]
                block = block + raw_ref[parts + done // HALF, :, :, lanes].astype(F32)
                result[:, part, lanes] = block.astype(BF)
            copy = pltpu.make_async_copy(
                result.at[:, pl.ds(done, HALF), :], out_ref.at[:, pl.ds(done, HALF), :], sems.at[done // HALF]
            )
            copy.start()
            copies.append(copy)
            done += HALF
    for copy in copies:
        copy.wait()


def result_kernel(scale, total_ref, given_ref, one_ref, two_ref):
    channels = one_ref.shape[2]
    rows = total_ref.shape[0] // 2
    sums = jnp.where(is_odd() == 1, total_ref[...], given_ref[...]) * scale
    first, second = sums[:rows], sums[rows:]
    first = unpack_taps(first, channels)
    second = unpack_taps(second, channels)
    for q in range(3):
        for p in range(3):
            lanes = slice(p * channels, (p + 1) * channels)
            one_ref[p, q] = first[q][:, lanes]
            two_ref[2 - p, 2 - q] = second[q][:, lanes].T


ALONG_X, ALONG_Y = 32, 1


def pairs(counts, partner, idle):
    lat_count, lon_count = counts
    listed = []
    for lat in range(lat_count):
        for lon in range(lon_count):
            to_lat, to_lon = partner(lat, lon) if lat % 2 else (lat, lon ^ idle)
            listed.append((lat * lon_count + lon, to_lat * lon_count + to_lon))
    return listed


def x_partner(mask):
    def partner(lat, lon):
        place = ((lat >> 1) * 2 + (lon >> 5)) ^ mask
        return (place >> 1) * 2 + (lat & 1), (place & 1) * 32 + (lon & 31)

    return partner


def y_partner(mask):
    return lambda lat, lon: (lat, lon ^ mask)


def z_partner(mask):
    return lambda lat, lon: (lat, lon ^ (mask << 2))


def exchange(value, partner, idle):
    counts = (lax.axis_size("lat"), lax.axis_size("lon"))
    return lax.ppermute(value, ("lat", "lon"), pairs(counts, partner, idle))


def sum_of_four(value, partner, masks, idle, beside=None):
    first, second, third = [exchange(value, partner(mask), idle) for mask in masks]
    result = None
    if beside is not None:
        *result, value = beside(value)
    return (value + first) + (second + third), result


def sum_everywhere(mine, widen, finish):
    total = mine + core_exchange(mine)
    total, _ = sum_of_four(total, x_partner, (1, 3, 2), ALONG_Y)
    total, shifted = sum_of_four(total, y_partner, (1, 3, 2), ALONG_X, widen)
    total, (input_grad,) = sum_of_four(
        total, z_partner, (1, 2, 3), ALONG_X, lambda value: finish(*shifted, value)
    )
    total = total + exchange(total, z_partner(6), ALONG_X)
    given = core_exchange(total)
    return total, given, input_grad


def mid_exchange(edges):
    count = lax.axis_size("lat")
    return lax.ppermute(edges, "lat", [(i, (i - 1 if i % 2 == 0 else i + 1) % count) for i in range(count)])


def core_exchange(value):
    return lax.ppermute(value, "lat", [(i, i ^ 1) for i in range(lax.axis_size("lat"))])


def on_device(inputs, kernel_one, kernel_two, cotangent):
    channels, lon_cells, lat_cells = inputs.shape
    cells = lon_cells * lat_cells * lax.axis_size("lat") * lax.axis_size("lon")
    rows = channels * lon_cells
    two = 2 * channels
    parts = lon_cells // HALF
    weights = shape(3, GROUP * channels, WINDOW * channels)
    folded = shape(4 * rows // lat_cells, lat_cells)
    raw, one, two_kernel, perm, core_out, mid_out = call(
        border_kernel,
        [
            shape(2 * parts, channels, HALF, lat_cells),
            shape(*kernel_one.shape),
            shape(*kernel_two.shape),
            shape(HALF * channels, HALF * channels),
            folded,
            folded,
        ],
        [pltpu.SemaphoreType.DMA((2 + 2 * parts,))],
        10**8,
        inputs,
        cotangent,
        kernel_one,
        kernel_two,
        hbm_in=(0, 1, 2, 3),
    )
    mid_in = mid_exchange(mid_out)
    x_rows, cot_rows, first, back, core_out = call(
        row_kernel,
        [shape(rows, lat_cells), shape(rows, lat_cells), weights, weights, folded],
        [],
        10**9,
        raw,
        perm,
        one,
        two_kernel,
        core_out,
    )
    core_in = core_exchange(core_out)

    message = shape(2 * two + HALF, lat_cells)
    edges = shape(HALF, rows)
    far_out, near_out, core_in, mid_in = call(
        message_kernel, [message, message, edges, edges], [], 10**6, x_rows, cot_rows, core_in, mid_in
    )
    count = lax.axis_size("lon")
    far_in = lax.ppermute(far_out, "lon", [(i, (i + 1 if i % 2 else i - 1) % count) for i in range(count)])
    near_in = lax.ppermute(near_out, "lon", [(i, i ^ 1) for i in range(count)])

    inner_rows = rows - two
    shifted = pltpu.VMEM((3, rows, lat_cells), BF)
    pre_inner, inner_grads = call(
        inner_kernel,
        [shape(inner_rows, lat_cells), shape(2, 3, channels, 128, dtype=F32)],
        [shifted, shifted, pltpu.VMEM((2, 3, GROUP * channels, WINDOW * channels), F32)],
        4 * 10**9,
        x_rows, cot_rows, core_in, mid_in, first, back,
    )
    edge_shifted = pltpu.VMEM((2, 3, 2 * two, lat_cells), BF)
    partial = shape(2 * 9 * channels * channels // 128, 128, dtype=F32)
    pre_low, pre_high, grads, from_left, from_right = call(
        edge_kernel,
        [shape(two, lat_cells), shape(two, lat_cells), partial, message, message],
        [edge_shifted, edge_shifted],
        10**9,
        x_rows, cot_rows, core_in, mid_in, far_in, near_in, first, back, inner_grads,
    )
    def widen(partial):
        return call(
            outer_kernel,
            [shape(3, rows + two, lat_cells), weights, shape(*partial.shape, dtype=F32)],
            [
                pltpu.VMEM((rows + 2 * two, lat_cells), BF),
                pltpu.VMEM((2, HALF, rows + 2 * two), F32),
            ],
            10**9,
            x_rows, cot_rows, core_in, mid_in, from_left, from_right, first, back,
            pre_low, pre_inner, pre_high, one, partial,
        )

    def finish(shifted, last, partial):
        return call(
            last_kernel,
            [shape(channels, lon_cells, lat_cells), shape(*partial.shape, dtype=F32)],
            [
                pltpu.VMEM((lat_cells // 128, rows, 128), F32),
                pltpu.VMEM((channels, lon_cells, lat_cells), BF),
                pltpu.SemaphoreType.DMA((lon_cells // HALF,)),
            ],
            2 * 10**9,
            shifted, last, raw, partial,
            hbm_out=(0,),
        )

    total, given, input_grad = sum_everywhere(grads, widen, finish)
    grad_one, grad_two = call(
        functools.partial(result_kernel, 1.0 / math.sqrt(cells)),
        [shape(3, 3, channels, channels, dtype=F32)] * 2,
        [],
        10**6,
        total,
        given,
    )
    return (input_grad, grad_one, grad_two)


def solution(mesh):
    placed = (P(None, "lon", "lat"), P(), P(), P(None, "lon", "lat"))
    return jax.shard_map(
        on_device,
        mesh=mesh,
        in_specs=placed,
        out_specs=(P(None, "lon", "lat"), P(), P()),
        check_vma=False,
    )
```

```python
import functools
import math

import jax
import jax.numpy as jnp
from jax import lax
from jax.experimental import pallas as pl
from jax.experimental.pallas import tpu as pltpu
from jax.sharding import PartitionSpec as P

BF = jnp.bfloat16
F32 = jnp.float32
GROUP = 6
WINDOW = GROUP + 2
HALF = 16
PARAMS = pltpu.CompilerParams(vmem_limit_bytes=16 * 2**20)


def dot(left, right):
    return lax.dot_general(left, right, (((1,), (0,)), ((), ())), preferred_element_type=F32)


def dot_lanes(left, right):
    return lax.dot_general(left, right, (((1,), (1,)), ((), ())), preferred_element_type=F32)


def dot_rows(left, right):
    return lax.dot_general(left, right, (((0,), (0,)), ((), ())), preferred_element_type=F32)


def iota(shape, dim):
    return lax.broadcasted_iota(jnp.int32, shape, dim)


def call(kernel, outs, scratch, flops, *operands, hbm_in=(), hbm_out=()):
    spaces = [pltpu.HBM if i in hbm_in else pltpu.VMEM for i in range(len(operands))]
    out_spaces = [pltpu.HBM if i in hbm_out else pltpu.VMEM for i in range(len(outs))]
    bytes_moved = sum(o.size * o.dtype.itemsize for o in (*operands, *outs))
    operands = [pltpu.with_memory_space_constraint(o, pltpu.HBM) if i in hbm_in else o for i, o in enumerate(operands)]
    return pl.pallas_call(
        kernel,
        out_shape=outs,
        in_specs=[pl.BlockSpec(memory_space=space) for space in spaces],
        out_specs=[pl.BlockSpec(memory_space=space) for space in out_spaces],
        scratch_shapes=scratch,
        compiler_params=PARAMS,
        cost_estimate=pl.CostEstimate(flops=flops, bytes_accessed=bytes_moved, transcendentals=0),
    )(*operands)


def shape(*dims, dtype=BF):
    return jax.ShapeDtypeStruct(dims, dtype)


def is_odd():
    return lax.axis_index("lat") % 2


def border_kernel(x_hbm, cot_hbm, one_hbm, two_hbm, raw_ref, one_ref, two_ref, perm_ref, core_ref, mid_ref, sems):
    channels, lon_cells, lat_cells = x_hbm.shape
    parts = lon_cells // HALF
    pieces = [(one_hbm, one_ref), (two_hbm, two_ref)]
    for place, source in enumerate((x_hbm, cot_hbm)):
        for part in range(parts):
            pieces.append((source.at[:, pl.ds(part * HALF, HALF), :], raw_ref.at[place * parts + part]))
    copies = [pltpu.make_async_copy(*piece, sems.at[number]) for number, piece in enumerate(pieces)]
    for copy in copies:
        copy.start()
    to_row = iota(perm_ref.shape, 0)
    from_row = iota(perm_ref.shape, 1)
    moved = (to_row % channels) * HALF + to_row // channels
    perm_ref[...] = jnp.where(from_row == moved, 1.0, 0.0).astype(BF)
    odd = is_odd()
    row = iota((2 * HALF, lat_cells), 0)
    lane = iota((2 * HALF, lat_cells), 1)
    high = jnp.where(row < HALF, 1 - odd, odd)
    cell = jnp.where(high == 1, lat_cells - 2, 0) + row % 2
    chosen = [
        (((row % HALF) // 2 == place) & (lane == cell)).astype(F32).astype(BF) for place in range(2)
    ]
    rows = HALF * channels
    for copy in copies:
        copy.wait()
    folded = [[], []]
    for part in range(parts):
        edges = sum(
            dot_lanes(chosen[place], raw_ref[place * parts + part].reshape(rows, lat_cells)) for place in range(2)
        )
        edges = dot_lanes(edges.astype(BF), perm_ref[...])
        for first in range(0, rows, lat_cells):
            for half in range(2):
                folded[half].append(edges[half * HALF : half * HALF + 4, first : first + lat_cells])
    core_ref[...] = jnp.concatenate(folded[0], 0).astype(BF)
    mid_ref[...] = jnp.concatenate(folded[1], 0).astype(BF)


def unfold(edges):
    wide = edges.astype(F32)
    lanes = jnp.concatenate([wide[first : first + 4] for first in range(0, wide.shape[0], 4)], 1)
    return jnp.concatenate([lanes, jnp.zeros((HALF - 4, lanes.shape[1]), F32)], 0)


def row_kernel(raw_ref, perm_ref, one_ref, two_ref, core_ref, xl_ref, cl_ref, first_ref, back_ref, passed_ref):
    passed_ref[...] = core_ref[...]
    rows = perm_ref.shape[0]
    parts = xl_ref.shape[0] // rows
    for place, target in enumerate((xl_ref, cl_ref)):
        for part in range(parts):
            block = raw_ref[place * parts + part].reshape(rows, target.shape[1])
            target[part * rows : (part + 1) * rows, :] = dot(perm_ref[...], block).astype(BF)
    write_band(one_ref, False, first_ref)
    write_band(two_ref, True, back_ref)


def write_band(kernel, transposed, target):
    channels = kernel.shape[2]
    lanes = WINDOW * channels
    tiled = (iota((channels, lanes), 1) % channels == iota((channels, lanes), 0)).astype(F32).astype(BF)
    block = iota((channels, lanes), 1) // channels
    for q in range(3):
        if transposed:
            bases = [dot_rows(kernel[2 - p, 2 - q], tiled) for p in range(3)]
        else:
            bases = [dot(kernel[p, q], tiled) for p in range(3)]
        for a in range(GROUP):
            band = jnp.zeros((channels, lanes), F32)
            for p in range(3):
                band = jnp.where(block == a + p, bases[p], band)
            target[q, a * channels : (a + 1) * channels, :] = band.astype(BF)


def lon_is_odd():
    return lax.axis_index("lon") % 2


def message_kernel(x_ref, cot_ref, core_in, mid_in, far_ref, near_ref, core_ref, mid_ref):
    rows, lat_cells = x_ref.shape
    two = (far_ref.shape[0] - HALF) // 2
    core, mid = unfold(core_in[...]), unfold(mid_in[...])
    core_ref[...] = core.astype(BF)
    mid_ref[...] = mid.astype(BF)
    odd = lon_is_odd()
    for target, high in ((far_ref, odd), (near_ref, 1 - odd)):
        part = pl.ds(pl.multiple_of(high * (rows - two), two), two)
        target[0:two, :] = x_ref[part, :]
        target[two : 2 * two, :] = cot_ref[part, :]
        halos = [
            jnp.where(high == 1, value[:, rows - two :], value[:, :two]).astype(BF) for value in (core, mid)
        ]
        target[2 * two :, : 2 * two] = jnp.concatenate(halos, 1)
        target[2 * two :, 2 * two :] = jnp.zeros((HALF, lat_cells - 2 * two), BF)


def halo_place(odd, place, lat_cells):
    row = iota((2 * HALF, lat_cells), 0)
    lane = iota((2 * HALF, lat_cells), 1)
    from_low = jnp.where(row < HALF, odd, 1 - odd) == 1
    wanted_row = 2 * place + jnp.where(from_low, 1, 0)
    wanted_lane = jnp.where(from_low, 0, lat_cells - 1)
    lat = lax.axis_index("lat")
    inside = jnp.where(row < HALF, 1, lat * (lax.axis_size("lat") - 1 - lat))
    return ((row % HALF == wanted_row) & (lane == wanted_lane) & (inside > 0)).astype(F32).astype(BF)


def write_shifted(values, edge_columns, target, rows):
    lat_cells = values.shape[1]
    lane = iota(values.shape, 1)
    columns = edge_columns.astype(BF)
    target[0, rows, :] = jnp.where(lane == 0, columns, pltpu.roll(values, 1, 1))
    target[1, rows, :] = values
    target[2, rows, :] = jnp.where(lane == lat_cells - 1, columns, pltpu.roll(values, lat_cells - 1, 1))


def activate(pre_act, back_grad):
    sigmoid_value = 1.0 / (1.0 + jnp.exp(-pre_act))
    activation = pre_act * sigmoid_value
    slope = sigmoid_value + activation * (1.0 - sigmoid_value)
    return activation, back_grad * slope


def conv_rows(weight_ref, shifted, rows, out_rows):
    count = rows.stop - rows.start
    return sum(dot(weight_ref[q, :out_rows, :count], shifted[q, rows, :]) for q in range(3))


def inner_kernel(x_ref, cot_ref, core_ref, mid_ref, first_ref, back_ref, pre_ref, grads_ref, xs, cs, total):
    lat_cells = x_ref.shape[1]
    channels = grads_ref.shape[2]
    odd = is_odd()
    halos = jnp.concatenate([core_ref[...], mid_ref[...]], 0)
    everything = slice(0, x_ref.shape[0])
    for place, (source, target) in enumerate(((x_ref, xs), (cot_ref, cs))):
        columns = dot_rows(halos, halo_place(odd, place, lat_cells))
        write_shifted(source[...], columns, target, everything)
    group_rows = GROUP * channels
    for k in range(pre_ref.shape[0] // group_rows):
        rows = slice(k * group_rows, k * group_rows + WINDOW * channels)
        pre_act = conv_rows(first_ref, xs, rows, group_rows)
        back_grad = conv_rows(back_ref, cs, rows, group_rows)
        activation, pre_grad = activate(pre_act, back_grad)
        activation = activation.astype(BF)
        pre_grad = pre_grad.astype(BF)
        pre_ref[k * group_rows : (k + 1) * group_rows, :] = pre_grad
        for q in range(3):
            for place, (own, raw) in enumerate(((pre_grad, xs), (activation, cs))):
                term = dot_lanes(own, raw[q, rows, :])
                if k == 0:
                    total[place, q] = term
                else:
                    total[place, q] += term
    for place in range(2):
        for q in range(3):
            summed = jnp.zeros((channels, WINDOW * channels), F32)
            for a in range(GROUP):
                band = total[place, q, a * channels : (a + 1) * channels, :]
                if a:
                    band = pltpu.roll(band, WINDOW * channels - a * channels, 1)
                summed = summed + band
            grads_ref[place, q] = summed[:, :128]


def sides_of(far, near):
    far, near = far.astype(F32), near.astype(F32)
    odd = lon_is_odd()
    return jnp.where(odd == 1, near, far), jnp.where(odd == 1, far, near)


def write_edges(side, sent, sent_halos, own_refs, shifted, two):
    x_ref, cot_ref, core_ref, mid_ref = own_refs
    own_rows, lat_cells = x_ref.shape
    own = slice(0, two) if side == 0 else slice(own_rows - two, own_rows)
    own_halos = jnp.concatenate([core_ref[:, own], mid_ref[:, own]], 0).astype(F32)
    order = (sent_halos, own_halos) if side == 0 else (own_halos, sent_halos)
    halos = jnp.concatenate(order, 1).astype(BF)
    for place, source in enumerate((x_ref, cot_ref)):
        order = (sent[place], source[own, :]) if side == 0 else (source[own, :], sent[place])
        values = jnp.concatenate(order, 0)
        columns = dot_rows(halos, halo_place(is_odd(), place, lat_cells))
        write_shifted(values, columns, shifted[place].at[side], slice(0, values.shape[0]))


def edge_kernel(x_ref, cot_ref, core_ref, mid_ref, far_ref, near_ref, first_ref, back_ref, grads_ref,
                out_ref, xs_sides, cs_sides):
    channels = grads_ref.shape[2]
    two = 2 * channels
    sums = [[grads_ref[place, q][:, : 3 * channels] for q in range(3)] for place in range(2)]
    parts = []
    for first in (0, channels):
        rows = [far_ref[place * two + first : place * two + first + channels, :] for place in range(2)]
        more = [near_ref[place * two + first : place * two + first + channels, :] for place in range(2)]
        parts.append([sides_of(*pair) for pair in zip(rows, more)])
    halos = sides_of(far_ref[2 * two :, : 2 * two], near_ref[2 * two :, : 2 * two])
    for side in range(2):
        sent = [parts[1 - side][place][side].astype(BF) for place in range(2)]
        lanes = [half * two + (1 - side) * channels for half in range(2)]
        sent_halos = jnp.concatenate([halos[side][:, lane : lane + channels] for lane in lanes], 0)
        write_edges(side, sent, sent_halos, (x_ref, cot_ref, core_ref, mid_ref), (xs_sides, cs_sides), two)
    rows = slice(0, 3 * channels)
    pre_acts = [conv_rows(first_ref, xs_sides.at[side], rows, channels) for side in range(2)]
    back_grads = [conv_rows(back_ref, cs_sides.at[side], rows, channels) for side in range(2)]
    for side in range(2):
        activation, pre_grad = activate(pre_acts[side], back_grads[side])
        activation, pre_grad = activation.astype(BF), pre_grad.astype(BF)
        for q in range(3):
            sums[0][q] = sums[0][q] + dot_lanes(pre_grad, xs_sides[side, q, :, :])
            sums[1][q] = sums[1][q] + dot_lanes(activation, cs_sides[side, q, :, :])
    out_ref[...] = jnp.concatenate([pack_taps(taps) for taps in sums], 0)


def rim_kernel(x_ref, cot_ref, core_ref, mid_ref, far_ref, near_ref, first_ref, back_ref,
               partial_ref, low_ref, high_ref, left_ref, right_ref, passed_ref, xs_sides, cs_sides):
    passed_ref[...] = partial_ref[...]
    two = low_ref.shape[0]
    messages = sides_of(far_ref[...], near_ref[...])
    for side, target in enumerate((left_ref, right_ref)):
        target[...] = messages[side].astype(BF)
        sent = [messages[side][place * two : (place + 1) * two].astype(BF) for place in range(2)]
        halos = messages[side][2 * two :]
        sent_halos = jnp.concatenate([halos[:, :two], halos[:, two : 2 * two]], 0)
        write_edges(side, sent, sent_halos, (x_ref, cot_ref, core_ref, mid_ref), (xs_sides, cs_sides), two)
    rows = slice(0, 2 * two)
    for side, target in enumerate((low_ref, high_ref)):
        pre_act = conv_rows(first_ref, xs_sides.at[side], rows, two)
        back_grad = conv_rows(back_ref, cs_sides.at[side], rows, two)
        target[...] = activate(pre_act, back_grad)[1].astype(BF)


def pack_taps(taps):
    channels = taps[0].shape[0]
    main = [
        jnp.concatenate([taps[q], taps[2][:, q * channels : (q + 1) * channels]], 1) for q in range(2)
    ]
    rest = taps[2][:, 2 * channels :]
    count = 128 // channels
    rows = channels // count
    last = jnp.concatenate([rest[i * rows : (i + 1) * rows] for i in range(count)], 1)
    return jnp.concatenate([*main, last], 0)


def unpack_taps(packed, channels):
    used = 3 * channels
    count = 128 // channels
    main = [packed[q * channels : (q + 1) * channels] for q in range(2)]
    rest = packed[2 * channels :]
    last = jnp.concatenate([rest[:, i * channels : (i + 1) * channels] for i in range(count)], 0)
    third = jnp.concatenate([main[0][:, used:], main[1][:, used:], last], 1)
    return [main[0], main[1], third]


def outer_kernel(x_ref, cot_ref, core_ref, mid_ref, left_ref, right_ref, first_ref, back_ref, low_ref, pre_ref,
                 high_ref, one_ref, partial_ref, ps, last_ref, passed_ref, rows_buffer, strips):
    passed_ref[...] = partial_ref[...]
    write_band(one_ref, True, last_ref)
    lat_cells = x_ref.shape[1]
    channels = low_ref.shape[0] // 2
    two = 2 * channels
    own_rows = x_ref.shape[0]
    wide_rows = own_rows + 2 * two
    odd = is_odd()
    core, mid = core_ref[...].astype(F32), mid_ref[...].astype(F32)
    lat = lax.axis_index("lat")
    lat_count = lax.axis_size("lat")

    def halo_lanes(value, first):
        parts = [left_ref[2 * two : 2 * two + HALF, first : first + two].astype(F32), value,
                 right_ref[2 * two : 2 * two + HALF, first : first + two].astype(F32)]
        return parts

    def put(target, parts):
        target[:, 0:two] = parts[0]
        target[:, two : two + own_rows] = parts[1]
        target[:, two + own_rows : wide_rows] = parts[2]

    put(strips.at[0], halo_lanes(core, 0))
    put(strips.at[1], halo_lanes(mid, two))
    core_wide, mid_wide = strips[0], strips[1]
    low = jnp.where(odd == 1, core_wide, mid_wide)
    high = jnp.where(odd == 1, mid_wide, core_wide)
    row = iota((HALF, lat_cells), 0)
    lane = iota((HALF, lat_cells), 1)
    ends = ((row < 2) & (lane == row * (lat_cells - 1))).astype(F32).astype(BF)
    values = []
    span = 4 * channels
    window = 6 * channels
    for place, (source, weight_ref) in enumerate(((x_ref, first_ref), (cot_ref, back_ref))):
        rows_buffer[0:two, :] = left_ref[place * two : (place + 1) * two, :]
        rows_buffer[two : two + own_rows, :] = source[...]
        rows_buffer[two + own_rows : wide_rows, :] = right_ref[place * two : (place + 1) * two, :]
        own = dot_lanes(ends, rows_buffer[...])
        low_rows = [low[2 * place : 2 * place + 1], low[2 * place + 1 : 2 * place + 2], own[0:1]]
        high_rows = [own[1:2], high[2 * place : 2 * place + 1], high[2 * place + 1 : 2 * place + 2]]
        total = None
        for q in range(3):
            which = iota((HALF, wide_rows), 0)
            strip = jnp.where(which == 0, low_rows[q], jnp.where(which == 1, high_rows[q], 0.0))
            strip = jnp.concatenate([strip, jnp.zeros((HALF, 128), F32)], 1)
            stacked = jnp.concatenate(
                [strip[:, k : k + window] for k in range(0, wide_rows, span)], 0
            ).astype(BF)
            term = dot_lanes(stacked, weight_ref[q, :span, :window])
            total = term if total is None else total + term
        values.append(total)
    _, pre_grad = activate(*values)
    beyond = jnp.where(iota(pre_grad.shape, 0) % HALF == 0, lat, lat_count - 1 - lat)
    pre_grad = jnp.where(beyond > 0, pre_grad, 0.0)
    pre_strip = jnp.concatenate(
        [pre_grad[k : k + HALF] for k in range(0, pre_grad.shape[0], HALF)], 1
    ).astype(BF)
    wide = pre_ref.shape[0] + 2 * two
    columns = dot_rows(pre_strip, ends)[:wide]
    rows_buffer[0:two, :] = low_ref[...]
    rows_buffer[two : wide - two, :] = pre_ref[...]
    rows_buffer[wide - two : wide, :] = high_ref[...]
    write_shifted(rows_buffer[0:wide, :], columns, ps, slice(0, wide))


def last_kernel(ps, last_ref, raw_ref, partial_ref, out_ref, passed_ref, placed, result, sems):
    passed_ref[...] = partial_ref[...]
    channels, lon_cells, lat_cells = out_ref.shape
    parts = lon_cells // HALF
    copies = []
    done = 0
    for first in range(0, lon_cells, GROUP):
        lons = min(GROUP, lon_cells - first)
        rows = slice(first * channels, (first + lons + 2) * channels)
        total = conv_rows(last_ref, ps, rows, lons * channels)
        for a in range(lons):
            lon_rows = total[a * channels : (a + 1) * channels]
            for tile in range(lat_cells // 128):
                lanes = slice(tile * 128, (tile + 1) * 128)
                placed[tile, pl.ds(first + a, channels, stride=lon_cells), :] = lon_rows[:, lanes]
        if first + lons >= done + HALF:
            part = slice(done, done + HALF)
            for tile in range(lat_cells // 128):
                lanes = slice(tile * 128, (tile + 1) * 128)
                block = placed[tile].reshape(channels, lon_cells, 128)[:, part, :]
                block = block + raw_ref[parts + done // HALF, :, :, lanes].astype(F32)
                result[:, part, lanes] = block.astype(BF)
            copy = pltpu.make_async_copy(
                result.at[:, pl.ds(done, HALF), :], out_ref.at[:, pl.ds(done, HALF), :], sems.at[done // HALF]
            )
            copy.start()
            copies.append(copy)
            done += HALF
    for copy in copies:
        copy.wait()


def result_kernel(scale, total_ref, given_ref, one_ref, two_ref):
    channels = one_ref.shape[2]
    rows = total_ref.shape[0] // 2
    sums = jnp.where(is_odd() == 1, total_ref[...], given_ref[...]) * scale
    first, second = sums[:rows], sums[rows:]
    first = unpack_taps(first, channels)
    second = unpack_taps(second, channels)
    for q in range(3):
        for p in range(3):
            lanes = slice(p * channels, (p + 1) * channels)
            one_ref[p, q] = first[q][:, lanes]
            two_ref[2 - p, 2 - q] = second[q][:, lanes].T


ALONG_X, ALONG_Y = 32, 1


def pairs(counts, partner, idle):
    lat_count, lon_count = counts
    listed = []
    for lat in range(lat_count):
        for lon in range(lon_count):
            to_lat, to_lon = partner(lat, lon) if lat % 2 else (lat, lon ^ idle)
            listed.append((lat * lon_count + lon, to_lat * lon_count + to_lon))
    return listed


def x_partner(mask):
    def partner(lat, lon):
        place = ((lat >> 1) * 2 + (lon >> 5)) ^ mask
        return (place >> 1) * 2 + (lat & 1), (place & 1) * 32 + (lon & 31)

    return partner


def y_partner(mask):
    return lambda lat, lon: (lat, lon ^ mask)


def z_partner(mask):
    return lambda lat, lon: (lat, lon ^ (mask << 2))


def exchange(value, partner, idle):
    counts = (lax.axis_size("lat"), lax.axis_size("lon"))
    return lax.ppermute(value, ("lat", "lon"), pairs(counts, partner, idle))


def sum_of_four(value, partner, masks, idle, beside):
    first, second, third = [exchange(value, partner(mask), idle) for mask in masks]
    *result, value = beside(value)
    return (value + first) + (second + third), result


def sum_everywhere(mine, rim, widen, finish):
    total = mine + core_exchange(mine)
    total, edges = sum_of_four(total, x_partner, (1, 3, 2), ALONG_Y, rim)
    total, shifted = sum_of_four(
        total, y_partner, (1, 3, 2), ALONG_X, lambda value: widen(*edges, value)
    )
    total, (input_grad,) = sum_of_four(
        total, z_partner, (1, 2, 3), ALONG_X, lambda value: finish(*shifted, value)
    )
    total = total + exchange(total, z_partner(6), ALONG_X)
    given = core_exchange(total)
    return total, given, input_grad


def mid_exchange(edges):
    count = lax.axis_size("lat")
    return lax.ppermute(edges, "lat", [(i, (i - 1 if i % 2 == 0 else i + 1) % count) for i in range(count)])


def core_exchange(value):
    return lax.ppermute(value, "lat", [(i, i ^ 1) for i in range(lax.axis_size("lat"))])


def on_device(inputs, kernel_one, kernel_two, cotangent):
    channels, lon_cells, lat_cells = inputs.shape
    cells = lon_cells * lat_cells * lax.axis_size("lat") * lax.axis_size("lon")
    rows = channels * lon_cells
    two = 2 * channels
    parts = lon_cells // HALF
    weights = shape(3, GROUP * channels, WINDOW * channels)
    folded = shape(4 * rows // lat_cells, lat_cells)
    raw, one, two_kernel, perm, core_out, mid_out = call(
        border_kernel,
        [
            shape(2 * parts, channels, HALF, lat_cells),
            shape(*kernel_one.shape),
            shape(*kernel_two.shape),
            shape(HALF * channels, HALF * channels),
            folded,
            folded,
        ],
        [pltpu.SemaphoreType.DMA((2 + 2 * parts,))],
        10**8,
        inputs,
        cotangent,
        kernel_one,
        kernel_two,
        hbm_in=(0, 1, 2, 3),
    )
    mid_in = mid_exchange(mid_out)
    x_rows, cot_rows, first, back, core_out = call(
        row_kernel,
        [shape(rows, lat_cells), shape(rows, lat_cells), weights, weights, folded],
        [],
        10**9,
        raw,
        perm,
        one,
        two_kernel,
        core_out,
    )
    core_in = core_exchange(core_out)

    message = shape(2 * two + HALF, lat_cells)
    edges = shape(HALF, rows)
    far_out, near_out, core_in, mid_in = call(
        message_kernel, [message, message, edges, edges], [], 10**6, x_rows, cot_rows, core_in, mid_in
    )
    count = lax.axis_size("lon")
    far_in = lax.ppermute(far_out, "lon", [(i, (i + 1 if i % 2 else i - 1) % count) for i in range(count)])
    near_in = lax.ppermute(near_out, "lon", [(i, i ^ 1) for i in range(count)])

    inner_rows = rows - two
    shifted = pltpu.VMEM((3, rows, lat_cells), BF)
    pre_inner, inner_grads = call(
        inner_kernel,
        [shape(inner_rows, lat_cells), shape(2, 3, channels, 128, dtype=F32)],
        [shifted, shifted, pltpu.VMEM((2, 3, GROUP * channels, WINDOW * channels), F32)],
        4 * 10**9,
        x_rows, cot_rows, core_in, mid_in, first, back,
    )
    partial = shape(2 * 9 * channels * channels // 128, 128, dtype=F32)
    edge_shifted = pltpu.VMEM((2, 3, 3 * channels, lat_cells), BF)
    (grads,) = call(
        edge_kernel,
        [partial],
        [edge_shifted, edge_shifted],
        10**9,
        x_rows, cot_rows, core_in, mid_in, far_in, near_in, first, back, inner_grads,
    )

    def rim(partial):
        rim_shifted = pltpu.VMEM((2, 3, 2 * two, lat_cells), BF)
        return call(
            rim_kernel,
            [shape(two, lat_cells), shape(two, lat_cells), message, message, shape(*partial.shape, dtype=F32)],
            [rim_shifted, rim_shifted],
            10**9,
            x_rows, cot_rows, core_in, mid_in, far_in, near_in, first, back, partial,
        )

    def widen(pre_low, pre_high, from_left, from_right, partial):
        return call(
            outer_kernel,
            [shape(3, rows + two, lat_cells), weights, shape(*partial.shape, dtype=F32)],
            [
                pltpu.VMEM((rows + 2 * two, lat_cells), BF),
                pltpu.VMEM((2, HALF, rows + 2 * two), F32),
            ],
            10**9,
            x_rows, cot_rows, core_in, mid_in, from_left, from_right, first, back,
            pre_low, pre_inner, pre_high, one, partial,
        )

    def finish(shifted, last, partial):
        return call(
            last_kernel,
            [shape(channels, lon_cells, lat_cells), shape(*partial.shape, dtype=F32)],
            [
                pltpu.VMEM((lat_cells // 128, rows, 128), F32),
                pltpu.VMEM((channels, lon_cells, lat_cells), BF),
                pltpu.SemaphoreType.DMA((lon_cells // HALF,)),
            ],
            2 * 10**9,
            shifted, last, raw, partial,
            hbm_out=(0,),
        )

    total, given, input_grad = sum_everywhere(grads, rim, widen, finish)
    grad_one, grad_two = call(
        functools.partial(result_kernel, 1.0 / math.sqrt(cells)),
        [shape(3, 3, channels, channels, dtype=F32)] * 2,
        [],
        10**6,
        total,
        given,
    )
    return (input_grad, grad_one, grad_two)


def solution(mesh):
    placed = (P(None, "lon", "lat"), P(), P(), P(None, "lon", "lat"))
    return jax.shard_map(
        on_device,
        mesh=mesh,
        in_specs=placed,
        out_specs=(P(None, "lon", "lat"), P(), P()),
        check_vma=False,
    )
```

```python
import functools
import math

import jax
import jax.numpy as jnp
from jax import lax
from jax.experimental import pallas as pl
from jax.experimental.pallas import tpu as pltpu
from jax.sharding import PartitionSpec as P

BF = jnp.bfloat16
F32 = jnp.float32
GROUP = 6
WINDOW = GROUP + 2
HALF = 16
PARAMS = pltpu.CompilerParams(vmem_limit_bytes=16 * 2**20)


def dot(left, right):
    return lax.dot_general(left, right, (((1,), (0,)), ((), ())), preferred_element_type=F32)


def dot_lanes(left, right):
    return lax.dot_general(left, right, (((1,), (1,)), ((), ())), preferred_element_type=F32)


def dot_rows(left, right):
    return lax.dot_general(left, right, (((0,), (0,)), ((), ())), preferred_element_type=F32)


def iota(shape, dim):
    return lax.broadcasted_iota(jnp.int32, shape, dim)


def call(kernel, outs, scratch, flops, *operands, hbm_in=(), hbm_out=()):
    spaces = [pltpu.HBM if i in hbm_in else pltpu.VMEM for i in range(len(operands))]
    out_spaces = [pltpu.HBM if i in hbm_out else pltpu.VMEM for i in range(len(outs))]
    bytes_moved = sum(o.size * o.dtype.itemsize for o in (*operands, *outs))
    operands = [pltpu.with_memory_space_constraint(o, pltpu.HBM) if i in hbm_in else o for i, o in enumerate(operands)]
    return pl.pallas_call(
        kernel,
        out_shape=outs,
        in_specs=[pl.BlockSpec(memory_space=space) for space in spaces],
        out_specs=[pl.BlockSpec(memory_space=space) for space in out_spaces],
        scratch_shapes=scratch,
        compiler_params=PARAMS,
        cost_estimate=pl.CostEstimate(flops=flops, bytes_accessed=bytes_moved, transcendentals=0),
    )(*operands)


def shape(*dims, dtype=BF):
    return jax.ShapeDtypeStruct(dims, dtype)


def is_odd():
    return lax.axis_index("lat") % 2


def border_kernel(x_hbm, cot_hbm, one_hbm, two_hbm, raw_ref, one_ref, two_ref, perm_ref, core_ref, mid_ref, sems):
    channels, lon_cells, lat_cells = x_hbm.shape
    parts = lon_cells // HALF
    pieces = [(one_hbm, one_ref), (two_hbm, two_ref)]
    for place, source in enumerate((x_hbm, cot_hbm)):
        for part in range(parts):
            pieces.append((source.at[:, pl.ds(part * HALF, HALF), :], raw_ref.at[place * parts + part]))
    copies = [pltpu.make_async_copy(*piece, sems.at[number]) for number, piece in enumerate(pieces)]
    for copy in copies:
        copy.start()
    to_row = iota(perm_ref.shape, 0)
    from_row = iota(perm_ref.shape, 1)
    moved = (to_row % channels) * HALF + to_row // channels
    perm_ref[...] = jnp.where(from_row == moved, 1.0, 0.0).astype(BF)
    odd = is_odd()
    row = iota((2 * HALF, lat_cells), 0)
    lane = iota((2 * HALF, lat_cells), 1)
    high = jnp.where(row < HALF, 1 - odd, odd)
    cell = jnp.where(high == 1, lat_cells - 2, 0) + row % 2
    chosen = [
        (((row % HALF) // 2 == place) & (lane == cell)).astype(F32).astype(BF) for place in range(2)
    ]
    rows = HALF * channels
    for copy in copies:
        copy.wait()
    folded = [[], []]
    for part in range(parts):
        edges = sum(
            dot_lanes(chosen[place], raw_ref[place * parts + part].reshape(rows, lat_cells)) for place in range(2)
        )
        edges = dot_lanes(edges.astype(BF), perm_ref[...])
        for first in range(0, rows, lat_cells):
            for half in range(2):
                folded[half].append(edges[half * HALF : half * HALF + 4, first : first + lat_cells])
    core_ref[...] = jnp.concatenate(folded[0], 0).astype(BF)
    mid_ref[...] = jnp.concatenate(folded[1], 0).astype(BF)


def unfold(edges):
    wide = edges.astype(F32)
    lanes = jnp.concatenate([wide[first : first + 4] for first in range(0, wide.shape[0], 4)], 1)
    return jnp.concatenate([lanes, jnp.zeros((HALF - 4, lanes.shape[1]), F32)], 0)


def row_kernel(raw_ref, perm_ref, one_ref, two_ref, core_ref, xl_ref, cl_ref, first_ref, back_ref, passed_ref):
    passed_ref[...] = core_ref[...]
    rows = perm_ref.shape[0]
    parts = xl_ref.shape[0] // rows
    for place, target in enumerate((xl_ref, cl_ref)):
        for part in range(parts):
            block = raw_ref[place * parts + part].reshape(rows, target.shape[1])
            target[part * rows : (part + 1) * rows, :] = dot(perm_ref[...], block).astype(BF)
    write_band(one_ref, False, first_ref)
    write_band(two_ref, True, back_ref)


def write_band(kernel, transposed, target):
    channels = kernel.shape[2]
    lanes = WINDOW * channels
    tiled = (iota((channels, lanes), 1) % channels == iota((channels, lanes), 0)).astype(F32).astype(BF)
    block = iota((channels, lanes), 1) // channels
    for q in range(3):
        if transposed:
            bases = [dot_rows(kernel[2 - p, 2 - q], tiled) for p in range(3)]
        else:
            bases = [dot(kernel[p, q], tiled) for p in range(3)]
        for a in range(GROUP):
            band = jnp.zeros((channels, lanes), F32)
            for p in range(3):
                band = jnp.where(block == a + p, bases[p], band)
            target[q, a * channels : (a + 1) * channels, :] = band.astype(BF)


def lon_is_odd():
    return lax.axis_index("lon") % 2


def message_kernel(x_ref, cot_ref, core_in, mid_in, far_ref, near_ref, core_ref, mid_ref):
    rows, lat_cells = x_ref.shape
    two = (far_ref.shape[0] - HALF) // 2
    core, mid = unfold(core_in[...]), unfold(mid_in[...])
    core_ref[...] = core.astype(BF)
    mid_ref[...] = mid.astype(BF)
    odd = lon_is_odd()
    for target, high in ((far_ref, odd), (near_ref, 1 - odd)):
        part = pl.ds(pl.multiple_of(high * (rows - two), two), two)
        target[0:two, :] = x_ref[part, :]
        target[two : 2 * two, :] = cot_ref[part, :]
        halos = [
            jnp.where(high == 1, value[:, rows - two :], value[:, :two]).astype(BF) for value in (core, mid)
        ]
        target[2 * two :, : 2 * two] = jnp.concatenate(halos, 1)
        target[2 * two :, 2 * two :] = jnp.zeros((HALF, lat_cells - 2 * two), BF)


def halo_place(odd, place, lat_cells):
    row = iota((2 * HALF, lat_cells), 0)
    lane = iota((2 * HALF, lat_cells), 1)
    from_low = jnp.where(row < HALF, odd, 1 - odd) == 1
    wanted_row = 2 * place + jnp.where(from_low, 1, 0)
    wanted_lane = jnp.where(from_low, 0, lat_cells - 1)
    lat = lax.axis_index("lat")
    inside = jnp.where(row < HALF, 1, lat * (lax.axis_size("lat") - 1 - lat))
    return ((row % HALF == wanted_row) & (lane == wanted_lane) & (inside > 0)).astype(F32).astype(BF)


def write_shifted(values, edge_columns, target, rows):
    lat_cells = values.shape[1]
    lane = iota(values.shape, 1)
    columns = edge_columns.astype(BF)
    target[0, rows, :] = jnp.where(lane == 0, columns, pltpu.roll(values, 1, 1))
    target[1, rows, :] = values
    target[2, rows, :] = jnp.where(lane == lat_cells - 1, columns, pltpu.roll(values, lat_cells - 1, 1))


def activate(pre_act, back_grad):
    sigmoid_value = 1.0 / (1.0 + jnp.exp(-pre_act))
    activation = pre_act * sigmoid_value
    slope = sigmoid_value + activation * (1.0 - sigmoid_value)
    return activation, back_grad * slope


def conv_rows(weight_ref, shifted, rows, out_rows):
    count = rows.stop - rows.start
    return sum(dot(weight_ref[q, :out_rows, :count], shifted[q, rows, :]) for q in range(3))


def inner_kernel(x_ref, cot_ref, core_ref, mid_ref, first_ref, back_ref, pre_ref, grads_ref, xs, cs, total):
    lat_cells = x_ref.shape[1]
    channels = grads_ref.shape[2]
    odd = is_odd()
    halos = jnp.concatenate([core_ref[...], mid_ref[...]], 0)
    everything = slice(0, x_ref.shape[0])
    for place, (source, target) in enumerate(((x_ref, xs), (cot_ref, cs))):
        columns = dot_rows(halos, halo_place(odd, place, lat_cells))
        write_shifted(source[...], columns, target, everything)
    group_rows = GROUP * channels
    for k in range(pre_ref.shape[0] // group_rows):
        rows = slice(k * group_rows, k * group_rows + WINDOW * channels)
        pre_act = conv_rows(first_ref, xs, rows, group_rows)
        back_grad = conv_rows(back_ref, cs, rows, group_rows)
        activation, pre_grad = activate(pre_act, back_grad)
        activation = activation.astype(BF)
        pre_grad = pre_grad.astype(BF)
        pre_ref[k * group_rows : (k + 1) * group_rows, :] = pre_grad
        for q in range(3):
            for place, (own, raw) in enumerate(((pre_grad, xs), (activation, cs))):
                term = dot_lanes(own, raw[q, rows, :])
                if k == 0:
                    total[place, q] = term
                else:
                    total[place, q] += term
    for place in range(2):
        for q in range(3):
            summed = jnp.zeros((channels, WINDOW * channels), F32)
            for a in range(GROUP):
                band = total[place, q, a * channels : (a + 1) * channels, :]
                if a:
                    band = pltpu.roll(band, WINDOW * channels - a * channels, 1)
                summed = summed + band
            grads_ref[place, q] = summed[:, :128]


def edge_kernel(x_ref, cot_ref, core_ref, mid_ref, far_ref, near_ref, first_ref, back_ref, grads_ref,
                low_ref, high_ref, out_ref, left_ref, right_ref, xs_sides, cs_sides):
    lat_cells = x_ref.shape[1]
    channels = grads_ref.shape[2]
    odd = is_odd()
    two = 2 * channels
    own_rows = x_ref.shape[0]
    sums = [[grads_ref[place, q][:, : 3 * channels] for q in range(3)] for place in range(2)]
    far, near = far_ref[...].astype(F32), near_ref[...].astype(F32)
    left_ref[...] = jnp.where(lon_is_odd() == 1, near, far).astype(BF)
    right_ref[...] = jnp.where(lon_is_odd() == 1, far, near).astype(BF)
    sides = ((left_ref, low_ref), (right_ref, high_ref))
    for side, (message, _) in enumerate(sides):
        own = slice(0, two) if side == 0 else slice(own_rows - two, own_rows)
        sent = message[2 * two : 2 * two + HALF, :]
        sent_halos = jnp.concatenate([sent[:, :two], sent[:, two : 2 * two]], 0).astype(F32)
        own_halos = jnp.concatenate([core_ref[:, own], mid_ref[:, own]], 0).astype(F32)
        order = (sent_halos, own_halos) if side == 0 else (own_halos, sent_halos)
        halos = jnp.concatenate(order, 1).astype(BF)
        for place, (source, shifted) in enumerate(((x_ref, xs_sides), (cot_ref, cs_sides))):
            sent_rows = message[place * two : (place + 1) * two, :]
            order = (sent_rows, source[own, :]) if side == 0 else (source[own, :], sent_rows)
            columns = dot_rows(halos, halo_place(odd, place, lat_cells))
            write_shifted(jnp.concatenate(order, 0), columns, shifted.at[side], slice(0, 2 * two))
    rows = slice(0, 2 * two)
    pre_acts = [conv_rows(first_ref, xs_sides.at[side], rows, two) for side in range(2)]
    back_grads = [conv_rows(back_ref, cs_sides.at[side], rows, two) for side in range(2)]
    for side, (_, target) in enumerate(sides):
        activation, pre_grad = activate(pre_acts[side], back_grads[side])
        pre_grad = pre_grad.astype(BF)
        target[...] = pre_grad
        mine = slice(channels, two) if side == 0 else slice(0, channels)
        near = slice(channels, 2 * two) if side == 0 else slice(0, 3 * channels)
        activation = activation[mine].astype(BF)
        pre_grad = pre_grad[mine]
        for q in range(3):
            sums[0][q] = sums[0][q] + dot_lanes(pre_grad, xs_sides[side, q, near, :])
            sums[1][q] = sums[1][q] + dot_lanes(activation, cs_sides[side, q, near, :])
    out_ref[...] = jnp.concatenate([pack_taps(taps) for taps in sums], 0)


def pack_taps(taps):
    channels = taps[0].shape[0]
    main = [
        jnp.concatenate([taps[q], taps[2][:, q * channels : (q + 1) * channels]], 1) for q in range(2)
    ]
    rest = taps[2][:, 2 * channels :]
    count = 128 // channels
    rows = channels // count
    last = jnp.concatenate([rest[i * rows : (i + 1) * rows] for i in range(count)], 1)
    return jnp.concatenate([*main, last], 0)


def unpack_taps(packed, channels):
    used = 3 * channels
    count = 128 // channels
    main = [packed[q * channels : (q + 1) * channels] for q in range(2)]
    rest = packed[2 * channels :]
    last = jnp.concatenate([rest[:, i * channels : (i + 1) * channels] for i in range(count)], 0)
    third = jnp.concatenate([main[0][:, used:], main[1][:, used:], last], 1)
    return [main[0], main[1], third]


def outer_kernel(x_ref, cot_ref, core_ref, mid_ref, left_ref, right_ref, first_ref, back_ref, low_ref, pre_ref,
                 high_ref, one_ref, partial_ref, ps, last_ref, passed_ref, rows_buffer, strips):
    passed_ref[...] = partial_ref[...]
    write_band(one_ref, True, last_ref)
    lat_cells = x_ref.shape[1]
    channels = low_ref.shape[0] // 2
    two = 2 * channels
    own_rows = x_ref.shape[0]
    wide_rows = own_rows + 2 * two
    odd = is_odd()
    core, mid = core_ref[...].astype(F32), mid_ref[...].astype(F32)
    lat = lax.axis_index("lat")
    lat_count = lax.axis_size("lat")

    def halo_lanes(value, first):
        parts = [left_ref[2 * two : 2 * two + HALF, first : first + two].astype(F32), value,
                 right_ref[2 * two : 2 * two + HALF, first : first + two].astype(F32)]
        return parts

    def put(target, parts):
        target[:, 0:two] = parts[0]
        target[:, two : two + own_rows] = parts[1]
        target[:, two + own_rows : wide_rows] = parts[2]

    put(strips.at[0], halo_lanes(core, 0))
    put(strips.at[1], halo_lanes(mid, two))
    core_wide, mid_wide = strips[0], strips[1]
    low = jnp.where(odd == 1, core_wide, mid_wide)
    high = jnp.where(odd == 1, mid_wide, core_wide)
    row = iota((HALF, lat_cells), 0)
    lane = iota((HALF, lat_cells), 1)
    ends = ((row < 2) & (lane == row * (lat_cells - 1))).astype(F32).astype(BF)
    values = []
    span = 4 * channels
    window = 6 * channels
    for place, (source, weight_ref) in enumerate(((x_ref, first_ref), (cot_ref, back_ref))):
        rows_buffer[0:two, :] = left_ref[place * two : (place + 1) * two, :]
        rows_buffer[two : two + own_rows, :] = source[...]
        rows_buffer[two + own_rows : wide_rows, :] = right_ref[place * two : (place + 1) * two, :]
        own = dot_lanes(ends, rows_buffer[...])
        low_rows = [low[2 * place : 2 * place + 1], low[2 * place + 1 : 2 * place + 2], own[0:1]]
        high_rows = [own[1:2], high[2 * place : 2 * place + 1], high[2 * place + 1 : 2 * place + 2]]
        total = None
        for q in range(3):
            which = iota((HALF, wide_rows), 0)
            strip = jnp.where(which == 0, low_rows[q], jnp.where(which == 1, high_rows[q], 0.0))
            strip = jnp.concatenate([strip, jnp.zeros((HALF, 128), F32)], 1)
            stacked = jnp.concatenate(
                [strip[:, k : k + window] for k in range(0, wide_rows, span)], 0
            ).astype(BF)
            term = dot_lanes(stacked, weight_ref[q, :span, :window])
            total = term if total is None else total + term
        values.append(total)
    _, pre_grad = activate(*values)
    beyond = jnp.where(iota(pre_grad.shape, 0) % HALF == 0, lat, lat_count - 1 - lat)
    pre_grad = jnp.where(beyond > 0, pre_grad, 0.0)
    pre_strip = jnp.concatenate(
        [pre_grad[k : k + HALF] for k in range(0, pre_grad.shape[0], HALF)], 1
    ).astype(BF)
    wide = pre_ref.shape[0] + 2 * two
    columns = dot_rows(pre_strip, ends)[:wide]
    rows_buffer[0:two, :] = low_ref[...]
    rows_buffer[two : wide - two, :] = pre_ref[...]
    rows_buffer[wide - two : wide, :] = high_ref[...]
    write_shifted(rows_buffer[0:wide, :], columns, ps, slice(0, wide))


def last_kernel(ps, last_ref, raw_ref, partial_ref, out_ref, passed_ref, placed, result, sems):
    passed_ref[...] = partial_ref[...]
    channels, lon_cells, lat_cells = out_ref.shape
    parts = lon_cells // HALF
    copies = []
    done = 0
    for first in range(0, lon_cells, GROUP):
        lons = min(GROUP, lon_cells - first)
        rows = slice(first * channels, (first + lons + 2) * channels)
        total = conv_rows(last_ref, ps, rows, lons * channels)
        for a in range(lons):
            lon_rows = total[a * channels : (a + 1) * channels]
            for tile in range(lat_cells // 128):
                lanes = slice(tile * 128, (tile + 1) * 128)
                placed[tile, pl.ds(first + a, channels, stride=lon_cells), :] = lon_rows[:, lanes]
        if first + lons >= done + HALF:
            part = slice(done, done + HALF)
            for tile in range(lat_cells // 128):
                lanes = slice(tile * 128, (tile + 1) * 128)
                block = placed[tile].reshape(channels, lon_cells, 128)[:, part, :]
                block = block + raw_ref[parts + done // HALF, :, :, lanes].astype(F32)
                result[:, part, lanes] = block.astype(BF)
            copy = pltpu.make_async_copy(
                result.at[:, pl.ds(done, HALF), :], out_ref.at[:, pl.ds(done, HALF), :], sems.at[done // HALF]
            )
            copy.start()
            copies.append(copy)
            done += HALF
    for copy in copies:
        copy.wait()


def result_kernel(scale, total_ref, given_ref, one_ref, two_ref):
    channels = one_ref.shape[2]
    rows = total_ref.shape[0] // 2
    sums = jnp.where(is_odd() == 1, total_ref[...], given_ref[...]) * scale
    first, second = sums[:rows], sums[rows:]
    first = unpack_taps(first, channels)
    second = unpack_taps(second, channels)
    for q in range(3):
        for p in range(3):
            lanes = slice(p * channels, (p + 1) * channels)
            one_ref[p, q] = first[q][:, lanes]
            two_ref[2 - p, 2 - q] = second[q][:, lanes].T


ALONG_X, ALONG_Y = 32, 1


def pairs(counts, partner, idle):
    lat_count, lon_count = counts
    listed = []
    for lat in range(lat_count):
        for lon in range(lon_count):
            to_lat, to_lon = partner(lat, lon) if lat % 2 else (lat, lon ^ idle)
            listed.append((lat * lon_count + lon, to_lat * lon_count + to_lon))
    return listed


def x_partner(mask):
    def partner(lat, lon):
        place = ((lat >> 1) * 2 + (lon >> 5)) ^ mask
        return (place >> 1) * 2 + (lat & 1), (place & 1) * 32 + (lon & 31)

    return partner


def y_partner(mask):
    return lambda lat, lon: (lat, lon ^ mask)


def z_partner(mask):
    return lambda lat, lon: (lat, lon ^ (mask << 2))


def exchange(value, partner, idle):
    counts = (lax.axis_size("lat"), lax.axis_size("lon"))
    return lax.ppermute(value, ("lat", "lon"), pairs(counts, partner, idle))


def sum_of_four(value, partner, masks, idle, beside=None):
    first, second, third = [exchange(value, partner(mask), idle) for mask in masks]
    result = None
    if beside is not None:
        *result, value = beside(value)
    return (value + first) + (second + third), result


def sum_everywhere(mine, widen, finish):
    total = mine + core_exchange(mine)
    total, _ = sum_of_four(total, z_partner, (1, 2, 3), ALONG_X)
    total = total + exchange(total, z_partner(6), ALONG_X)
    total, shifted = sum_of_four(total, x_partner, (1, 3, 2), ALONG_Y, widen)
    total, (input_grad,) = sum_of_four(
        total, y_partner, (1, 3, 2), ALONG_X, lambda value: finish(*shifted, value)
    )
    given = core_exchange(total)
    return total, given, input_grad


def mid_exchange(edges):
    count = lax.axis_size("lat")
    return lax.ppermute(edges, "lat", [(i, (i - 1 if i % 2 == 0 else i + 1) % count) for i in range(count)])


def core_exchange(value):
    return lax.ppermute(value, "lat", [(i, i ^ 1) for i in range(lax.axis_size("lat"))])


def on_device(inputs, kernel_one, kernel_two, cotangent):
    channels, lon_cells, lat_cells = inputs.shape
    cells = lon_cells * lat_cells * lax.axis_size("lat") * lax.axis_size("lon")
    rows = channels * lon_cells
    two = 2 * channels
    parts = lon_cells // HALF
    weights = shape(3, GROUP * channels, WINDOW * channels)
    folded = shape(4 * rows // lat_cells, lat_cells)
    raw, one, two_kernel, perm, core_out, mid_out = call(
        border_kernel,
        [
            shape(2 * parts, channels, HALF, lat_cells),
            shape(*kernel_one.shape),
            shape(*kernel_two.shape),
            shape(HALF * channels, HALF * channels),
            folded,
            folded,
        ],
        [pltpu.SemaphoreType.DMA((2 + 2 * parts,))],
        10**8,
        inputs,
        cotangent,
        kernel_one,
        kernel_two,
        hbm_in=(0, 1, 2, 3),
    )
    mid_in = mid_exchange(mid_out)
    x_rows, cot_rows, first, back, core_out = call(
        row_kernel,
        [shape(rows, lat_cells), shape(rows, lat_cells), weights, weights, folded],
        [],
        10**9,
        raw,
        perm,
        one,
        two_kernel,
        core_out,
    )
    core_in = core_exchange(core_out)

    message = shape(2 * two + HALF, lat_cells)
    edges = shape(HALF, rows)
    far_out, near_out, core_in, mid_in = call(
        message_kernel, [message, message, edges, edges], [], 10**6, x_rows, cot_rows, core_in, mid_in
    )
    count = lax.axis_size("lon")
    far_in = lax.ppermute(far_out, "lon", [(i, (i + 1 if i % 2 else i - 1) % count) for i in range(count)])
    near_in = lax.ppermute(near_out, "lon", [(i, i ^ 1) for i in range(count)])

    inner_rows = rows - two
    shifted = pltpu.VMEM((3, rows, lat_cells), BF)
    pre_inner, inner_grads = call(
        inner_kernel,
        [shape(inner_rows, lat_cells), shape(2, 3, channels, 128, dtype=F32)],
        [shifted, shifted, pltpu.VMEM((2, 3, GROUP * channels, WINDOW * channels), F32)],
        4 * 10**9,
        x_rows, cot_rows, core_in, mid_in, first, back,
    )
    edge_shifted = pltpu.VMEM((2, 3, 2 * two, lat_cells), BF)
    partial = shape(2 * 9 * channels * channels // 128, 128, dtype=F32)
    pre_low, pre_high, grads, from_left, from_right = call(
        edge_kernel,
        [shape(two, lat_cells), shape(two, lat_cells), partial, message, message],
        [edge_shifted, edge_shifted],
        10**9,
        x_rows, cot_rows, core_in, mid_in, far_in, near_in, first, back, inner_grads,
    )
    def widen(partial):
        return call(
            outer_kernel,
            [shape(3, rows + two, lat_cells), weights, shape(*partial.shape, dtype=F32)],
            [
                pltpu.VMEM((rows + 2 * two, lat_cells), BF),
                pltpu.VMEM((2, HALF, rows + 2 * two), F32),
            ],
            10**9,
            x_rows, cot_rows, core_in, mid_in, from_left, from_right, first, back,
            pre_low, pre_inner, pre_high, one, partial,
        )

    def finish(shifted, last, partial):
        return call(
            last_kernel,
            [shape(channels, lon_cells, lat_cells), shape(*partial.shape, dtype=F32)],
            [
                pltpu.VMEM((lat_cells // 128, rows, 128), F32),
                pltpu.VMEM((channels, lon_cells, lat_cells), BF),
                pltpu.SemaphoreType.DMA((lon_cells // HALF,)),
            ],
            2 * 10**9,
            shifted, last, raw, partial,
            hbm_out=(0,),
        )

    total, given, input_grad = sum_everywhere(grads, widen, finish)
    grad_one, grad_two = call(
        functools.partial(result_kernel, 1.0 / math.sqrt(cells)),
        [shape(3, 3, channels, channels, dtype=F32)] * 2,
        [],
        10**6,
        total,
        given,
    )
    return (input_grad, grad_one, grad_two)


def solution(mesh):
    placed = (P(None, "lon", "lat"), P(), P(), P(None, "lon", "lat"))
    return jax.shard_map(
        on_device,
        mesh=mesh,
        in_specs=placed,
        out_specs=(P(None, "lon", "lat"), P(), P()),
        check_vma=False,
    )
```

```python
import functools
import math

import jax
import jax.numpy as jnp
from jax import lax
from jax.experimental import pallas as pl
from jax.experimental.pallas import tpu as pltpu
from jax.sharding import PartitionSpec as P

BF = jnp.bfloat16
F32 = jnp.float32
GROUP = 6
WINDOW = GROUP + 2
HALF = 16
PARAMS = pltpu.CompilerParams(vmem_limit_bytes=16 * 2**20)


def dot(left, right):
    return lax.dot_general(left, right, (((1,), (0,)), ((), ())), preferred_element_type=F32)


def dot_lanes(left, right):
    return lax.dot_general(left, right, (((1,), (1,)), ((), ())), preferred_element_type=F32)


def dot_rows(left, right):
    return lax.dot_general(left, right, (((0,), (0,)), ((), ())), preferred_element_type=F32)


def iota(shape, dim):
    return lax.broadcasted_iota(jnp.int32, shape, dim)


def call(kernel, outs, scratch, flops, *operands, hbm_in=(), hbm_out=()):
    spaces = [pltpu.HBM if i in hbm_in else pltpu.VMEM for i in range(len(operands))]
    out_spaces = [pltpu.HBM if i in hbm_out else pltpu.VMEM for i in range(len(outs))]
    bytes_moved = sum(o.size * o.dtype.itemsize for o in (*operands, *outs))
    operands = [pltpu.with_memory_space_constraint(o, pltpu.HBM) if i in hbm_in else o for i, o in enumerate(operands)]
    return pl.pallas_call(
        kernel,
        out_shape=outs,
        in_specs=[pl.BlockSpec(memory_space=space) for space in spaces],
        out_specs=[pl.BlockSpec(memory_space=space) for space in out_spaces],
        scratch_shapes=scratch,
        compiler_params=PARAMS,
        cost_estimate=pl.CostEstimate(flops=flops, bytes_accessed=bytes_moved, transcendentals=0),
    )(*operands)


def shape(*dims, dtype=BF):
    return jax.ShapeDtypeStruct(dims, dtype)


def is_odd():
    return lax.axis_index("lat") % 2


def border_kernel(x_hbm, cot_hbm, one_hbm, two_hbm, raw_ref, one_ref, two_ref, perm_ref, core_ref, mid_ref, sems):
    channels, lon_cells, lat_cells = x_hbm.shape
    parts = lon_cells // HALF
    pieces = [(one_hbm, one_ref), (two_hbm, two_ref)]
    for place, source in enumerate((x_hbm, cot_hbm)):
        for part in range(parts):
            pieces.append((source.at[:, pl.ds(part * HALF, HALF), :], raw_ref.at[place * parts + part]))
    copies = [pltpu.make_async_copy(*piece, sems.at[number]) for number, piece in enumerate(pieces)]
    for copy in copies:
        copy.start()
    to_row = iota(perm_ref.shape, 0)
    from_row = iota(perm_ref.shape, 1)
    moved = (to_row % channels) * HALF + to_row // channels
    perm_ref[...] = jnp.where(from_row == moved, 1.0, 0.0).astype(BF)
    odd = is_odd()
    row = iota((2 * HALF, lat_cells), 0)
    lane = iota((2 * HALF, lat_cells), 1)
    high = jnp.where(row < HALF, 1 - odd, odd)
    cell = jnp.where(high == 1, lat_cells - 2, 0) + row % 2
    chosen = [
        (((row % HALF) // 2 == place) & (lane == cell)).astype(F32).astype(BF) for place in range(2)
    ]
    rows = HALF * channels
    for copy in copies:
        copy.wait()
    folded = [[], []]
    for part in range(parts):
        edges = sum(
            dot_lanes(chosen[place], raw_ref[place * parts + part].reshape(rows, lat_cells)) for place in range(2)
        )
        edges = dot_lanes(edges.astype(BF), perm_ref[...])
        for first in range(0, rows, lat_cells):
            for half in range(2):
                folded[half].append(edges[half * HALF : half * HALF + 4, first : first + lat_cells])
    core_ref[...] = jnp.concatenate(folded[0], 0).astype(BF)
    mid_ref[...] = jnp.concatenate(folded[1], 0).astype(BF)


def unfold(edges):
    wide = edges.astype(F32)
    lanes = jnp.concatenate([wide[first : first + 4] for first in range(0, wide.shape[0], 4)], 1)
    return jnp.concatenate([lanes, jnp.zeros((HALF - 4, lanes.shape[1]), F32)], 0)


def row_kernel(raw_ref, perm_ref, one_ref, two_ref, core_ref, xl_ref, cl_ref, first_ref, back_ref, passed_ref):
    passed_ref[...] = core_ref[...]
    rows = perm_ref.shape[0]
    parts = xl_ref.shape[0] // rows
    for place, target in enumerate((xl_ref, cl_ref)):
        for part in range(parts):
            block = raw_ref[place * parts + part].reshape(rows, target.shape[1])
            target[part * rows : (part + 1) * rows, :] = dot(perm_ref[...], block).astype(BF)
    write_band(one_ref, False, first_ref)
    write_band(two_ref, True, back_ref)


def write_band(kernel, transposed, target):
    channels = kernel.shape[2]
    lanes = WINDOW * channels
    tiled = (iota((channels, lanes), 1) % channels == iota((channels, lanes), 0)).astype(F32).astype(BF)
    block = iota((channels, lanes), 1) // channels
    for q in range(3):
        if transposed:
            bases = [dot_rows(kernel[2 - p, 2 - q], tiled) for p in range(3)]
        else:
            bases = [dot(kernel[p, q], tiled) for p in range(3)]
        for a in range(GROUP):
            band = jnp.zeros((channels, lanes), F32)
            for p in range(3):
                band = jnp.where(block == a + p, bases[p], band)
            target[q, a * channels : (a + 1) * channels, :] = band.astype(BF)


def lon_is_odd():
    return lax.axis_index("lon") % 2


def message_kernel(x_ref, cot_ref, core_in, mid_in, far_ref, near_ref, core_ref, mid_ref):
    rows, lat_cells = x_ref.shape
    two = (far_ref.shape[0] - HALF) // 2
    core, mid = unfold(core_in[...]), unfold(mid_in[...])
    core_ref[...] = core.astype(BF)
    mid_ref[...] = mid.astype(BF)
    odd = lon_is_odd()
    for target, high in ((far_ref, odd), (near_ref, 1 - odd)):
        part = pl.ds(pl.multiple_of(high * (rows - two), two), two)
        target[0:two, :] = x_ref[part, :]
        target[two : 2 * two, :] = cot_ref[part, :]
        halos = [
            jnp.where(high == 1, value[:, rows - two :], value[:, :two]).astype(BF) for value in (core, mid)
        ]
        target[2 * two :, : 2 * two] = jnp.concatenate(halos, 1)
        target[2 * two :, 2 * two :] = jnp.zeros((HALF, lat_cells - 2 * two), BF)


def halo_place(odd, place, lat_cells):
    row = iota((2 * HALF, lat_cells), 0)
    lane = iota((2 * HALF, lat_cells), 1)
    from_low = jnp.where(row < HALF, odd, 1 - odd) == 1
    wanted_row = 2 * place + jnp.where(from_low, 1, 0)
    wanted_lane = jnp.where(from_low, 0, lat_cells - 1)
    lat = lax.axis_index("lat")
    inside = jnp.where(row < HALF, 1, lat * (lax.axis_size("lat") - 1 - lat))
    return ((row % HALF == wanted_row) & (lane == wanted_lane) & (inside > 0)).astype(F32).astype(BF)


def halo_places(odd, lat_cells):
    return jnp.concatenate([halo_place(odd, place, lat_cells) for place in range(2)], 1)


def write_shifted(values, edge_columns, target, rows):
    lat_cells = values.shape[1]
    lane = iota(values.shape, 1)
    columns = edge_columns.astype(BF)
    target[0, rows, :] = jnp.where(lane == 0, columns, pltpu.roll(values, 1, 1))
    target[1, rows, :] = values
    target[2, rows, :] = jnp.where(lane == lat_cells - 1, columns, pltpu.roll(values, lat_cells - 1, 1))


def activate(pre_act, back_grad):
    sigmoid_value = 1.0 / (1.0 + jnp.exp(-pre_act))
    activation = pre_act * sigmoid_value
    slope = sigmoid_value + activation * (1.0 - sigmoid_value)
    return activation, back_grad * slope


def conv_rows(weight_ref, shifted, rows, out_rows):
    count = rows.stop - rows.start
    return sum(dot(weight_ref[q, :out_rows, :count], shifted[q, rows, :]) for q in range(3))


def inner_kernel(x_ref, cot_ref, core_ref, mid_ref, first_ref, back_ref, pre_ref, grads_ref, xs, cs, total):
    lat_cells = x_ref.shape[1]
    channels = grads_ref.shape[2]
    odd = is_odd()
    halos = jnp.concatenate([core_ref[...], mid_ref[...]], 0)
    everything = slice(0, x_ref.shape[0])
    columns = dot_rows(halos, halo_places(odd, lat_cells))
    for place, (source, target) in enumerate(((x_ref, xs), (cot_ref, cs))):
        write_shifted(source[...], columns[:, place * lat_cells : (place + 1) * lat_cells], target, everything)
    group_rows = GROUP * channels
    for k in range(pre_ref.shape[0] // group_rows):
        rows = slice(k * group_rows, k * group_rows + WINDOW * channels)
        pre_act = conv_rows(first_ref, xs, rows, group_rows)
        back_grad = conv_rows(back_ref, cs, rows, group_rows)
        activation, pre_grad = activate(pre_act, back_grad)
        activation = activation.astype(BF)
        pre_grad = pre_grad.astype(BF)
        pre_ref[k * group_rows : (k + 1) * group_rows, :] = pre_grad
        for q in range(3):
            for place, (own, raw) in enumerate(((pre_grad, xs), (activation, cs))):
                term = dot_lanes(own, raw[q, rows, :])
                if k == 0:
                    total[place, q] = term
                else:
                    total[place, q] += term
    for place in range(2):
        for q in range(3):
            summed = jnp.zeros((channels, WINDOW * channels), F32)
            for a in range(GROUP):
                band = total[place, q, a * channels : (a + 1) * channels, :]
                if a:
                    band = pltpu.roll(band, WINDOW * channels - a * channels, 1)
                summed = summed + band
            grads_ref[place, q] = summed[:, :128]


def edge_kernel(x_ref, cot_ref, core_ref, mid_ref, far_ref, near_ref, first_ref, back_ref, grads_ref,
                low_ref, high_ref, out_ref, left_ref, right_ref, xs_sides, cs_sides):
    lat_cells = x_ref.shape[1]
    channels = grads_ref.shape[2]
    odd = is_odd()
    two = 2 * channels
    own_rows = x_ref.shape[0]
    sums = [[grads_ref[place, q][:, : 3 * channels] for q in range(3)] for place in range(2)]
    far, near = far_ref[...].astype(F32), near_ref[...].astype(F32)
    left_ref[...] = jnp.where(lon_is_odd() == 1, near, far).astype(BF)
    right_ref[...] = jnp.where(lon_is_odd() == 1, far, near).astype(BF)
    sides = ((left_ref, low_ref), (right_ref, high_ref))
    places = halo_places(odd, lat_cells)
    for side, (message, _) in enumerate(sides):
        own = slice(0, two) if side == 0 else slice(own_rows - two, own_rows)
        sent = message[2 * two : 2 * two + HALF, :]
        sent_halos = jnp.concatenate([sent[:, :two], sent[:, two : 2 * two]], 0).astype(F32)
        own_halos = jnp.concatenate([core_ref[:, own], mid_ref[:, own]], 0).astype(F32)
        order = (sent_halos, own_halos) if side == 0 else (own_halos, sent_halos)
        halos = jnp.concatenate(order, 1).astype(BF)
        both = dot_rows(halos, places)
        for place, (source, shifted) in enumerate(((x_ref, xs_sides), (cot_ref, cs_sides))):
            sent_rows = message[place * two : (place + 1) * two, :]
            order = (sent_rows, source[own, :]) if side == 0 else (source[own, :], sent_rows)
            columns = both[:, place * lat_cells : (place + 1) * lat_cells]
            write_shifted(jnp.concatenate(order, 0), columns, shifted.at[side], slice(0, 2 * two))
    rows = slice(0, 2 * two)
    pre_acts = [conv_rows(first_ref, xs_sides.at[side], rows, two) for side in range(2)]
    back_grads = [conv_rows(back_ref, cs_sides.at[side], rows, two) for side in range(2)]
    for side, (_, target) in enumerate(sides):
        activation, pre_grad = activate(pre_acts[side], back_grads[side])
        pre_grad = pre_grad.astype(BF)
        target[...] = pre_grad
        mine = slice(channels, two) if side == 0 else slice(0, channels)
        near = slice(channels, 2 * two) if side == 0 else slice(0, 3 * channels)
        activation = activation[mine].astype(BF)
        pre_grad = pre_grad[mine]
        for q in range(3):
            sums[0][q] = sums[0][q] + dot_lanes(pre_grad, xs_sides[side, q, near, :])
            sums[1][q] = sums[1][q] + dot_lanes(activation, cs_sides[side, q, near, :])
    out_ref[...] = jnp.concatenate([pack_taps(taps) for taps in sums], 0)


def pack_taps(taps):
    channels = taps[0].shape[0]
    main = [
        jnp.concatenate([taps[q], taps[2][:, q * channels : (q + 1) * channels]], 1) for q in range(2)
    ]
    rest = taps[2][:, 2 * channels :]
    count = 128 // channels
    rows = channels // count
    last = jnp.concatenate([rest[i * rows : (i + 1) * rows] for i in range(count)], 1)
    return jnp.concatenate([*main, last], 0)


def unpack_taps(packed, channels):
    used = 3 * channels
    count = 128 // channels
    main = [packed[q * channels : (q + 1) * channels] for q in range(2)]
    rest = packed[2 * channels :]
    last = jnp.concatenate([rest[:, i * channels : (i + 1) * channels] for i in range(count)], 0)
    third = jnp.concatenate([main[0][:, used:], main[1][:, used:], last], 1)
    return [main[0], main[1], third]


def outer_kernel(x_ref, cot_ref, core_ref, mid_ref, left_ref, right_ref, first_ref, back_ref, low_ref, pre_ref,
                 high_ref, one_ref, partial_ref, ps, last_ref, passed_ref, rows_buffer, strips):
    passed_ref[...] = partial_ref[...]
    write_band(one_ref, True, last_ref)
    lat_cells = x_ref.shape[1]
    channels = low_ref.shape[0] // 2
    two = 2 * channels
    own_rows = x_ref.shape[0]
    wide_rows = own_rows + 2 * two
    odd = is_odd()
    core, mid = core_ref[...].astype(F32), mid_ref[...].astype(F32)
    lat = lax.axis_index("lat")
    lat_count = lax.axis_size("lat")

    def halo_lanes(value, first):
        parts = [left_ref[2 * two : 2 * two + HALF, first : first + two].astype(F32), value,
                 right_ref[2 * two : 2 * two + HALF, first : first + two].astype(F32)]
        return parts

    def put(target, parts):
        target[:, 0:two] = parts[0]
        target[:, two : two + own_rows] = parts[1]
        target[:, two + own_rows : wide_rows] = parts[2]

    put(strips.at[0], halo_lanes(core, 0))
    put(strips.at[1], halo_lanes(mid, two))
    core_wide, mid_wide = strips[0], strips[1]
    low = jnp.where(odd == 1, core_wide, mid_wide)
    high = jnp.where(odd == 1, mid_wide, core_wide)
    row = iota((HALF, lat_cells), 0)
    lane = iota((HALF, lat_cells), 1)
    ends = ((row < 2) & (lane == row * (lat_cells - 1))).astype(F32).astype(BF)
    values = []
    span = 4 * channels
    window = 6 * channels
    for place, (source, weight_ref) in enumerate(((x_ref, first_ref), (cot_ref, back_ref))):
        rows_buffer[0:two, :] = left_ref[place * two : (place + 1) * two, :]
        rows_buffer[two : two + own_rows, :] = source[...]
        rows_buffer[two + own_rows : wide_rows, :] = right_ref[place * two : (place + 1) * two, :]
        own = dot_lanes(ends, rows_buffer[...])
        low_rows = [low[2 * place : 2 * place + 1], low[2 * place + 1 : 2 * place + 2], own[0:1]]
        high_rows = [own[1:2], high[2 * place : 2 * place + 1], high[2 * place + 1 : 2 * place + 2]]
        total = None
        for q in range(3):
            which = iota((HALF, wide_rows), 0)
            strip = jnp.where(which == 0, low_rows[q], jnp.where(which == 1, high_rows[q], 0.0))
            strip = jnp.concatenate([strip, jnp.zeros((HALF, 128), F32)], 1)
            stacked = jnp.concatenate(
                [strip[:, k : k + window] for k in range(0, wide_rows, span)], 0
            ).astype(BF)
            term = dot_lanes(stacked, weight_ref[q, :span, :window])
            total = term if total is None else total + term
        values.append(total)
    _, pre_grad = activate(*values)
    beyond = jnp.where(iota(pre_grad.shape, 0) % HALF == 0, lat, lat_count - 1 - lat)
    pre_grad = jnp.where(beyond > 0, pre_grad, 0.0)
    pre_strip = jnp.concatenate(
        [pre_grad[k : k + HALF] for k in range(0, pre_grad.shape[0], HALF)], 1
    ).astype(BF)
    wide = pre_ref.shape[0] + 2 * two
    columns = dot_rows(pre_strip, ends)[:wide]
    rows_buffer[0:two, :] = low_ref[...]
    rows_buffer[two : wide - two, :] = pre_ref[...]
    rows_buffer[wide - two : wide, :] = high_ref[...]
    write_shifted(rows_buffer[0:wide, :], columns, ps, slice(0, wide))


def last_kernel(ps, last_ref, raw_ref, partial_ref, out_ref, passed_ref, placed, result, sems):
    passed_ref[...] = partial_ref[...]
    channels, lon_cells, lat_cells = out_ref.shape
    parts = lon_cells // HALF
    copies = []
    done = 0
    for first in range(0, lon_cells, GROUP):
        lons = min(GROUP, lon_cells - first)
        rows = slice(first * channels, (first + lons + 2) * channels)
        total = conv_rows(last_ref, ps, rows, lons * channels)
        for a in range(lons):
            lon_rows = total[a * channels : (a + 1) * channels]
            for tile in range(lat_cells // 128):
                lanes = slice(tile * 128, (tile + 1) * 128)
                placed[tile, pl.ds(first + a, channels, stride=lon_cells), :] = lon_rows[:, lanes]
        if first + lons >= done + HALF:
            part = slice(done, done + HALF)
            for tile in range(lat_cells // 128):
                lanes = slice(tile * 128, (tile + 1) * 128)
                block = placed[tile].reshape(channels, lon_cells, 128)[:, part, :]
                block = block + raw_ref[parts + done // HALF, :, :, lanes].astype(F32)
                result[:, part, lanes] = block.astype(BF)
            copy = pltpu.make_async_copy(
                result.at[:, pl.ds(done, HALF), :], out_ref.at[:, pl.ds(done, HALF), :], sems.at[done // HALF]
            )
            copy.start()
            copies.append(copy)
            done += HALF
    for copy in copies:
        copy.wait()


def result_kernel(scale, total_ref, given_ref, one_ref, two_ref):
    channels = one_ref.shape[2]
    rows = total_ref.shape[0] // 2
    sums = jnp.where(is_odd() == 1, total_ref[...], given_ref[...]) * scale
    first, second = sums[:rows], sums[rows:]
    first = unpack_taps(first, channels)
    second = unpack_taps(second, channels)
    for q in range(3):
        for p in range(3):
            lanes = slice(p * channels, (p + 1) * channels)
            one_ref[p, q] = first[q][:, lanes]
            two_ref[2 - p, 2 - q] = second[q][:, lanes].T


ALONG_X, ALONG_Y = 32, 1


def pairs(counts, partner, idle):
    lat_count, lon_count = counts
    listed = []
    for lat in range(lat_count):
        for lon in range(lon_count):
            to_lat, to_lon = partner(lat, lon) if lat % 2 else (lat, lon ^ idle)
            listed.append((lat * lon_count + lon, to_lat * lon_count + to_lon))
    return listed


def x_partner(mask):
    def partner(lat, lon):
        place = ((lat >> 1) * 2 + (lon >> 5)) ^ mask
        return (place >> 1) * 2 + (lat & 1), (place & 1) * 32 + (lon & 31)

    return partner


def y_partner(mask):
    return lambda lat, lon: (lat, lon ^ mask)


def z_partner(mask):
    return lambda lat, lon: (lat, lon ^ (mask << 2))


def exchange(value, partner, idle):
    counts = (lax.axis_size("lat"), lax.axis_size("lon"))
    return lax.ppermute(value, ("lat", "lon"), pairs(counts, partner, idle))


def sum_of_four(value, partner, masks, idle, beside=None):
    first, second, third = [exchange(value, partner(mask), idle) for mask in masks]
    result = None
    if beside is not None:
        *result, value = beside(value)
    return (value + first) + (second + third), result


def sum_everywhere(mine, widen, finish):
    total = mine + core_exchange(mine)
    total, _ = sum_of_four(total, x_partner, (1, 3, 2), ALONG_Y)
    total, shifted = sum_of_four(total, y_partner, (1, 3, 2), ALONG_X, widen)
    total, (input_grad,) = sum_of_four(
        total, z_partner, (1, 2, 3), ALONG_X, lambda value: finish(*shifted, value)
    )
    total = total + exchange(total, z_partner(6), ALONG_X)
    given = core_exchange(total)
    return total, given, input_grad


def mid_exchange(edges):
    count = lax.axis_size("lat")
    return lax.ppermute(edges, "lat", [(i, (i - 1 if i % 2 == 0 else i + 1) % count) for i in range(count)])


def core_exchange(value):
    return lax.ppermute(value, "lat", [(i, i ^ 1) for i in range(lax.axis_size("lat"))])


def on_device(inputs, kernel_one, kernel_two, cotangent):
    channels, lon_cells, lat_cells = inputs.shape
    cells = lon_cells * lat_cells * lax.axis_size("lat") * lax.axis_size("lon")
    rows = channels * lon_cells
    two = 2 * channels
    parts = lon_cells // HALF
    weights = shape(3, GROUP * channels, WINDOW * channels)
    folded = shape(4 * rows // lat_cells, lat_cells)
    raw, one, two_kernel, perm, core_out, mid_out = call(
        border_kernel,
        [
            shape(2 * parts, channels, HALF, lat_cells),
            shape(*kernel_one.shape),
            shape(*kernel_two.shape),
            shape(HALF * channels, HALF * channels),
            folded,
            folded,
        ],
        [pltpu.SemaphoreType.DMA((2 + 2 * parts,))],
        10**8,
        inputs,
        cotangent,
        kernel_one,
        kernel_two,
        hbm_in=(0, 1, 2, 3),
    )
    mid_in = mid_exchange(mid_out)
    x_rows, cot_rows, first, back, core_out = call(
        row_kernel,
        [shape(rows, lat_cells), shape(rows, lat_cells), weights, weights, folded],
        [],
        10**9,
        raw,
        perm,
        one,
        two_kernel,
        core_out,
    )
    core_in = core_exchange(core_out)

    message = shape(2 * two + HALF, lat_cells)
    edges = shape(HALF, rows)
    far_out, near_out, core_in, mid_in = call(
        message_kernel, [message, message, edges, edges], [], 10**6, x_rows, cot_rows, core_in, mid_in
    )
    count = lax.axis_size("lon")
    far_in = lax.ppermute(far_out, "lon", [(i, (i + 1 if i % 2 else i - 1) % count) for i in range(count)])
    near_in = lax.ppermute(near_out, "lon", [(i, i ^ 1) for i in range(count)])

    inner_rows = rows - two
    shifted = pltpu.VMEM((3, rows, lat_cells), BF)
    pre_inner, inner_grads = call(
        inner_kernel,
        [shape(inner_rows, lat_cells), shape(2, 3, channels, 128, dtype=F32)],
        [shifted, shifted, pltpu.VMEM((2, 3, GROUP * channels, WINDOW * channels), F32)],
        4 * 10**9,
        x_rows, cot_rows, core_in, mid_in, first, back,
    )
    edge_shifted = pltpu.VMEM((2, 3, 2 * two, lat_cells), BF)
    partial = shape(2 * 9 * channels * channels // 128, 128, dtype=F32)
    pre_low, pre_high, grads, from_left, from_right = call(
        edge_kernel,
        [shape(two, lat_cells), shape(two, lat_cells), partial, message, message],
        [edge_shifted, edge_shifted],
        10**9,
        x_rows, cot_rows, core_in, mid_in, far_in, near_in, first, back, inner_grads,
    )
    def widen(partial):
        return call(
            outer_kernel,
            [shape(3, rows + two, lat_cells), weights, shape(*partial.shape, dtype=F32)],
            [
                pltpu.VMEM((rows + 2 * two, lat_cells), BF),
                pltpu.VMEM((2, HALF, rows + 2 * two), F32),
            ],
            10**9,
            x_rows, cot_rows, core_in, mid_in, from_left, from_right, first, back,
            pre_low, pre_inner, pre_high, one, partial,
        )

    def finish(shifted, last, partial):
        return call(
            last_kernel,
            [shape(channels, lon_cells, lat_cells), shape(*partial.shape, dtype=F32)],
            [
                pltpu.VMEM((lat_cells // 128, rows, 128), F32),
                pltpu.VMEM((channels, lon_cells, lat_cells), BF),
                pltpu.SemaphoreType.DMA((lon_cells // HALF,)),
            ],
            2 * 10**9,
            shifted, last, raw, partial,
            hbm_out=(0,),
        )

    total, given, input_grad = sum_everywhere(grads, widen, finish)
    grad_one, grad_two = call(
        functools.partial(result_kernel, 1.0 / math.sqrt(cells)),
        [shape(3, 3, channels, channels, dtype=F32)] * 2,
        [],
        10**6,
        total,
        given,
    )
    return (input_grad, grad_one, grad_two)


def solution(mesh):
    placed = (P(None, "lon", "lat"), P(), P(), P(None, "lon", "lat"))
    return jax.shard_map(
        on_device,
        mesh=mesh,
        in_specs=placed,
        out_specs=(P(None, "lon", "lat"), P(), P()),
        check_vma=False,
    )
```

```python
import functools
import math

import jax
import jax.numpy as jnp
from jax import lax
from jax.experimental import pallas as pl
from jax.experimental.pallas import tpu as pltpu
from jax.sharding import PartitionSpec as P

BF = jnp.bfloat16
F32 = jnp.float32
GROUP = 6
WINDOW = GROUP + 2
HALF = 16
PARAMS = pltpu.CompilerParams(vmem_limit_bytes=16 * 2**20)


def dot(left, right):
    return lax.dot_general(left, right, (((1,), (0,)), ((), ())), preferred_element_type=F32)


def dot_lanes(left, right):
    return lax.dot_general(left, right, (((1,), (1,)), ((), ())), preferred_element_type=F32)


def dot_rows(left, right):
    return lax.dot_general(left, right, (((0,), (0,)), ((), ())), preferred_element_type=F32)


def iota(shape, dim):
    return lax.broadcasted_iota(jnp.int32, shape, dim)


def call(kernel, outs, scratch, flops, *operands, hbm_in=(), hbm_out=()):
    spaces = [pltpu.HBM if i in hbm_in else pltpu.VMEM for i in range(len(operands))]
    out_spaces = [pltpu.HBM if i in hbm_out else pltpu.VMEM for i in range(len(outs))]
    bytes_moved = sum(o.size * o.dtype.itemsize for o in (*operands, *outs))
    operands = [pltpu.with_memory_space_constraint(o, pltpu.HBM) if i in hbm_in else o for i, o in enumerate(operands)]
    return pl.pallas_call(
        kernel,
        out_shape=outs,
        in_specs=[pl.BlockSpec(memory_space=space) for space in spaces],
        out_specs=[pl.BlockSpec(memory_space=space) for space in out_spaces],
        scratch_shapes=scratch,
        compiler_params=PARAMS,
        cost_estimate=pl.CostEstimate(flops=flops, bytes_accessed=bytes_moved, transcendentals=0),
    )(*operands)


def shape(*dims, dtype=BF):
    return jax.ShapeDtypeStruct(dims, dtype)


def is_odd():
    return lax.axis_index("lat") % 2


def border_kernel(x_hbm, cot_hbm, one_hbm, two_hbm, raw_ref, one_ref, two_ref, perm_ref, core_ref, mid_ref, sems):
    channels, lon_cells, lat_cells = x_hbm.shape
    parts = lon_cells // HALF
    pieces = [(one_hbm, one_ref), (two_hbm, two_ref)]
    for place, source in enumerate((x_hbm, cot_hbm)):
        for part in range(parts):
            pieces.append((source.at[:, pl.ds(part * HALF, HALF), :], raw_ref.at[place * parts + part]))
    copies = [pltpu.make_async_copy(*piece, sems.at[number]) for number, piece in enumerate(pieces)]
    for copy in copies:
        copy.start()
    to_row = iota(perm_ref.shape, 0)
    from_row = iota(perm_ref.shape, 1)
    moved = (to_row % channels) * HALF + to_row // channels
    perm_ref[...] = jnp.where(from_row == moved, 1.0, 0.0).astype(BF)
    odd = is_odd()
    row = iota((2 * HALF, lat_cells), 0)
    lane = iota((2 * HALF, lat_cells), 1)
    high = jnp.where(row < HALF, 1 - odd, odd)
    cell = jnp.where(high == 1, lat_cells - 2, 0) + row % 2
    chosen = [
        (((row % HALF) // 2 == place) & (lane == cell)).astype(F32).astype(BF) for place in range(2)
    ]
    rows = HALF * channels
    for copy in copies:
        copy.wait()
    folded = [[], []]
    for part in range(parts):
        edges = sum(
            dot_lanes(chosen[place], raw_ref[place * parts + part].reshape(rows, lat_cells)) for place in range(2)
        )
        edges = dot_lanes(edges.astype(BF), perm_ref[...])
        for first in range(0, rows, lat_cells):
            for half in range(2):
                folded[half].append(edges[half * HALF : half * HALF + 4, first : first + lat_cells])
    core_ref[...] = jnp.concatenate(folded[0], 0).astype(BF)
    mid_ref[...] = jnp.concatenate(folded[1], 0).astype(BF)


def unfold(edges):
    wide = edges.astype(F32)
    lanes = jnp.concatenate([wide[first : first + 4] for first in range(0, wide.shape[0], 4)], 1)
    return jnp.concatenate([lanes, jnp.zeros((HALF - 4, lanes.shape[1]), F32)], 0)


def row_kernel(raw_ref, perm_ref, one_ref, two_ref, core_ref, xl_ref, cl_ref, first_ref, back_ref, passed_ref):
    passed_ref[...] = core_ref[...]
    rows = perm_ref.shape[0]
    parts = xl_ref.shape[0] // rows
    for place, target in enumerate((xl_ref, cl_ref)):
        for part in range(parts):
            block = raw_ref[place * parts + part].reshape(rows, target.shape[1])
            target[part * rows : (part + 1) * rows, :] = dot(perm_ref[...], block).astype(BF)
    write_band(one_ref, False, first_ref)
    write_band(two_ref, True, back_ref)


def write_band(kernel, transposed, target):
    channels = kernel.shape[2]
    lanes = WINDOW * channels
    tiled = (iota((channels, lanes), 1) % channels == iota((channels, lanes), 0)).astype(F32).astype(BF)
    block = iota((channels, lanes), 1) // channels
    for q in range(3):
        if transposed:
            bases = [dot_rows(kernel[2 - p, 2 - q], tiled) for p in range(3)]
        else:
            bases = [dot(kernel[p, q], tiled) for p in range(3)]
        for a in range(GROUP):
            band = jnp.zeros((channels, lanes), F32)
            for p in range(3):
                band = jnp.where(block == a + p, bases[p], band)
            target[q, a * channels : (a + 1) * channels, :] = band.astype(BF)


def lon_is_odd():
    return lax.axis_index("lon") % 2


def message_kernel(x_ref, cot_ref, core_in, mid_in, far_ref, near_ref, core_ref, mid_ref):
    rows, lat_cells = x_ref.shape
    two = (far_ref.shape[0] - HALF) // 2
    core, mid = unfold(core_in[...]), unfold(mid_in[...])
    core_ref[...] = core.astype(BF)
    mid_ref[...] = mid.astype(BF)
    odd = lon_is_odd()
    for target, high in ((far_ref, odd), (near_ref, 1 - odd)):
        part = pl.ds(pl.multiple_of(high * (rows - two), two), two)
        target[0:two, :] = x_ref[part, :]
        target[two : 2 * two, :] = cot_ref[part, :]
        halos = [
            jnp.where(high == 1, value[:, rows - two :], value[:, :two]).astype(BF) for value in (core, mid)
        ]
        target[2 * two :, : 2 * two] = jnp.concatenate(halos, 1)
        target[2 * two :, 2 * two :] = jnp.zeros((HALF, lat_cells - 2 * two), BF)


def halo_place(odd, place, lat_cells):
    row = iota((2 * HALF, lat_cells), 0)
    lane = iota((2 * HALF, lat_cells), 1)
    from_low = jnp.where(row < HALF, odd, 1 - odd) == 1
    wanted_row = 2 * place + jnp.where(from_low, 1, 0)
    wanted_lane = jnp.where(from_low, 0, lat_cells - 1)
    lat = lax.axis_index("lat")
    inside = jnp.where(row < HALF, 1, lat * (lax.axis_size("lat") - 1 - lat))
    return ((row % HALF == wanted_row) & (lane == wanted_lane) & (inside > 0)).astype(F32).astype(BF)


def halo_places(odd, lat_cells):
    return jnp.concatenate([halo_place(odd, place, lat_cells) for place in range(2)], 1)


def write_shifted(values, edge_columns, target, rows):
    lat_cells = values.shape[1]
    lane = iota(values.shape, 1)
    columns = edge_columns.astype(BF)
    target[0, rows, :] = jnp.where(lane == 0, columns, pltpu.roll(values, 1, 1))
    target[1, rows, :] = values
    target[2, rows, :] = jnp.where(lane == lat_cells - 1, columns, pltpu.roll(values, lat_cells - 1, 1))


def activate(pre_act, back_grad):
    sigmoid_value = 1.0 / (1.0 + jnp.exp(-pre_act))
    activation = pre_act * sigmoid_value
    slope = sigmoid_value + activation * (1.0 - sigmoid_value)
    return activation, back_grad * slope


def conv_rows(weight_ref, shifted, rows, out_rows):
    count = rows.stop - rows.start
    return sum(dot(weight_ref[q, :out_rows, :count], shifted[q, rows, :]) for q in range(3))


def inner_kernel(x_ref, cot_ref, core_ref, mid_ref, first_ref, back_ref, pre_ref, grads_ref, xs, cs, total):
    lat_cells = x_ref.shape[1]
    channels = grads_ref.shape[2]
    odd = is_odd()
    halos = jnp.concatenate([core_ref[...], mid_ref[...]], 0)
    everything = slice(0, x_ref.shape[0])
    columns = dot_rows(halos, halo_places(odd, lat_cells))
    for place, (source, target) in enumerate(((x_ref, xs), (cot_ref, cs))):
        write_shifted(source[...], columns[:, place * lat_cells : (place + 1) * lat_cells], target, everything)
    group_rows = GROUP * channels
    for k in range(pre_ref.shape[0] // group_rows):
        rows = slice(k * group_rows, k * group_rows + WINDOW * channels)
        pre_act = conv_rows(first_ref, xs, rows, group_rows)
        back_grad = conv_rows(back_ref, cs, rows, group_rows)
        activation, pre_grad = activate(pre_act, back_grad)
        activation = activation.astype(BF)
        pre_grad = pre_grad.astype(BF)
        pre_ref[k * group_rows : (k + 1) * group_rows, :] = pre_grad
        for q in range(3):
            for place, (own, raw) in enumerate(((pre_grad, xs), (activation, cs))):
                term = dot_lanes(own, raw[q, rows, :])
                if k == 0:
                    total[place, q] = term
                else:
                    total[place, q] += term
    for place in range(2):
        for q in range(3):
            summed = jnp.zeros((channels, WINDOW * channels), F32)
            for a in range(GROUP):
                band = total[place, q, a * channels : (a + 1) * channels, :]
                if a:
                    band = pltpu.roll(band, WINDOW * channels - a * channels, 1)
                summed = summed + band
            grads_ref[place, q] = summed[:, :128]


def edge_kernel(x_ref, cot_ref, core_ref, mid_ref, far_ref, near_ref, first_ref, back_ref, grads_ref,
                low_ref, high_ref, out_ref, left_ref, right_ref, xs_sides, cs_sides):
    lat_cells = x_ref.shape[1]
    channels = grads_ref.shape[2]
    odd = is_odd()
    two = 2 * channels
    own_rows = x_ref.shape[0]
    sums = [[grads_ref[place, q][:, : 3 * channels] for q in range(3)] for place in range(2)]
    far, near = far_ref[...], near_ref[...]
    left_ref[...] = jnp.where(lon_is_odd() == 1, near, far)
    right_ref[...] = jnp.where(lon_is_odd() == 1, far, near)
    sides = ((left_ref, low_ref), (right_ref, high_ref))
    places = halo_places(odd, lat_cells)
    for side, (message, _) in enumerate(sides):
        own = slice(0, two) if side == 0 else slice(own_rows - two, own_rows)
        sent = message[2 * two : 2 * two + HALF, :]
        sent_halos = jnp.concatenate([sent[:, :two], sent[:, two : 2 * two]], 0).astype(F32)
        own_halos = jnp.concatenate([core_ref[:, own], mid_ref[:, own]], 0).astype(F32)
        order = (sent_halos, own_halos) if side == 0 else (own_halos, sent_halos)
        halos = jnp.concatenate(order, 1).astype(BF)
        both = dot_rows(halos, places)
        for place, (source, shifted) in enumerate(((x_ref, xs_sides), (cot_ref, cs_sides))):
            sent_rows = message[place * two : (place + 1) * two, :]
            order = (sent_rows, source[own, :]) if side == 0 else (source[own, :], sent_rows)
            columns = both[:, place * lat_cells : (place + 1) * lat_cells]
            write_shifted(jnp.concatenate(order, 0), columns, shifted.at[side], slice(0, 2 * two))
    rows = slice(0, 2 * two)
    pre_acts = [conv_rows(first_ref, xs_sides.at[side], rows, two) for side in range(2)]
    back_grads = [conv_rows(back_ref, cs_sides.at[side], rows, two) for side in range(2)]
    for side, (_, target) in enumerate(sides):
        activation, pre_grad = activate(pre_acts[side], back_grads[side])
        pre_grad = pre_grad.astype(BF)
        target[...] = pre_grad
        mine = slice(channels, two) if side == 0 else slice(0, channels)
        near = slice(channels, 2 * two) if side == 0 else slice(0, 3 * channels)
        activation = activation[mine].astype(BF)
        pre_grad = pre_grad[mine]
        for q in range(3):
            sums[0][q] = sums[0][q] + dot_lanes(pre_grad, xs_sides[side, q, near, :])
            sums[1][q] = sums[1][q] + dot_lanes(activation, cs_sides[side, q, near, :])
    out_ref[...] = jnp.concatenate([pack_taps(taps) for taps in sums], 0)


def pack_taps(taps):
    channels = taps[0].shape[0]
    main = [
        jnp.concatenate([taps[q], taps[2][:, q * channels : (q + 1) * channels]], 1) for q in range(2)
    ]
    rest = taps[2][:, 2 * channels :]
    count = 128 // channels
    rows = channels // count
    last = jnp.concatenate([rest[i * rows : (i + 1) * rows] for i in range(count)], 1)
    return jnp.concatenate([*main, last], 0)


def unpack_taps(packed, channels):
    used = 3 * channels
    count = 128 // channels
    main = [packed[q * channels : (q + 1) * channels] for q in range(2)]
    rest = packed[2 * channels :]
    last = jnp.concatenate([rest[:, i * channels : (i + 1) * channels] for i in range(count)], 0)
    third = jnp.concatenate([main[0][:, used:], main[1][:, used:], last], 1)
    return [main[0], main[1], third]


def outer_kernel(x_ref, cot_ref, core_ref, mid_ref, left_ref, right_ref, first_ref, back_ref, low_ref, pre_ref,
                 high_ref, one_ref, partial_ref, ps, last_ref, passed_ref, rows_buffer, strips):
    passed_ref[...] = partial_ref[...]
    write_band(one_ref, True, last_ref)
    lat_cells = x_ref.shape[1]
    channels = low_ref.shape[0] // 2
    two = 2 * channels
    own_rows = x_ref.shape[0]
    wide_rows = own_rows + 2 * two
    odd = is_odd()
    core, mid = core_ref[...].astype(F32), mid_ref[...].astype(F32)
    lat = lax.axis_index("lat")
    lat_count = lax.axis_size("lat")

    def halo_lanes(value, first):
        parts = [left_ref[2 * two : 2 * two + HALF, first : first + two].astype(F32), value,
                 right_ref[2 * two : 2 * two + HALF, first : first + two].astype(F32)]
        return parts

    def put(target, parts):
        target[:, 0:two] = parts[0]
        target[:, two : two + own_rows] = parts[1]
        target[:, two + own_rows : wide_rows] = parts[2]

    put(strips.at[0], halo_lanes(core, 0))
    put(strips.at[1], halo_lanes(mid, two))
    core_wide, mid_wide = strips[0], strips[1]
    low = jnp.where(odd == 1, core_wide, mid_wide)
    high = jnp.where(odd == 1, mid_wide, core_wide)
    row = iota((HALF, lat_cells), 0)
    lane = iota((HALF, lat_cells), 1)
    ends = ((row < 2) & (lane == row * (lat_cells - 1))).astype(F32).astype(BF)
    values = []
    span = 4 * channels
    window = 6 * channels
    for place, (source, weight_ref) in enumerate(((x_ref, first_ref), (cot_ref, back_ref))):
        rows_buffer[0:two, :] = left_ref[place * two : (place + 1) * two, :]
        rows_buffer[two : two + own_rows, :] = source[...]
        rows_buffer[two + own_rows : wide_rows, :] = right_ref[place * two : (place + 1) * two, :]
        own = dot_lanes(ends, rows_buffer[...])
        low_rows = [low[2 * place : 2 * place + 1], low[2 * place + 1 : 2 * place + 2], own[0:1]]
        high_rows = [own[1:2], high[2 * place : 2 * place + 1], high[2 * place + 1 : 2 * place + 2]]
        total = None
        for q in range(3):
            which = iota((HALF, wide_rows), 0)
            strip = jnp.where(which == 0, low_rows[q], jnp.where(which == 1, high_rows[q], 0.0))
            strip = jnp.concatenate([strip, jnp.zeros((HALF, 128), F32)], 1)
            stacked = jnp.concatenate(
                [strip[:, k : k + window] for k in range(0, wide_rows, span)], 0
            ).astype(BF)
            term = dot_lanes(stacked, weight_ref[q, :span, :window])
            total = term if total is None else total + term
        values.append(total)
    _, pre_grad = activate(*values)
    beyond = jnp.where(iota(pre_grad.shape, 0) % HALF == 0, lat, lat_count - 1 - lat)
    pre_grad = jnp.where(beyond > 0, pre_grad, 0.0)
    pre_strip = jnp.concatenate(
        [pre_grad[k : k + HALF] for k in range(0, pre_grad.shape[0], HALF)], 1
    ).astype(BF)
    wide = pre_ref.shape[0] + 2 * two
    columns = dot_rows(pre_strip, ends)[:wide]
    rows_buffer[0:two, :] = low_ref[...]
    rows_buffer[two : wide - two, :] = pre_ref[...]
    rows_buffer[wide - two : wide, :] = high_ref[...]
    write_shifted(rows_buffer[0:wide, :], columns, ps, slice(0, wide))


def last_kernel(ps, last_ref, raw_ref, partial_ref, out_ref, passed_ref, placed, result, sems):
    passed_ref[...] = partial_ref[...]
    channels, lon_cells, lat_cells = out_ref.shape
    parts = lon_cells // HALF
    copies = []
    done = 0
    for first in range(0, lon_cells, GROUP):
        lons = min(GROUP, lon_cells - first)
        rows = slice(first * channels, (first + lons + 2) * channels)
        total = conv_rows(last_ref, ps, rows, lons * channels)
        for a in range(lons):
            lon_rows = total[a * channels : (a + 1) * channels]
            for tile in range(lat_cells // 128):
                lanes = slice(tile * 128, (tile + 1) * 128)
                placed[tile, pl.ds(first + a, channels, stride=lon_cells), :] = lon_rows[:, lanes]
        if first + lons >= done + HALF:
            part = slice(done, done + HALF)
            for tile in range(lat_cells // 128):
                lanes = slice(tile * 128, (tile + 1) * 128)
                block = placed[tile].reshape(channels, lon_cells, 128)[:, part, :]
                block = block + raw_ref[parts + done // HALF, :, :, lanes].astype(F32)
                result[:, part, lanes] = block.astype(BF)
            copy = pltpu.make_async_copy(
                result.at[:, pl.ds(done, HALF), :], out_ref.at[:, pl.ds(done, HALF), :], sems.at[done // HALF]
            )
            copy.start()
            copies.append(copy)
            done += HALF
    for copy in copies:
        copy.wait()


def result_kernel(scale, total_ref, given_ref, one_ref, two_ref):
    channels = one_ref.shape[2]
    rows = total_ref.shape[0] // 2
    sums = jnp.where(is_odd() == 1, total_ref[...], given_ref[...]) * scale
    first, second = sums[:rows], sums[rows:]
    first = unpack_taps(first, channels)
    second = unpack_taps(second, channels)
    for q in range(3):
        for p in range(3):
            lanes = slice(p * channels, (p + 1) * channels)
            one_ref[p, q] = first[q][:, lanes]
            two_ref[2 - p, 2 - q] = second[q][:, lanes].T


ALONG_X, ALONG_Y = 32, 1


def pairs(counts, partner, idle):
    lat_count, lon_count = counts
    listed = []
    for lat in range(lat_count):
        for lon in range(lon_count):
            to_lat, to_lon = partner(lat, lon) if lat % 2 else (lat, lon ^ idle)
            listed.append((lat * lon_count + lon, to_lat * lon_count + to_lon))
    return listed


def x_partner(mask):
    def partner(lat, lon):
        place = ((lat >> 1) * 2 + (lon >> 5)) ^ mask
        return (place >> 1) * 2 + (lat & 1), (place & 1) * 32 + (lon & 31)

    return partner


def y_partner(mask):
    return lambda lat, lon: (lat, lon ^ mask)


def z_partner(mask):
    return lambda lat, lon: (lat, lon ^ (mask << 2))


def exchange(value, partner, idle):
    counts = (lax.axis_size("lat"), lax.axis_size("lon"))
    return lax.ppermute(value, ("lat", "lon"), pairs(counts, partner, idle))


def sum_of_four(value, partner, masks, idle, beside=None):
    first, second, third = [exchange(value, partner(mask), idle) for mask in masks]
    result = None
    if beside is not None:
        *result, value = beside(value)
    return (value + first) + (second + third), result


def sum_everywhere(mine, widen, finish):
    total = mine + core_exchange(mine)
    total, _ = sum_of_four(total, x_partner, (1, 3, 2), ALONG_Y)
    total, shifted = sum_of_four(total, y_partner, (1, 3, 2), ALONG_X, widen)
    total, (input_grad,) = sum_of_four(
        total, z_partner, (1, 2, 3), ALONG_X, lambda value: finish(*shifted, value)
    )
    total = total + exchange(total, z_partner(6), ALONG_X)
    given = core_exchange(total)
    return total, given, input_grad


def mid_exchange(edges):
    count = lax.axis_size("lat")
    return lax.ppermute(edges, "lat", [(i, (i - 1 if i % 2 == 0 else i + 1) % count) for i in range(count)])


def core_exchange(value):
    return lax.ppermute(value, "lat", [(i, i ^ 1) for i in range(lax.axis_size("lat"))])


def on_device(inputs, kernel_one, kernel_two, cotangent):
    channels, lon_cells, lat_cells = inputs.shape
    cells = lon_cells * lat_cells * lax.axis_size("lat") * lax.axis_size("lon")
    rows = channels * lon_cells
    two = 2 * channels
    parts = lon_cells // HALF
    weights = shape(3, GROUP * channels, WINDOW * channels)
    folded = shape(4 * rows // lat_cells, lat_cells)
    raw, one, two_kernel, perm, core_out, mid_out = call(
        border_kernel,
        [
            shape(2 * parts, channels, HALF, lat_cells),
            shape(*kernel_one.shape),
            shape(*kernel_two.shape),
            shape(HALF * channels, HALF * channels),
            folded,
            folded,
        ],
        [pltpu.SemaphoreType.DMA((2 + 2 * parts,))],
        10**8,
        inputs,
        cotangent,
        kernel_one,
        kernel_two,
        hbm_in=(0, 1, 2, 3),
    )
    mid_in = mid_exchange(mid_out)
    x_rows, cot_rows, first, back, core_out = call(
        row_kernel,
        [shape(rows, lat_cells), shape(rows, lat_cells), weights, weights, folded],
        [],
        10**9,
        raw,
        perm,
        one,
        two_kernel,
        core_out,
    )
    core_in = core_exchange(core_out)

    message = shape(2 * two + HALF, lat_cells)
    edges = shape(HALF, rows)
    far_out, near_out, core_in, mid_in = call(
        message_kernel, [message, message, edges, edges], [], 10**6, x_rows, cot_rows, core_in, mid_in
    )
    count = lax.axis_size("lon")
    far_in = lax.ppermute(far_out, "lon", [(i, (i + 1 if i % 2 else i - 1) % count) for i in range(count)])
    near_in = lax.ppermute(near_out, "lon", [(i, i ^ 1) for i in range(count)])

    inner_rows = rows - two
    shifted = pltpu.VMEM((3, rows, lat_cells), BF)
    pre_inner, inner_grads = call(
        inner_kernel,
        [shape(inner_rows, lat_cells), shape(2, 3, channels, 128, dtype=F32)],
        [shifted, shifted, pltpu.VMEM((2, 3, GROUP * channels, WINDOW * channels), F32)],
        4 * 10**9,
        x_rows, cot_rows, core_in, mid_in, first, back,
    )
    edge_shifted = pltpu.VMEM((2, 3, 2 * two, lat_cells), BF)
    partial = shape(2 * 9 * channels * channels // 128, 128, dtype=F32)
    pre_low, pre_high, grads, from_left, from_right = call(
        edge_kernel,
        [shape(two, lat_cells), shape(two, lat_cells), partial, message, message],
        [edge_shifted, edge_shifted],
        10**9,
        x_rows, cot_rows, core_in, mid_in, far_in, near_in, first, back, inner_grads,
    )
    def widen(partial):
        return call(
            outer_kernel,
            [shape(3, rows + two, lat_cells), weights, shape(*partial.shape, dtype=F32)],
            [
                pltpu.VMEM((rows + 2 * two, lat_cells), BF),
                pltpu.VMEM((2, HALF, rows + 2 * two), F32),
            ],
            10**9,
            x_rows, cot_rows, core_in, mid_in, from_left, from_right, first, back,
            pre_low, pre_inner, pre_high, one, partial,
        )

    def finish(shifted, last, partial):
        return call(
            last_kernel,
            [shape(channels, lon_cells, lat_cells), shape(*partial.shape, dtype=F32)],
            [
                pltpu.VMEM((lat_cells // 128, rows, 128), F32),
                pltpu.VMEM((channels, lon_cells, lat_cells), BF),
                pltpu.SemaphoreType.DMA((lon_cells // HALF,)),
            ],
            2 * 10**9,
            shifted, last, raw, partial,
            hbm_out=(0,),
        )

    total, given, input_grad = sum_everywhere(grads, widen, finish)
    grad_one, grad_two = call(
        functools.partial(result_kernel, 1.0 / math.sqrt(cells)),
        [shape(3, 3, channels, channels, dtype=F32)] * 2,
        [],
        10**6,
        total,
        given,
    )
    return (input_grad, grad_one, grad_two)


def solution(mesh):
    placed = (P(None, "lon", "lat"), P(), P(), P(None, "lon", "lat"))
    return jax.shard_map(
        on_device,
        mesh=mesh,
        in_specs=placed,
        out_specs=(P(None, "lon", "lat"), P(), P()),
        check_vma=False,
    )
```
